128 devices in a mesh: clu: 128 (over y, x, z, core).
Axes of the slice: x: 4, y: 4, z: 4, core: 2. Of those that a mesh axis runs over, the one named last changes fastest.
Arguments:
- start_vector: float32 [512, 8, 256], P('clu'), may hold values from -6 to 6
- leaf_size: int32 [512], P('clu'), may hold values from 64 to 256, as said below
- diag_blocks: bfloat16 [512, 256, 256], P('clu'), as said below
- near_blocks: bfloat16 [2048, 256, 256], P('clu'), may hold values from -0.09375 to 0.09375
- near_count: int32 [128], P('clu'), may hold values from 12 to 16, as said below
- near_first: int32 [2048], P('clu'), may hold values from 0 to 3
- near_second: int32 [2048], P('clu'), may hold values from 1 to 7, as said below
- leaf_basis: bfloat16 [512, 64, 256], P('clu'), may hold values from -0.375 to 0.375
- transfer: float32 [512, 64, 64], P('clu'), may hold values from -0.5 to 0.5
- coupling: float32 [32768, 64, 64], P('clu'), may hold values from -0.1875 to 0.1875
- send_slot: int32 [128, 256], P('clu'), may hold values from -1 to 5, as said below
- far_target: int32 [128, 256], P('clu'), may hold values from -1 to 5, as said below
Outputs:
- products: float32 [4, 512, 8, 256], P(None, 'clu')
The draws below stay inside these ranges and needn't reach their ends.
Inputs may be any that keep to these rules, and one draw needn't show every extreme that they name: Positions from leaf_size[l] to 255 of leaf l are padding. Device d uses its first near_count[d] near-field slots, and some device uses all 16. near_second exceeds near_first of the same entry by 1 to 4; values from 4 on name leaves of the next device, and the last device continues at device 0. `send_slot`: for c < 1: a leaf slot (below 4) if devices d and p are at most 8 apart around the axis, else -1. For other c: a parent slot. `far_target`: for c < 1: a leaf slot (below 4) if devices d and p are at most 8 apart around the axis, else -1. For other c: a parent slot. `diag_blocks`: each block is symmetric.
All inputs are finite; a program needn't handle non-finite values.
Results may differ from the reference program's by a relative error of at most 0.01.
Values may be sent and summed in bfloat16 or wider, within the bound.
A program may use at most 128 MiB of HBM per device.

```python
import math
import jax
import jax.numpy as jnp
from jax import lax

B = 256
K = 64
R = 8
L_DEV = 4
C = 2
REACH = 8
PRODUCTS = 4
NEAR_CAP = 16
NLEAF = 512
N_CLU = 128


def near_pairs(key):
    total_pairs = N_CLU * NEAR_CAP
    position = jnp.arange(total_pairs, dtype=jnp.int32)
    first_leaf = jax.random.randint(jax.random.fold_in(key, 11), (total_pairs,), 0, L_DEV)
    offset = jax.random.randint(jax.random.fold_in(key, 12), (total_pairs,), 1, L_DEV + 1)
    top_pick = jax.random.randint(jax.random.fold_in(key, 13), (), 0, total_pairs)
    low_pick = (top_pick + jax.random.randint(jax.random.fold_in(key, 14), (), 1, total_pairs)) % total_pairs
    first_leaf = jnp.where(position == top_pick, L_DEV - 1, jnp.where(position == low_pick, 0, first_leaf))
    offset = jnp.where(position == top_pick, L_DEV, jnp.where(position == low_pick, 1, offset))
    return (first_leaf.astype(jnp.int32), (first_leaf + offset).astype(jnp.int32))


def slot_draw(key):
    columns = jnp.arange(N_CLU * C, dtype=jnp.int32)
    kind = columns % C
    peers = columns // C
    rows = jnp.arange(N_CLU, dtype=jnp.int32)
    apart = (rows[:, None] - peers[None, :]) % N_CLU
    cycle_gap = jnp.minimum(apart, N_CLU - apart)
    leaf_slot = jax.random.randint(jax.random.fold_in(key, 21), (N_CLU, N_CLU * C), 0, L_DEV)
    leaf_slot = jnp.where(cycle_gap <= REACH, leaf_slot, -1)
    parent_slot = L_DEV + jax.random.randint(jax.random.fold_in(key, 22), (N_CLU, N_CLU * C), 0, L_DEV // 2)
    return jnp.where(kind[None, :] < C // 2, leaf_slot, parent_slot).astype(jnp.int32)


def forced_range(key, length, lowest, highest):
    position = jnp.arange(length, dtype=jnp.int32)
    values = jax.random.randint(jax.random.fold_in(key, 31), (length,), lowest, highest + 1)
    top_pick = jax.random.randint(jax.random.fold_in(key, 32), (), 0, length)
    low_pick = (top_pick + jax.random.randint(jax.random.fold_in(key, 33), (), 1, length)) % length
    values = jnp.where(position == top_pick, highest, jnp.where(position == low_pick, lowest, values))
    return values.astype(jnp.int32)


def draw_leaf_size(key, part):
    key = jax.random.fold_in(key, 1)
    return forced_range(key, L_DEV * N_CLU, B // 4, B)


def draw_near_count(key, part):
    key = jax.random.fold_in(key, 2)
    return forced_range(key, N_CLU, 3 * L_DEV, NEAR_CAP)


def draw_near_first(key, part):
    first_leaf, second_leaf = near_pairs(key)
    return first_leaf


def draw_near_second(key, part):
    first_leaf, second_leaf = near_pairs(key)
    return second_leaf


def draw_send_slot(key, part):
    key = jax.random.fold_in(key, 5)
    return slot_draw(key)


def draw_far_target(key, part):
    key = jax.random.fold_in(key, 6)
    return slot_draw(key)


def draw_diag_blocks(key, part):
    key = jax.random.fold_in(key, 7)
    gaussian = jax.random.normal(key, (L_DEV * N_CLU, B, B), jnp.float32)
    symmetric = (gaussian + jnp.swapaxes(gaussian, 1, 2)) * (0.3 / math.sqrt(2.0 * B))
    return (symmetric + jnp.eye(B, dtype=jnp.float32)[None, :, :]).astype(jnp.bfloat16)


def shard_levels(own_key, shape, shards, low, largest):
    gain, own = 1.0, jax.random.fold_in(own_key, 6)
    for dim, shards_of in shards:
        steps = jnp.exp(jax.random.uniform(jax.random.fold_in(own, dim), (shards_of,), jnp.float32, low / len(shards), largest / len(shards)))
        gain = gain * jnp.repeat(steps, shape[dim] // shards_of).reshape([-1 if axis == dim else 1 for axis in range(len(shape))])
    return gain


def centred(rng, shape, scale, reach, pieces=(), held_as=jnp.bfloat16):
    gain = shard_levels(rng, shape, pieces, -0.22, 0.18) if pieces else 1.0
    values = jax.random.normal(rng, shape, jnp.float32) * scale * gain
    return jnp.minimum(jnp.maximum(values, -reach), reach).astype(held_as)


def setup_inputs(seed: int = 0) -> dict:
    keys = jax.random.split(jax.random.key(seed), 13)
    return {
        "start_vector": centred(keys[0], (NLEAF, R, B), 1.0, 6.0, ((0, 128),), jnp.float32),
        "leaf_size": draw_leaf_size(jax.random.fold_in(keys[12], 71), 0),
        "diag_blocks": draw_diag_blocks(jax.random.fold_in(keys[12], 71), 0),
        "near_blocks": centred(keys[3], (N_CLU * NEAR_CAP, B, B), (16 * B) ** -0.5, 0.09375, ((0, 128),)),
        "near_count": draw_near_count(jax.random.fold_in(keys[12], 71), 0),
        "near_first": draw_near_first(jax.random.fold_in(keys[12], 71), 0),
        "near_second": draw_near_second(jax.random.fold_in(keys[12], 71), 0),
        "leaf_basis": centred(keys[7], (NLEAF, K, B), B ** -0.5, 0.375, ((0, 128),)),
        "transfer": centred(keys[8], (NLEAF, K, K), (2 * K) ** -0.5, 0.5, ((0, 128),), jnp.float32),
        "coupling": centred(keys[9], (N_CLU * N_CLU * C, K, K), (16 * K) ** -0.5, 0.1875, ((0, 128),), jnp.float32),
        "send_slot": draw_send_slot(jax.random.fold_in(keys[12], 71), 0),
        "far_target": draw_far_target(jax.random.fold_in(keys[12], 71), 0),
    }


def reference(start_vector, leaf_size, diag_blocks, near_blocks, near_count, near_first, near_second, leaf_basis, transfer, coupling, send_slot, far_target):
    highest = lax.Precision.HIGHEST
    leaf_total = L_DEV * N_CLU
    cluster_slots = L_DEV + L_DEV // 2
    points = jnp.arange(B, dtype=jnp.int32)
    point_mask = (points[None, :] < leaf_size[:, None]).astype(jnp.float32)[:, None, :]
    pair_index = jnp.arange(N_CLU * NEAR_CAP, dtype=jnp.int32)
    owner = pair_index // NEAR_CAP
    live_pairs = ((pair_index % NEAR_CAP) < near_count[owner]).astype(jnp.float32)[:, None, None]
    target_leaf = (owner * L_DEV + near_first).astype(jnp.int32)
    source_leaf = ((owner * L_DEV + near_second) % leaf_total).astype(jnp.int32)
    slots_send = jnp.transpose(send_slot.reshape(N_CLU, N_CLU, C), (1, 0, 2))
    slots_recv = far_target.reshape(N_CLU, N_CLU, C)
    far_live = ((slots_recv >= 0) & (slots_send >= 0)).astype(jnp.float32).reshape(-1)[:, None, None]
    devices = jnp.arange(N_CLU, dtype=jnp.int32)
    target_slot = (devices[:, None, None] * cluster_slots + jnp.maximum(slots_recv, 0)).reshape(-1).astype(jnp.int32)
    source_slot = (devices[None, :, None] * cluster_slots + jnp.maximum(slots_send, 0)).reshape(-1).astype(jnp.int32)
    blocks_near = near_blocks.astype(jnp.float32)
    blocks_diag = diag_blocks.astype(jnp.float32)
    basis = leaf_basis.astype(jnp.float32)
    vector = start_vector * point_mask
    results = []
    for product in range(PRODUCTS):
        rounded = lax.optimization_barrier(vector.astype(jnp.bfloat16)).astype(jnp.float32)
        output = jnp.einsum('lij,lrj->lri', blocks_diag, rounded)
        forward = jnp.einsum('qij,qrj->qri', blocks_near, rounded[source_leaf]) * live_pairs
        backward = jnp.einsum('qij,qri->qrj', blocks_near, rounded[target_leaf]) * live_pairs
        output = output.at[target_leaf].add(forward).at[source_leaf].add(backward)
        leaf_coef = jnp.einsum('lkj,lrj->lrk', basis, rounded)
        parent_coef = jnp.einsum('lrm,lmk->lrk', leaf_coef, transfer, precision=highest)
        parent_coef = parent_coef.reshape(leaf_total // 2, 2, R, K).sum(axis=1)
        all_coef = jnp.concatenate([leaf_coef.reshape(N_CLU, L_DEV, R, K), parent_coef.reshape(N_CLU, L_DEV // 2, R, K)], axis=1)
        all_coef = all_coef.reshape(N_CLU * cluster_slots, R, K)
        far_in = jnp.einsum('qkm,qrm->qrk', coupling, all_coef[source_slot], precision=highest) * far_live
        far_out = jnp.einsum('qkm,qrk->qrm', coupling, all_coef[target_slot], precision=highest) * far_live
        far_sum = jnp.zeros_like(all_coef).at[target_slot].add(far_in).at[source_slot].add(far_out)
        far_sum = far_sum.reshape(N_CLU, cluster_slots, R, K)
        leaf_far = far_sum[:, :L_DEV].reshape(leaf_total, R, K)
        parent_far = jnp.repeat(far_sum[:, L_DEV:].reshape(leaf_total // 2, R, K), 2, axis=0)
        leaf_far = leaf_far + jnp.einsum('lmk,lrk->lrm', transfer, parent_far, precision=highest)
        leaf_round = lax.optimization_barrier(leaf_far.astype(jnp.bfloat16)).astype(jnp.float32)
        output = output + jnp.einsum('lkj,lrk->lrj', basis, leaf_round)
        vector = output * point_mask
        results.append(vector)
    return jnp.stack(results)
```

```python
import functools

import jax
import jax.numpy as jnp
from jax import lax
from jax.experimental import pallas as pl
from jax.experimental.pallas import tpu as pltpu
from jax.sharding import PartitionSpec as P

PRODUCTS = 4
REACH = 8
NEAR = 2 * REACH + 1
GROUPS = 3
LOADS = 4
LEAVES = 4
RANK = 64
RHS = 8
POINTS = 256
CAPACITY = 16
MESH = pl.DeviceIdType.MESH
F32 = jnp.float32
BF16 = jnp.bfloat16


def nn(a, b):
    return jnp.dot(a, b, preferred_element_type=F32)


def nt(a, b):
    return lax.dot_general(a, b, (((1,), (1,)), ((), ())), preferred_element_type=F32)


def swap_halves(a):
    return pltpu.roll(a, RANK, 1)


def pairs_of(first, last):
    return [list(range(j, min(j + 2, last))) for j in range(first, last, 2)]


def side_by_side(parts):
    return parts[0] if len(parts) == 1 else jnp.concatenate(parts, axis=1)


def kernel(
    devices,
    start,
    leaf_size,
    diag_hbm,
    near_hbm,
    near_count,
    near_first,
    near_second,
    basis,
    transfer,
    coupling,
    send_slot,
    far_target,
    out,
    parent_raw,
    leaf_raw,
    parent_w,
    leaf_w,
    near,
    diag,
    both_basis,
    pick,
    point_mask,
    vector,
    extended,
    send,
    recv,
    x_out,
    x_in,
    near_out,
    near_in,
    load_sem,
    send_sem,
    recv_sem,
    side_sem,
):
    me = lax.axis_index("clu")
    far_count = devices - NEAR
    group = far_count // GROUPS
    load_rows = devices // LOADS

    def peer(j):
        return lax.rem(me + (j - REACH + devices), devices)

    def tile_of(j):
        return 2 * j if j < NEAR else j + NEAR

    parent_loads = [
        pltpu.make_async_copy(
            coupling.at[pl.ds(c * load_rows, load_rows), 1],
            parent_raw.at[pl.ds(c * load_rows, load_rows)],
            load_sem.at[c],
        )
        for c in range(LOADS)
    ]
    near_load = pltpu.make_async_copy(near_hbm, near, load_sem.at[LOADS + 1])
    diag_load = pltpu.make_async_copy(diag_hbm, diag, load_sem.at[LOADS + 2])
    for j in range(NEAR):
        pltpu.make_async_copy(
            coupling.at[peer(j), 0], leaf_raw.at[j], load_sem.at[LOADS]
        ).start()
    for load in parent_loads:
        load.start()
    near_load.start()
    diag_load.start()

    barrier = pltpu.get_barrier_semaphore()

    def greet(step, carry):
        pl.semaphore_signal(
            barrier, inc=1, device_id=(lax.rem(me + step, devices),), device_id_type=MESH
        )
        return carry

    lax.fori_loop(1, devices, greet, 0)

    point_ids = lax.broadcasted_iota(jnp.int32, (RHS, POINTS), 1)
    for l in range(LEAVES):
        inside = jnp.where(point_ids < leaf_size[l], 1.0, 0.0)
        point_mask[l] = inside
        vector[l] = start[l] * inside
    for e in range(CAPACITY):
        live = e < near_count[0]
        for t in range(LEAVES):
            pick[e, t] = jnp.where(live & (near_first[e] == t), 1.0, 0.0)
        for s in range(2 * LEAVES):
            pick[e, LEAVES + s] = jnp.where(live & (near_second[e] == s), 1.0, 0.0)

    for l in range(LEAVES):
        moved = transfer[l].T
        high = moved.astype(BF16)
        low = (moved - high.astype(F32)).astype(BF16)
        own = basis[l]
        both_basis[l] = jnp.concatenate(
            [own.astype(F32), nn(high, own) + nn(low, own)], axis=0
        ).astype(BF16)

    lane = lax.broadcasted_iota(jnp.int32, (RANK, 2 * RANK), 1)
    row = lax.broadcasted_iota(jnp.int32, (RANK, 2 * RANK), 0)
    unit = jnp.where(lane == row + RANK, 1.0, 0.0)
    left = lane < RANK

    def weights(raw, target, source, slots):
        wide = jnp.where(left, jnp.concatenate([raw, raw], axis=1), unit)
        slot = jnp.where(left, target, source)
        return [jnp.where(slot == s, wide, 0.0).astype(BF16) for s in slots]

    pltpu.make_async_copy(leaf_raw, leaf_raw, load_sem.at[LOADS]).wait()

    def build_leaf(j, carry):
        column = 2 * peer(j)
        parts = weights(
            leaf_raw[j], far_target[0, column], send_slot[0, column], range(LEAVES)
        )
        for s, part in enumerate(parts):
            leaf_w[j, s * RANK : (s + 1) * RANK, :] = part
        return carry

    lax.fori_loop(0, NEAR, build_leaf, 0)

    def build_parent(p, carry):
        column = 2 * p + 1
        parts = weights(
            parent_raw[p],
            far_target[0, column],
            send_slot[0, column],
            range(LEAVES, LEAVES + LEAVES // 2),
        )
        j = lax.rem(p - me + (REACH + devices), devices)
        for s, part in enumerate(parts):
            parent_w[j, s * RANK : (s + 1) * RANK, :] = part
        return carry

    for c in range(LOADS):
        parent_loads[c].wait()
        lax.fori_loop(c * load_rows, (c + 1) * load_rows, build_parent, 0)

    near_load.wait()
    diag_load.wait()
    pl.semaphore_wait(barrier, devices - 1)

    half = lax.broadcasted_iota(jnp.int32, (RHS, 2 * RANK), 1) < RANK

    def remote(src, dst, out_sem, in_sem, target):
        return pltpu.make_async_remote_copy(
            src_ref=src,
            dst_ref=dst,
            send_sem=out_sem,
            recv_sem=in_sem,
            device_id=(target,),
            device_id_type=MESH,
        )

    def x_copy(n):
        return remote(
            x_out.at[n], x_in.at[n], side_sem.at[n, 0], side_sem.at[n, 1], peer(REACH - 1)
        )

    def near_copy(n):
        return remote(
            near_out.at[n], near_in.at[n], side_sem.at[n, 2], side_sem.at[n, 3], peer(REACH + 1)
        )

    def far_copy(n, j):
        if j < NEAR:
            src, dst, count, box = tile_of(j), tile_of(NEAR - 1 - j), 2, 0
        else:
            src, dst, count = tile_of(j), tile_of(devices + NEAR - 1 - j), 1
            box = 1 + (j - NEAR) // group
        return remote(
            send.at[n, pl.ds(src, count)],
            recv.at[n, pl.ds(dst, count)],
            send_sem.at[n],
            recv_sem.at[n, box],
            peer(j),
        )

    def product(n, carry):
        exact = [vector[l] for l in range(LEAVES)]
        rounded = [value.astype(BF16) for value in exact]
        x_out[n] = jnp.concatenate(exact, axis=0).astype(BF16)
        x_copy(n).start()

        coef = [nt(rounded[l], both_basis[l]) for l in range(LEAVES)]
        leaf_coef = jnp.concatenate(
            [
                jnp.where(half, coef[0], swap_halves(coef[1])),
                jnp.where(half, coef[2], swap_halves(coef[3])),
            ],
            axis=1,
        ).astype(BF16)
        parent_coef = jnp.where(
            half, swap_halves(coef[0] + coef[1]), coef[2] + coef[3]
        ).astype(BF16)

        def fill(values, w, first, last, place):
            for js in pairs_of(first, last):
                made = nn(values, side_by_side([w[j] for j in js]))
                for i, j in enumerate(js):
                    tile = swap_halves(made[:, i * 2 * RANK : (i + 1) * 2 * RANK]).astype(BF16)
                    if j == REACH:
                        recv[n, place(j)] = tile
                    else:
                        send[n, place(j)] = tile

        fill(leaf_coef, leaf_w, 0, NEAR, lambda j: tile_of(j) + 1)
        fill(parent_coef, parent_w, 0, NEAR, tile_of)
        for j in range(NEAR):
            if j != REACH:
                far_copy(n, j).start()
        for g in range(GROUPS):
            first = NEAR + g * group
            fill(parent_coef, parent_w, first, first + group, tile_of)
            for j in range(first, first + group):
                far_copy(n, j).start()

        for l in range(LEAVES):
            extended[l] = rounded[l].astype(F32)
        backward = jnp.zeros((2 * LEAVES * RHS, POINTS), F32)
        for e in range(CAPACITY):
            own = extended[near_first[e]]
            spread = jnp.concatenate(
                [own * pick[e, LEAVES + s] for s in range(2 * LEAVES)], axis=0
            ).astype(BF16)
            backward = backward + nn(spread, near[e])
        near_out[n] = backward[LEAVES * RHS :].astype(BF16)
        near_copy(n).start()
        total = backward[: LEAVES * RHS] + jnp.concatenate(
            [nn(rounded[l], diag[l]) for l in range(LEAVES)], axis=0
        )

        x_copy(n).wait_recv()
        following = x_in[n].astype(F32)
        for l in range(LEAVES):
            extended[LEAVES + l] = following[l * RHS : (l + 1) * RHS]
        for e in range(CAPACITY):
            other = extended[near_second[e]]
            spread = jnp.concatenate(
                [other * pick[e, t] for t in range(LEAVES)], axis=0
            ).astype(BF16)
            total = total + nt(spread, near[e])

        def take(w, first, last, place, sofar):
            for js in pairs_of(first, last):
                got = side_by_side([recv[n, place(j)] for j in js])
                sofar = sofar + nt(got, side_by_side([w[j] for j in js]))
            return sofar

        def arrived(first, count, box):
            tiles = recv.at[n, pl.ds(first, count)]
            pltpu.make_async_copy(tiles, tiles, recv_sem.at[n, box]).wait()

        arrived(0, 2 * (NEAR - 1), 0)
        leaf_far = jnp.zeros((RHS, LEAVES * RANK), F32)
        leaf_far = take(leaf_w, 0, NEAR, lambda j: tile_of(j) + 1, leaf_far)
        parent_far = jnp.zeros((RHS, 2 * RANK), F32)
        parent_far = take(parent_w, 0, NEAR, tile_of, parent_far)
        for g in range(GROUPS):
            first = devices - (g + 1) * group
            arrived(tile_of(first), group, 1 + g)
            parent_far = take(parent_w, first, first + group, tile_of, parent_far)

        near_copy(n).wait_recv()
        total = total + near_in[n].astype(F32)
        for l in range(LEAVES):
            pair = leaf_far[:, (l // 2) * 2 * RANK : (l // 2 + 1) * 2 * RANK]
            both = jnp.where(
                half,
                pair if l % 2 == 0 else swap_halves(pair),
                swap_halves(parent_far) if l < 2 else parent_far,
            ).astype(BF16)
            value = total[l * RHS : (l + 1) * RHS] + nn(both, both_basis[l])
            value = value * point_mask[l]
            vector[l] = value
            out[n, l] = value
        return carry

    lax.fori_loop(0, PRODUCTS, product, 0)

    def finish(n, carry):
        sent = send.at[n, pl.ds(0, 2 * (NEAR - 1) + far_count)]
        pltpu.make_async_copy(sent, sent, send_sem.at[n]).wait()
        x_copy(n).wait_send()
        near_copy(n).wait_send()
        return carry

    lax.fori_loop(0, PRODUCTS, finish, 0)


def on_device(
    start_vector,
    leaf_size,
    diag_blocks,
    near_blocks,
    near_count,
    near_first,
    near_second,
    leaf_basis,
    transfer,
    coupling,
    send_slot,
    far_target,
):
    devices = lax.axis_size("clu")
    tiles = devices + NEAR
    vmem = pl.BlockSpec(memory_space=pltpu.VMEM)
    smem = pl.BlockSpec(memory_space=pltpu.SMEM)
    anywhere = pl.BlockSpec(memory_space=pl.ANY)
    sides = (PRODUCTS, LEAVES * RHS, POINTS)
    return pl.pallas_call(
        functools.partial(kernel, devices),
        out_shape=jax.ShapeDtypeStruct((PRODUCTS, LEAVES, RHS, POINTS), F32),
        in_specs=[
            vmem,
            smem,
            anywhere,
            anywhere,
            smem,
            smem,
            smem,
            vmem,
            vmem,
            anywhere,
            smem,
            smem,
        ],
        out_specs=vmem,
        scratch_shapes=[
            pltpu.VMEM((devices, RANK, RANK), F32),
            pltpu.VMEM((NEAR, RANK, RANK), F32),
            pltpu.VMEM((devices, 2 * RANK, 2 * RANK), BF16),
            pltpu.VMEM((NEAR, LEAVES * RANK, 2 * RANK), BF16),
            pltpu.VMEM((CAPACITY, POINTS, POINTS), BF16),
            pltpu.VMEM((LEAVES, POINTS, POINTS), BF16),
            pltpu.VMEM((LEAVES, 2 * RANK, POINTS), BF16),
            pltpu.SMEM((CAPACITY, 3 * LEAVES), F32),
            pltpu.VMEM((LEAVES, RHS, POINTS), F32),
            pltpu.VMEM((LEAVES, RHS, POINTS), F32),
            pltpu.VMEM((2 * LEAVES, RHS, POINTS), F32),
            pltpu.VMEM((PRODUCTS, tiles, RHS, 2 * RANK), BF16),
            pltpu.VMEM((PRODUCTS, tiles, RHS, 2 * RANK), BF16),
            pltpu.VMEM(sides, BF16),
            pltpu.VMEM(sides, BF16),
            pltpu.VMEM(sides, BF16),
            pltpu.VMEM(sides, BF16),
            pltpu.SemaphoreType.DMA((LOADS + 3,)),
            pltpu.SemaphoreType.DMA((PRODUCTS,)),
            pltpu.SemaphoreType.DMA((PRODUCTS, 1 + GROUPS)),
            pltpu.SemaphoreType.DMA((PRODUCTS, 4)),
        ],
        compiler_params=pltpu.CompilerParams(
            collective_id=0, has_side_effects=True, vmem_limit_bytes=48 * 1024 * 1024
        ),
        name="h2_products",
    )(
        start_vector,
        leaf_size,
        diag_blocks,
        near_blocks,
        near_count,
        near_first,
        near_second,
        leaf_basis,
        transfer,
        coupling.reshape(devices, 2, RANK, RANK),
        send_slot,
        far_target,
    )


def solution(mesh):
    in_specs = (
        P("clu", None, None),
        P("clu"),
        P("clu", None, None),
        P("clu", None, None),
        P("clu"),
        P("clu"),
        P("clu"),
        P("clu", None, None),
        P("clu", None, None),
        P("clu", None, None),
        P("clu", None),
        P("clu", None),
    )
    out_specs = P(None, "clu", None, None)
    return jax.shard_map(
        on_device, mesh=mesh, in_specs=in_specs, out_specs=out_specs, check_vma=False
    )
```

```python
import functools

import jax
import jax.numpy as jnp
from jax import lax
from jax.experimental import pallas as pl
from jax.experimental.pallas import tpu as pltpu
from jax.sharding import PartitionSpec as P

PRODUCTS = 4
REACH = 8
NEAR = 2 * REACH + 1
GROUPS = 3
LOADS = 4
LEAVES = 4
RANK = 64
HALF = RANK // 2
RHS = 8
POINTS = 256
CAPACITY = 16
MESH = pl.DeviceIdType.MESH
F32 = jnp.float32
BF16 = jnp.bfloat16


def nn(a, b):
    return jnp.dot(a, b, preferred_element_type=F32)


def nt(a, b):
    return lax.dot_general(a, b, (((1,), (1,)), ((), ())), preferred_element_type=F32)


def swap_halves(a):
    return pltpu.roll(a, RANK, 1)


def pairs_of(first, last):
    return [list(range(j, min(j + 2, last))) for j in range(first, last, 2)]


def side_by_side(parts):
    return parts[0] if len(parts) == 1 else jnp.concatenate(parts, axis=1)


def kernel(
    devices,
    start,
    leaf_size,
    diag_hbm,
    near_hbm,
    near_count,
    near_first,
    near_second,
    basis,
    transfer,
    coupling,
    send_slot,
    far_target,
    out,
    raw,
    turned,
    parent_w,
    leaf_w,
    near,
    diag,
    both_basis,
    pick,
    point_mask,
    vector,
    extended,
    send,
    recv,
    x_out,
    x_in,
    near_out,
    near_in,
    load_sem,
    send_sem,
    recv_sem,
    side_sem,
):
    me = lax.axis_index("clu")
    far_count = devices - NEAR
    group = far_count // GROUPS
    load_rows = HALF // LOADS
    pair_count = 2 * devices

    def wrap(index):
        if devices & (devices - 1):
            return lax.rem(index, devices)
        return index & (devices - 1)

    def peer(j):
        return wrap(me + (j - REACH + devices))

    def tile_of(j):
        return 2 * j if j < NEAR else j + NEAR

    raw_loads = [
        [
            pltpu.make_async_copy(
                coupling.at[pl.ds(first, load_rows)],
                raw.at[pl.ds(first, load_rows)],
                load_sem.at[c, h],
            )
            for h, first in enumerate((c * load_rows, HALF + c * load_rows))
        ]
        for c in range(LOADS)
    ]
    near_load = pltpu.make_async_copy(near_hbm, near, load_sem.at[LOADS, 0])
    diag_load = pltpu.make_async_copy(diag_hbm, diag, load_sem.at[LOADS, 1])
    for loads in raw_loads:
        for load in loads:
            load.start()
    near_load.start()
    diag_load.start()

    barrier = pltpu.get_barrier_semaphore()

    def greet(step, carry):
        pl.semaphore_signal(
            barrier, inc=1, device_id=(wrap(me + step),), device_id_type=MESH
        )
        return carry

    lax.fori_loop(1, devices, greet, 0)

    point_ids = lax.broadcasted_iota(jnp.int32, (RHS, POINTS), 1)
    for l in range(LEAVES):
        inside = jnp.where(point_ids < leaf_size[l], 1.0, 0.0)
        point_mask[l] = inside
        vector[l] = start[l] * inside
    for e in range(CAPACITY):
        live = e < near_count[0]
        for t in range(LEAVES):
            pick[e, t] = jnp.where(live & (near_first[e] == t), 1.0, 0.0)
        for s in range(2 * LEAVES):
            pick[e, LEAVES + s] = jnp.where(live & (near_second[e] == s), 1.0, 0.0)

    for l in range(LEAVES):
        moved = transfer[l].T
        high = moved.astype(BF16)
        low = (moved - high.astype(F32)).astype(BF16)
        own = basis[l]
        both_basis[l] = jnp.concatenate(
            [own.astype(F32), nn(high, own) + nn(low, own)], axis=0
        ).astype(BF16)

    def turn(k, carry):
        both = jnp.concatenate([raw[k], raw[k + HALF]], axis=0)
        turned[pl.ds(k, pair_count, stride=HALF), :] = both.T
        return carry

    for c in range(LOADS):
        for load in raw_loads[c]:
            load.wait()
        lax.fori_loop(c * load_rows, (c + 1) * load_rows, turn, 0)

    lane = lax.broadcasted_iota(jnp.int32, (RANK, 2 * RANK), 1)
    row = lax.broadcasted_iota(jnp.int32, (RANK, 2 * RANK), 0)
    unit = jnp.where(lane == row + RANK, 1.0, 0.0)
    left = lane < RANK

    def weights(column, slots):
        low = turned[pl.ds(pl.multiple_of(column * HALF, HALF), HALF), :]
        wide = jnp.where(left, jnp.concatenate([low, swap_halves(low)], axis=0), unit)
        slot = jnp.where(left, far_target[0, column], send_slot[0, column])
        return [jnp.where(slot == s, wide, 0.0).astype(BF16) for s in slots]

    def build_leaf(j, carry):
        for s, part in enumerate(weights(2 * peer(j), range(LEAVES))):
            leaf_w[j, s * RANK : (s + 1) * RANK, :] = part
        return carry

    lax.fori_loop(0, NEAR, build_leaf, 0)

    def build_parent(j, carry):
        slots = range(LEAVES, LEAVES + LEAVES // 2)
        for s, part in enumerate(weights(2 * peer(j) + 1, slots)):
            parent_w[j, s * RANK : (s + 1) * RANK, :] = part
        return carry

    lax.fori_loop(0, devices, build_parent, 0, unroll=4)

    near_load.wait()
    diag_load.wait()
    pl.semaphore_wait(barrier, devices - 1)

    half = lax.broadcasted_iota(jnp.int32, (RHS, 2 * RANK), 1) < RANK

    def remote(src, dst, out_sem, in_sem, target):
        return pltpu.make_async_remote_copy(
            src_ref=src,
            dst_ref=dst,
            send_sem=out_sem,
            recv_sem=in_sem,
            device_id=(target,),
            device_id_type=MESH,
        )

    def x_copy(n):
        return remote(
            x_out.at[n], x_in.at[n], side_sem.at[n, 0], side_sem.at[n, 1], peer(REACH - 1)
        )

    def near_copy(n):
        return remote(
            near_out.at[n], near_in.at[n], side_sem.at[n, 2], side_sem.at[n, 3], peer(REACH + 1)
        )

    def far_copy(n, j):
        if j < NEAR:
            src, dst, count, box = tile_of(j), tile_of(NEAR - 1 - j), 2, 0
        else:
            src, dst, count = tile_of(j), tile_of(devices + NEAR - 1 - j), 1
            box = 1 + (j - NEAR) // group
        return remote(
            send.at[n, pl.ds(src, count)],
            recv.at[n, pl.ds(dst, count)],
            send_sem.at[n],
            recv_sem.at[n, box],
            peer(j),
        )

    def product(n, carry):
        exact = [vector[l] for l in range(LEAVES)]
        rounded = [value.astype(BF16) for value in exact]
        x_out[n] = jnp.concatenate(exact, axis=0).astype(BF16)
        x_copy(n).start()

        coef = [nt(rounded[l], both_basis[l]) for l in range(LEAVES)]
        leaf_coef = jnp.concatenate(
            [
                jnp.where(half, coef[0], swap_halves(coef[1])),
                jnp.where(half, coef[2], swap_halves(coef[3])),
            ],
            axis=1,
        ).astype(BF16)
        parent_coef = jnp.where(
            half, swap_halves(coef[0] + coef[1]), coef[2] + coef[3]
        ).astype(BF16)

        def fill(values, w, first, last, place):
            for js in pairs_of(first, last):
                made = nn(values, side_by_side([w[j] for j in js]))
                for i, j in enumerate(js):
                    tile = swap_halves(made[:, i * 2 * RANK : (i + 1) * 2 * RANK]).astype(BF16)
                    if j == REACH:
                        recv[n, place(j)] = tile
                    else:
                        send[n, place(j)] = tile

        fill(leaf_coef, leaf_w, 0, NEAR, lambda j: tile_of(j) + 1)
        fill(parent_coef, parent_w, 0, NEAR, tile_of)
        for j in range(NEAR):
            if j != REACH:
                far_copy(n, j).start()
        for g in range(GROUPS):
            first = NEAR + g * group
            fill(parent_coef, parent_w, first, first + group, tile_of)
            for j in range(first, first + group):
                far_copy(n, j).start()

        for l in range(LEAVES):
            extended[l] = rounded[l].astype(F32)
        backward = jnp.zeros((2 * LEAVES * RHS, POINTS), F32)
        for e in range(CAPACITY):
            own = extended[near_first[e]]
            spread = jnp.concatenate(
                [own * pick[e, LEAVES + s] for s in range(2 * LEAVES)], axis=0
            ).astype(BF16)
            backward = backward + nn(spread, near[e])
        near_out[n] = backward[LEAVES * RHS :].astype(BF16)
        near_copy(n).start()
        total = backward[: LEAVES * RHS] + jnp.concatenate(
            [nn(rounded[l], diag[l]) for l in range(LEAVES)], axis=0
        )

        x_copy(n).wait_recv()
        following = x_in[n].astype(F32)
        for l in range(LEAVES):
            extended[LEAVES + l] = following[l * RHS : (l + 1) * RHS]
        for e in range(CAPACITY):
            other = extended[near_second[e]]
            spread = jnp.concatenate(
                [other * pick[e, t] for t in range(LEAVES)], axis=0
            ).astype(BF16)
            total = total + nt(spread, near[e])

        def take(w, first, last, place, sofar):
            for js in pairs_of(first, last):
                got = side_by_side([recv[n, place(j)] for j in js])
                sofar = sofar + nt(got, side_by_side([w[j] for j in js]))
            return sofar

        def arrived(first, count, box):
            tiles = recv.at[n, pl.ds(first, count)]
            pltpu.make_async_copy(tiles, tiles, recv_sem.at[n, box]).wait()

        arrived(0, 2 * (NEAR - 1), 0)
        leaf_far = jnp.zeros((RHS, LEAVES * RANK), F32)
        leaf_far = take(leaf_w, 0, NEAR, lambda j: tile_of(j) + 1, leaf_far)
        parent_far = jnp.zeros((RHS, 2 * RANK), F32)
        parent_far = take(parent_w, 0, NEAR, tile_of, parent_far)
        for g in range(GROUPS):
            first = devices - (g + 1) * group
            arrived(tile_of(first), group, 1 + g)
            parent_far = take(parent_w, first, first + group, tile_of, parent_far)

        near_copy(n).wait_recv()
        total = total + near_in[n].astype(F32)
        for l in range(LEAVES):
            pair = leaf_far[:, (l // 2) * 2 * RANK : (l // 2 + 1) * 2 * RANK]
            both = jnp.where(
                half,
                pair if l % 2 == 0 else swap_halves(pair),
                swap_halves(parent_far) if l < 2 else parent_far,
            ).astype(BF16)
            value = total[l * RHS : (l + 1) * RHS] + nn(both, both_basis[l])
            value = value * point_mask[l]
            vector[l] = value
            out[n, l] = value
        return carry

    lax.fori_loop(0, PRODUCTS, product, 0)

    def finish(n, carry):
        sent = send.at[n, pl.ds(0, 2 * (NEAR - 1) + far_count)]
        pltpu.make_async_copy(sent, sent, send_sem.at[n]).wait()
        x_copy(n).wait_send()
        near_copy(n).wait_send()
        return carry

    lax.fori_loop(0, PRODUCTS, finish, 0)


def on_device(
    start_vector,
    leaf_size,
    diag_blocks,
    near_blocks,
    near_count,
    near_first,
    near_second,
    leaf_basis,
    transfer,
    coupling,
    send_slot,
    far_target,
):
    devices = lax.axis_size("clu")
    tiles = devices + NEAR
    vmem = pl.BlockSpec(memory_space=pltpu.VMEM)
    smem = pl.BlockSpec(memory_space=pltpu.SMEM)
    anywhere = pl.BlockSpec(memory_space=pl.ANY)
    sides = (PRODUCTS, LEAVES * RHS, POINTS)
    return pl.pallas_call(
        functools.partial(kernel, devices),
        out_shape=jax.ShapeDtypeStruct((PRODUCTS, LEAVES, RHS, POINTS), F32),
        in_specs=[
            vmem,
            smem,
            anywhere,
            anywhere,
            smem,
            smem,
            smem,
            vmem,
            vmem,
            anywhere,
            smem,
            smem,
        ],
        out_specs=vmem,
        scratch_shapes=[
            pltpu.VMEM((RANK, RANK, 2 * devices), F32),
            pltpu.VMEM((2 * devices * HALF, 2 * RANK), F32),
            pltpu.VMEM((devices, 2 * RANK, 2 * RANK), BF16),
            pltpu.VMEM((NEAR, LEAVES * RANK, 2 * RANK), BF16),
            pltpu.VMEM((CAPACITY, POINTS, POINTS), BF16),
            pltpu.VMEM((LEAVES, POINTS, POINTS), BF16),
            pltpu.VMEM((LEAVES, 2 * RANK, POINTS), BF16),
            pltpu.SMEM((CAPACITY, 3 * LEAVES), F32),
            pltpu.VMEM((LEAVES, RHS, POINTS), F32),
            pltpu.VMEM((LEAVES, RHS, POINTS), F32),
            pltpu.VMEM((2 * LEAVES, RHS, POINTS), F32),
            pltpu.VMEM((PRODUCTS, tiles, RHS, 2 * RANK), BF16),
            pltpu.VMEM((PRODUCTS, tiles, RHS, 2 * RANK), BF16),
            pltpu.VMEM(sides, BF16),
            pltpu.VMEM(sides, BF16),
            pltpu.VMEM(sides, BF16),
            pltpu.VMEM(sides, BF16),
            pltpu.SemaphoreType.DMA((LOADS + 1, 2)),
            pltpu.SemaphoreType.DMA((PRODUCTS,)),
            pltpu.SemaphoreType.DMA((PRODUCTS, 1 + GROUPS)),
            pltpu.SemaphoreType.DMA((PRODUCTS, 4)),
        ],
        compiler_params=pltpu.CompilerParams(
            collective_id=0, has_side_effects=True, vmem_limit_bytes=61 * 1024 * 1024
        ),
        name="h2_products",
    )(
        start_vector,
        leaf_size,
        diag_blocks,
        near_blocks,
        near_count,
        near_first,
        near_second,
        leaf_basis,
        transfer,
        coupling.transpose(1, 2, 0),
        send_slot,
        far_target,
    )


def solution(mesh):
    in_specs = (
        P("clu", None, None),
        P("clu"),
        P("clu", None, None),
        P("clu", None, None),
        P("clu"),
        P("clu"),
        P("clu"),
        P("clu", None, None),
        P("clu", None, None),
        P("clu", None, None),
        P("clu", None),
        P("clu", None),
    )
    out_specs = P(None, "clu", None, None)
    return jax.shard_map(
        on_device, mesh=mesh, in_specs=in_specs, out_specs=out_specs, check_vma=False
    )
```

```python
import functools

import jax
import jax.numpy as jnp
from jax import lax
from jax.experimental import pallas as pl
from jax.experimental.pallas import tpu as pltpu
from jax.sharding import PartitionSpec as P

PRODUCTS = 4
REACH = 8
NEAR = 2 * REACH + 1
GROUPS = 3
LOADS = 4
LEAVES = 4
RANK = 64
HALF = RANK // 2
RHS = 8
POINTS = 256
CAPACITY = 16
STRIDE = 4
MESH = pl.DeviceIdType.MESH
F32 = jnp.float32
BF16 = jnp.bfloat16


def nn(a, b):
    return jnp.dot(a, b, preferred_element_type=F32)


def nt(a, b):
    return lax.dot_general(a, b, (((1,), (1,)), ((), ())), preferred_element_type=F32)


def swap_halves(a):
    return pltpu.roll(a, RANK, 1)


def pairs_of(first, count):
    return [[first + i for i in range(k, min(k + 2, count))] for k in range(0, count, 2)]


def side_by_side(parts):
    return parts[0] if len(parts) == 1 else jnp.concatenate(parts, axis=1)


def kernel(
    devices,
    start,
    leaf_size,
    diag_hbm,
    near_hbm,
    near_count,
    near_first,
    near_second,
    basis,
    transfer,
    coupling,
    send_slot,
    far_target,
    out,
    raw,
    turned,
    parent_w,
    leaf_w,
    near,
    diag,
    both_basis,
    pick,
    point_mask,
    vector,
    extended,
    send,
    recv,
    x_out,
    x_in,
    near_out,
    near_in,
    load_sem,
    send_sem,
    recv_sem,
    side_sem,
):
    me = lax.axis_index("clu")
    far_count = devices - NEAR
    group = far_count // GROUPS
    load_rows = HALF // LOADS
    pair_count = 2 * devices

    def wrap(index):
        if devices & (devices - 1):
            return lax.rem(index, devices)
        return index & (devices - 1)

    def peer(j):
        return wrap(me + (j - REACH + devices))

    def close_tile(j):
        return 2 * j

    def leaf_tile(j):
        return 2 * j + 1

    def far_tile(j):
        return j + NEAR

    raw_loads = [
        [
            pltpu.make_async_copy(
                coupling.at[pl.ds(first, load_rows)],
                raw.at[pl.ds(first, load_rows)],
                load_sem.at[c, h],
            )
            for h, first in enumerate((c * load_rows, HALF + c * load_rows))
        ]
        for c in range(LOADS)
    ]
    near_load = pltpu.make_async_copy(near_hbm, near, load_sem.at[LOADS, 0])
    diag_load = pltpu.make_async_copy(diag_hbm, diag, load_sem.at[LOADS, 1])
    for loads in raw_loads:
        for load in loads:
            load.start()
    near_load.start()
    diag_load.start()

    barrier = pltpu.get_barrier_semaphore()

    def greet(step, carry):
        pl.semaphore_signal(
            barrier, inc=1, device_id=(wrap(me + step),), device_id_type=MESH
        )
        return carry

    lax.fori_loop(1, devices, greet, 0)

    point_ids = lax.broadcasted_iota(jnp.int32, (RHS, POINTS), 1)
    for l in range(LEAVES):
        inside = jnp.where(point_ids < leaf_size[l], 1.0, 0.0)
        point_mask[l] = inside
        vector[l] = start[l] * inside
    for e in range(CAPACITY):
        live = e < near_count[0]
        for t in range(LEAVES):
            pick[e, t] = jnp.where(live & (near_first[e] == t), 1.0, 0.0)
        for s in range(2 * LEAVES):
            pick[e, LEAVES + s] = jnp.where(live & (near_second[e] == s), 1.0, 0.0)

    for l in range(LEAVES):
        moved = transfer[l].T
        high = moved.astype(BF16)
        low = (moved - high.astype(F32)).astype(BF16)
        own = basis[l]
        both_basis[l] = jnp.concatenate(
            [own.astype(F32), nn(high, own) + nn(low, own)], axis=0
        ).astype(BF16)

    def turn(k, carry):
        both = jnp.concatenate([raw[k], raw[k + HALF]], axis=0)
        turned[pl.ds(k, pair_count, stride=HALF), :] = both.T
        return carry

    for c in range(LOADS):
        for load in raw_loads[c]:
            load.wait()
        lax.fori_loop(c * load_rows, (c + 1) * load_rows, turn, 0, unroll=4)

    lane = lax.broadcasted_iota(jnp.int32, (RANK, 2 * RANK), 1)
    row = lax.broadcasted_iota(jnp.int32, (RANK, 2 * RANK), 0)
    unit = jnp.where(lane == row + RANK, 1.0, 0.0)
    left = lane < RANK

    def weights(column, slots):
        low = turned[pl.ds(pl.multiple_of(column * HALF, HALF), HALF), :]
        wide = jnp.where(left, jnp.concatenate([low, swap_halves(low)], axis=0), unit)
        slot = jnp.where(left, far_target[0, column], send_slot[0, column])
        return [jnp.where(slot == s, wide, 0.0).astype(BF16) for s in slots]

    def build_leaf(j, carry):
        for s, part in enumerate(weights(2 * peer(j), range(LEAVES))):
            leaf_w[j, s * RANK : (s + 1) * RANK, :] = part
        return carry

    lax.fori_loop(0, NEAR, build_leaf, 0)

    def build_parent(j, carry):
        slots = range(LEAVES, LEAVES + LEAVES // 2)
        for s, part in enumerate(weights(2 * peer(j) + 1, slots)):
            parent_w[j, s * RANK : (s + 1) * RANK, :] = part
        return carry

    lax.fori_loop(0, devices, build_parent, 0, unroll=8 if devices % 8 == 0 else 1)

    near_load.wait()
    diag_load.wait()
    pl.semaphore_wait(barrier, devices - 1)

    half = lax.broadcasted_iota(jnp.int32, (RHS, 2 * RANK), 1) < RANK

    def remote(src, dst, out_sem, in_sem, target):
        return pltpu.make_async_remote_copy(
            src_ref=src,
            dst_ref=dst,
            send_sem=out_sem,
            recv_sem=in_sem,
            device_id=(target,),
            device_id_type=MESH,
        )

    def x_copy(n):
        return remote(
            x_out.at[n], x_in.at[n], side_sem.at[n, 0], side_sem.at[n, 1], peer(REACH - 1)
        )

    def near_copy(n):
        return remote(
            near_out.at[n], near_in.at[n], side_sem.at[n, 2], side_sem.at[n, 3], peer(REACH + 1)
        )

    def far_copy(n, j, g):
        return remote(
            send.at[n, pl.ds(far_tile(j), 1)],
            recv.at[n, pl.ds(far_tile(devices + NEAR - 1 - j), 1)],
            send_sem.at[n],
            recv_sem.at[n, 1 + g],
            peer(j),
        )

    def close_copy(n, j):
        return remote(
            send.at[n, pl.ds(close_tile(j), 2)],
            recv.at[n, pl.ds(close_tile(NEAR - 1 - j), 2)],
            send_sem.at[n],
            recv_sem.at[n, 0],
            peer(j),
        )

    def product(n, carry):
        exact = [vector[l] for l in range(LEAVES)]
        rounded = [value.astype(BF16) for value in exact]
        x_out[n] = jnp.concatenate(exact, axis=0).astype(BF16)
        x_copy(n).start()

        coef = [nt(rounded[l], both_basis[l]) for l in range(LEAVES)]
        leaf_coef = jnp.concatenate(
            [
                jnp.where(half, coef[0], swap_halves(coef[1])),
                jnp.where(half, coef[2], swap_halves(coef[3])),
            ],
            axis=1,
        ).astype(BF16)
        parent_coef = jnp.where(
            half, swap_halves(coef[0] + coef[1]), coef[2] + coef[3]
        ).astype(BF16)

        def fill(values, w, first, count, place):
            for js in pairs_of(first, count):
                made = nn(values, side_by_side([w[j] for j in js]))
                for i, j in enumerate(js):
                    tile = swap_halves(made[:, i * 2 * RANK : (i + 1) * 2 * RANK]).astype(BF16)
                    if isinstance(j, int) and j == REACH:
                        recv[n, place(j)] = tile
                    else:
                        send[n, place(j)] = tile

        fill(leaf_coef, leaf_w, 0, NEAR, leaf_tile)
        fill(parent_coef, parent_w, 0, NEAR, close_tile)
        for j in range(NEAR):
            if j != REACH:
                close_copy(n, j).start()

        def send_group(g, carry):
            first = NEAR + g * group
            fill(parent_coef, parent_w, first, group, far_tile)
            for i in range(group):
                far_copy(n, first + i, g).start()
            return carry

        lax.fori_loop(0, GROUPS, send_group, 0)

        for l in range(LEAVES):
            extended[l] = rounded[l].astype(F32)

        def add_backward(step, sofar):
            for i in range(STRIDE):
                e = step * STRIDE + i
                own = extended[near_first[e]]
                spread = jnp.concatenate(
                    [own * pick[e, LEAVES + s] for s in range(2 * LEAVES)], axis=0
                ).astype(BF16)
                sofar = sofar + nn(spread, near[e])
            return sofar

        backward = lax.fori_loop(
            0,
            CAPACITY // STRIDE,
            add_backward,
            jnp.zeros((2 * LEAVES * RHS, POINTS), F32),
        )
        near_out[n] = backward[LEAVES * RHS :].astype(BF16)
        near_copy(n).start()
        total = backward[: LEAVES * RHS] + jnp.concatenate(
            [nn(rounded[l], diag[l]) for l in range(LEAVES)], axis=0
        )

        x_copy(n).wait_recv()
        following = x_in[n].astype(F32)
        for l in range(LEAVES):
            extended[LEAVES + l] = following[l * RHS : (l + 1) * RHS]

        def add_forward(step, sofar):
            for i in range(STRIDE):
                e = step * STRIDE + i
                other = extended[near_second[e]]
                spread = jnp.concatenate(
                    [other * pick[e, t] for t in range(LEAVES)], axis=0
                ).astype(BF16)
                sofar = sofar + nt(spread, near[e])
            return sofar

        total = lax.fori_loop(0, CAPACITY // STRIDE, add_forward, total)

        def take(w, first, count, place, sofar):
            for js in pairs_of(first, count):
                got = side_by_side([recv[n, place(j)] for j in js])
                sofar = sofar + nt(got, side_by_side([w[j] for j in js]))
            return sofar

        def arrived(first, count, box):
            tiles = recv.at[n, pl.ds(first, count)]
            pltpu.make_async_copy(tiles, tiles, recv_sem.at[n, box]).wait()

        arrived(0, 2 * (NEAR - 1), 0)
        leaf_far = jnp.zeros((RHS, LEAVES * RANK), F32)
        leaf_far = take(leaf_w, 0, NEAR, leaf_tile, leaf_far)
        parent_far = jnp.zeros((RHS, 2 * RANK), F32)
        parent_far = take(parent_w, 0, NEAR, close_tile, parent_far)

        def take_group(g, sofar):
            first = devices - (g + 1) * group
            arrived(far_tile(first), group, 1 + g)
            return take(parent_w, first, group, far_tile, sofar)

        parent_far = lax.fori_loop(0, GROUPS, take_group, parent_far)

        near_copy(n).wait_recv()
        total = total + near_in[n].astype(F32)
        for l in range(LEAVES):
            pair = leaf_far[:, (l // 2) * 2 * RANK : (l // 2 + 1) * 2 * RANK]
            both = jnp.where(
                half,
                pair if l % 2 == 0 else swap_halves(pair),
                swap_halves(parent_far) if l < 2 else parent_far,
            ).astype(BF16)
            value = total[l * RHS : (l + 1) * RHS] + nn(both, both_basis[l])
            value = value * point_mask[l]
            vector[l] = value
            out[n, l] = value
        return carry

    lax.fori_loop(0, PRODUCTS, product, 0)

    def finish(n, carry):
        sent = send.at[n, pl.ds(0, 2 * (NEAR - 1) + far_count)]
        pltpu.make_async_copy(sent, sent, send_sem.at[n]).wait()
        x_copy(n).wait_send()
        near_copy(n).wait_send()
        return carry

    lax.fori_loop(0, PRODUCTS, finish, 0)


def on_device(
    start_vector,
    leaf_size,
    diag_blocks,
    near_blocks,
    near_count,
    near_first,
    near_second,
    leaf_basis,
    transfer,
    coupling,
    send_slot,
    far_target,
):
    devices = lax.axis_size("clu")
    tiles = devices + NEAR
    vmem = pl.BlockSpec(memory_space=pltpu.VMEM)
    smem = pl.BlockSpec(memory_space=pltpu.SMEM)
    hbm = pl.BlockSpec(memory_space=pltpu.HBM)
    sides = (PRODUCTS, LEAVES * RHS, POINTS)
    return pl.pallas_call(
        functools.partial(kernel, devices),
        out_shape=jax.ShapeDtypeStruct((PRODUCTS, LEAVES, RHS, POINTS), F32),
        in_specs=[
            vmem,
            smem,
            hbm,
            hbm,
            smem,
            smem,
            smem,
            vmem,
            vmem,
            hbm,
            smem,
            smem,
        ],
        out_specs=vmem,
        scratch_shapes=[
            pltpu.VMEM((RANK, RANK, 2 * devices), F32),
            pltpu.VMEM((2 * devices * HALF, 2 * RANK), F32),
            pltpu.VMEM((devices, 2 * RANK, 2 * RANK), BF16),
            pltpu.VMEM((NEAR, LEAVES * RANK, 2 * RANK), BF16),
            pltpu.VMEM((CAPACITY, POINTS, POINTS), BF16),
            pltpu.VMEM((LEAVES, POINTS, POINTS), BF16),
            pltpu.VMEM((LEAVES, 2 * RANK, POINTS), BF16),
            pltpu.SMEM((CAPACITY, 3 * LEAVES), F32),
            pltpu.VMEM((LEAVES, RHS, POINTS), F32),
            pltpu.VMEM((LEAVES, RHS, POINTS), F32),
            pltpu.VMEM((2 * LEAVES, RHS, POINTS), F32),
            pltpu.VMEM((PRODUCTS, tiles, RHS, 2 * RANK), BF16),
            pltpu.VMEM((PRODUCTS, tiles, RHS, 2 * RANK), BF16),
            pltpu.VMEM(sides, BF16),
            pltpu.VMEM(sides, BF16),
            pltpu.VMEM(sides, BF16),
            pltpu.VMEM(sides, BF16),
            pltpu.SemaphoreType.DMA((LOADS + 1, 2)),
            pltpu.SemaphoreType.DMA((PRODUCTS,)),
            pltpu.SemaphoreType.DMA((PRODUCTS, 1 + GROUPS)),
            pltpu.SemaphoreType.DMA((PRODUCTS, 4)),
        ],
        compiler_params=pltpu.CompilerParams(
            collective_id=0, has_side_effects=True, vmem_limit_bytes=56 * 1024 * 1024
        ),
        name="h2_products",
    )(
        start_vector,
        leaf_size,
        diag_blocks,
        near_blocks,
        near_count,
        near_first,
        near_second,
        leaf_basis,
        transfer,
        coupling.transpose(1, 2, 0),
        send_slot,
        far_target,
    )


def solution(mesh):
    in_specs = (
        P("clu", None, None),
        P("clu"),
        P("clu", None, None),
        P("clu", None, None),
        P("clu"),
        P("clu"),
        P("clu"),
        P("clu", None, None),
        P("clu", None, None),
        P("clu", None, None),
        P("clu", None),
        P("clu", None),
    )
    out_specs = P(None, "clu", None, None)
    return jax.shard_map(
        on_device, mesh=mesh, in_specs=in_specs, out_specs=out_specs, check_vma=False
    )
```

```python
import functools

import jax
import jax.numpy as jnp
from jax import lax
from jax.experimental import pallas as pl
from jax.experimental.pallas import tpu as pltpu
from jax.sharding import PartitionSpec as P

PRODUCTS = 4
REACH = 8
CLOSE = REACH + 1
NEAR = 2 * CLOSE
GROUPS = 5
LOADS = 4
LEAVES = 4
RANK = 64
HALF = RANK // 2
RHS = 8
POINTS = 256
CAPACITY = 16
STRIDE = 4
MESH = pl.DeviceIdType.MESH
F32 = jnp.float32
BF16 = jnp.bfloat16


def nn(a, b):
    return jnp.dot(a, b, preferred_element_type=F32)


def nt(a, b):
    return lax.dot_general(a, b, (((1,), (1,)), ((), ())), preferred_element_type=F32)


def swap_halves(a):
    return pltpu.roll(a, RANK, 1)


def side_by_side(parts):
    return parts[0] if len(parts) == 1 else jnp.concatenate(parts, axis=1)


def kernel(
    devices,
    start,
    leaf_size,
    diag_hbm,
    near_hbm,
    near_count,
    near_first,
    near_second,
    basis,
    transfer,
    coupling,
    send_slot,
    far_target,
    out,
    raw,
    turned,
    parent_w,
    leaf_w,
    near,
    diag,
    both_basis,
    pick,
    point_mask,
    vector,
    extended,
    close_out,
    far_out,
    close_in,
    far_in,
    x_out,
    x_in,
    near_out,
    near_in,
    load_sem,
    hand_sem,
    handed_sem,
    send_sem,
    recv_sem,
    side_sem,
):
    me = lax.axis_index("clu")
    core = lax.rem(me, 2)
    first_core = me - core
    partner = first_core + 1 - core
    chips = devices // 2
    far_chips = chips - CLOSE
    group = far_chips // GROUPS
    load_rows = HALF // LOADS
    pair_count = 2 * devices

    def wrap(index):
        if devices & (devices - 1):
            return lax.rem(index, devices)
        return index & (devices - 1)

    def at_position(j):
        return wrap(first_core + (j - REACH + devices))

    def peer(u):
        return wrap(me + (2 * u - REACH + devices))

    before = wrap(me + (devices - 1))
    after = wrap(me + 1)

    raw_loads = [
        [
            pltpu.make_async_copy(
                coupling.at[pl.ds(first, load_rows)],
                raw.at[pl.ds(first, load_rows)],
                load_sem.at[c, h],
            )
            for h, first in enumerate((c * load_rows, HALF + c * load_rows))
        ]
        for c in range(LOADS)
    ]
    near_load = pltpu.make_async_copy(near_hbm, near, load_sem.at[LOADS, 0])
    diag_load = pltpu.make_async_copy(diag_hbm, diag, load_sem.at[LOADS, 1])
    for loads in raw_loads:
        for load in loads:
            load.start()
    near_load.start()
    diag_load.start()

    barrier = pltpu.get_barrier_semaphore()

    def greet(target):
        pl.semaphore_signal(barrier, inc=1, device_id=(target,), device_id_type=MESH)

    def greet_chip(step, carry):
        greet(wrap(me + 2 * step))
        return carry

    greet(before)
    greet(after)
    lax.fori_loop(1, chips, greet_chip, 0, unroll=9 if chips % 9 == 1 else 1)

    point_ids = lax.broadcasted_iota(jnp.int32, (RHS, POINTS), 1)
    for l in range(LEAVES):
        inside = jnp.where(point_ids < leaf_size[l], 1.0, 0.0)
        point_mask[l] = inside
        vector[l] = start[l] * inside

    for l in range(LEAVES):
        moved = transfer[l].T
        high = moved.astype(BF16)
        low = (moved - high.astype(F32)).astype(BF16)
        own = basis[l]
        both_basis[l] = jnp.concatenate(
            [own.astype(F32), nn(high, own) + nn(low, own)], axis=0
        ).astype(BF16)

    def turn(k, carry):
        both = jnp.concatenate([raw[k], raw[k + HALF]], axis=0)
        turned[pl.ds(k, pair_count, stride=HALF), :] = both.T
        e = k // 2
        live = e < near_count[0]
        for i in range(6):
            column = 6 * (k % 2) + i
            leaf = jnp.where(column < LEAVES, near_first[e], near_second[e] + LEAVES)
            pick[e, column] = jnp.where(live & (leaf == column), 1.0, 0.0)
        return carry

    for c in range(LOADS):
        for load in raw_loads[c]:
            load.wait()
        lax.fori_loop(c * load_rows, (c + 1) * load_rows, turn, 0, unroll=4)

    lane = lax.broadcasted_iota(jnp.int32, (RANK, 2 * RANK), 1)
    row = lax.broadcasted_iota(jnp.int32, (RANK, 2 * RANK), 0)
    unit = jnp.where(lane == row + RANK, 1.0, 0.0)
    left = lane < RANK

    def weights(column, slots):
        low = turned[pl.ds(pl.multiple_of(column * HALF, HALF), HALF), :]
        wide = jnp.where(left, jnp.concatenate([low, swap_halves(low)], axis=0), unit)
        slot = jnp.where(left, far_target[0, column], send_slot[0, column])
        return [jnp.where(slot == s, wide, 0.0).astype(BF16) for s in slots]

    def build_leaf(j, carry):
        for s, part in enumerate(weights(2 * at_position(j), range(LEAVES))):
            leaf_w[j, s * RANK : (s + 1) * RANK, :] = part
        return carry

    lax.fori_loop(0, NEAR, build_leaf, 0, unroll=2)

    def build_parent(j, carry):
        slots = range(LEAVES, LEAVES + LEAVES // 2)
        for s, part in enumerate(weights(2 * at_position(j) + 1, slots)):
            parent_w[j, s * RANK : (s + 1) * RANK, :] = part
        return carry

    lax.fori_loop(0, devices, build_parent, 0, unroll=8 if devices % 8 == 0 else 1)

    near_load.wait()
    diag_load.wait()
    pl.semaphore_wait(barrier, chips + 1)

    half = lax.broadcasted_iota(jnp.int32, (RHS, 2 * RANK), 1) < RANK

    def remote(src, dst, out_sem, in_sem, target):
        return pltpu.make_async_remote_copy(
            src_ref=src,
            dst_ref=dst,
            send_sem=out_sem,
            recv_sem=in_sem,
            device_id=(target,),
            device_id_type=MESH,
        )

    def x_copy(n):
        return remote(
            x_out.at[n], x_in.at[n], side_sem.at[n, 0], side_sem.at[n, 1], before
        )

    def near_copy(n):
        return remote(
            near_out.at[n], near_in.at[n], side_sem.at[n, 2], side_sem.at[n, 3], after
        )

    def hand_close(n, level):
        return remote(
            close_out.at[n, :, 4 + level],
            close_out.at[n, :, 2 * level + core],
            hand_sem.at[n, 0],
            handed_sem.at[n, 0],
            partner,
        )

    def hand_far(n, g):
        chips_of = pl.ds(g * group, group)
        return remote(
            far_out.at[n, chips_of, 2],
            far_out.at[n, chips_of, core],
            hand_sem.at[n, 1],
            handed_sem.at[n, 1 + g],
            partner,
        )

    def send_close(n, u):
        return remote(
            close_out.at[n, u, pl.ds(0, 4)],
            close_in.at[n, CLOSE - 1 - u],
            send_sem.at[n, 0],
            recv_sem.at[n, 0],
            peer(u),
        )

    def send_far(n, f, g):
        return remote(
            far_out.at[n, f, pl.ds(0, 2)],
            far_in.at[n, far_chips - 1 - f],
            send_sem.at[n, 1],
            recv_sem.at[n, 1 + g],
            peer(f + CLOSE),
        )

    def wait_for(tiles, sem):
        pltpu.make_async_copy(tiles, tiles, sem).wait()

    def product(n, carry):
        exact = [vector[l] for l in range(LEAVES)]
        rounded = [value.astype(BF16) for value in exact]
        x_out[n] = jnp.concatenate(exact, axis=0).astype(BF16)
        x_copy(n).start()

        coef = [nt(rounded[l], both_basis[l]) for l in range(LEAVES)]
        leaf_coef = jnp.concatenate(
            [
                jnp.where(half, coef[0], swap_halves(coef[1])),
                jnp.where(half, coef[2], swap_halves(coef[3])),
            ],
            axis=1,
        ).astype(BF16)
        parent_coef = jnp.where(
            half, swap_halves(coef[0] + coef[1]), coef[2] + coef[3]
        ).astype(BF16)

        def made(values, w, u):
            both = nn(values, side_by_side([w[2 * u], w[2 * u + 1]]))
            return [swap_halves(both[:, : 2 * RANK]), swap_halves(both[:, 2 * RANK :])]

        for u in range(CLOSE):
            for level, (values, w) in enumerate(
                ((parent_coef, parent_w), (leaf_coef, leaf_w))
            ):
                first, second = made(values, w, u)
                close_out[n, u, 2 * level + core * (4 - level)] = first.astype(BF16)
                close_out[n, u, 4 + level - core * (3 - level)] = second.astype(BF16)
        for level in range(2):
            hand_close(n, level).start()

        def fill_group(g):
            for i in range(group):
                f = g * group + i
                first, second = made(parent_coef, parent_w, f + CLOSE)
                far_out[n, f, 2 * core] = first.astype(BF16)
                far_out[n, f, 2 - core] = second.astype(BF16)
            hand_far(n, g).start()

        def send_group(g):
            wait_for(far_out.at[n, pl.ds(g * group, group), 0], handed_sem.at[n, 1 + g])
            for i in range(group):
                send_far(n, g * group + i, g).start()

        fill_group(0)
        wait_for(close_out.at[n, :, pl.ds(0, 2)], handed_sem.at[n, 0])
        for u in range(CLOSE):
            if u != REACH // 2:
                send_close(n, u).start()

        def fill_and_send(g, carry):
            fill_group(g)
            send_group(g - 1)
            return carry

        lax.fori_loop(1, GROUPS, fill_and_send, 0)

        for l in range(LEAVES):
            extended[l] = rounded[l].astype(F32)

        def add_backward(step, sofar):
            for i in range(STRIDE):
                e = step * STRIDE + i
                own = extended[near_first[e]]
                spread = jnp.concatenate(
                    [own * pick[e, LEAVES + s] for s in range(2 * LEAVES)], axis=0
                ).astype(BF16)
                sofar = sofar + nn(spread, near[e])
            return sofar

        backward = lax.fori_loop(
            0, 2, add_backward, jnp.zeros((2 * LEAVES * RHS, POINTS), F32)
        )
        send_group(GROUPS - 1)
        backward = lax.fori_loop(2, CAPACITY // STRIDE, add_backward, backward)
        near_out[n] = backward[LEAVES * RHS :].astype(BF16)
        near_copy(n).start()
        total = backward[: LEAVES * RHS] + jnp.concatenate(
            [nn(rounded[l], diag[l]) for l in range(LEAVES)], axis=0
        )

        x_copy(n).wait_recv()
        following = x_in[n].astype(F32)
        for l in range(LEAVES):
            extended[LEAVES + l] = following[l * RHS : (l + 1) * RHS]

        def add_forward(step, sofar):
            for i in range(STRIDE):
                e = step * STRIDE + i
                other = extended[near_second[e]]
                spread = jnp.concatenate(
                    [other * pick[e, t] for t in range(LEAVES)], axis=0
                ).astype(BF16)
                sofar = sofar + nt(spread, near[e])
            return sofar

        total = lax.fori_loop(0, CAPACITY // STRIDE, add_forward, total)

        def taken(tiles, w, u, sofar):
            return sofar + nt(
                side_by_side(tiles), side_by_side([w[2 * u], w[2 * u + 1]])
            )

        wait_for(close_in.at[n, pl.ds(0, CLOSE - 1)], recv_sem.at[n, 0])
        leaf_far = jnp.zeros((RHS, LEAVES * RANK), F32)
        parent_far = jnp.zeros((RHS, 2 * RANK), F32)
        for u in range(CLOSE):
            box = close_out if u == REACH // 2 else close_in
            tiles = [box[n, u, s] for s in range(4)]
            parent_far = taken(tiles[:2], parent_w, u, parent_far)
            leaf_far = taken(tiles[2:], leaf_w, u, leaf_far)

        def take_group(g, sofar):
            first = far_chips - (g + 1) * group
            wait_for(far_in.at[n, pl.ds(first, group)], recv_sem.at[n, 1 + g])
            for i in range(group):
                f = first + i
                tiles = [far_in[n, f, s] for s in range(2)]
                sofar = taken(tiles, parent_w, f + CLOSE, sofar)
            return sofar

        parent_far = lax.fori_loop(0, GROUPS, take_group, parent_far)

        near_copy(n).wait_recv()
        total = total + near_in[n].astype(F32)
        for l in range(LEAVES):
            pair = leaf_far[:, (l // 2) * 2 * RANK : (l // 2 + 1) * 2 * RANK]
            both = jnp.where(
                half,
                pair if l % 2 == 0 else swap_halves(pair),
                swap_halves(parent_far) if l < 2 else parent_far,
            ).astype(BF16)
            value = total[l * RHS : (l + 1) * RHS] + nn(both, both_basis[l])
            value = value * point_mask[l]
            vector[l] = value
            out[n, l] = value
        return carry

    lax.fori_loop(0, PRODUCTS, product, 0)

    def finish(n, carry):
        wait_for(close_out.at[n, :, pl.ds(4, 2)], hand_sem.at[n, 0])
        wait_for(far_out.at[n, :, 2], hand_sem.at[n, 1])
        wait_for(close_out.at[n, pl.ds(0, CLOSE - 1), pl.ds(0, 4)], send_sem.at[n, 0])
        wait_for(far_out.at[n, :, pl.ds(0, 2)], send_sem.at[n, 1])
        x_copy(n).wait_send()
        near_copy(n).wait_send()
        return carry

    lax.fori_loop(0, PRODUCTS, finish, 0)


def on_device(
    start_vector,
    leaf_size,
    diag_blocks,
    near_blocks,
    near_count,
    near_first,
    near_second,
    leaf_basis,
    transfer,
    coupling,
    send_slot,
    far_target,
):
    devices = lax.axis_size("clu")
    far_chips = devices // 2 - CLOSE
    tile = (RHS, 2 * RANK)
    vmem = pl.BlockSpec(memory_space=pltpu.VMEM)
    smem = pl.BlockSpec(memory_space=pltpu.SMEM)
    hbm = pl.BlockSpec(memory_space=pltpu.HBM)
    sides = (PRODUCTS, LEAVES * RHS, POINTS)
    return pl.pallas_call(
        functools.partial(kernel, devices),
        out_shape=jax.ShapeDtypeStruct((PRODUCTS, LEAVES, RHS, POINTS), F32),
        in_specs=[
            vmem,
            smem,
            hbm,
            hbm,
            smem,
            smem,
            smem,
            vmem,
            vmem,
            hbm,
            smem,
            smem,
        ],
        out_specs=vmem,
        scratch_shapes=[
            pltpu.VMEM((RANK, RANK, 2 * devices), F32),
            pltpu.VMEM((2 * devices * HALF, 2 * RANK), F32),
            pltpu.VMEM((devices, 2 * RANK, 2 * RANK), BF16),
            pltpu.VMEM((NEAR, LEAVES * RANK, 2 * RANK), BF16),
            pltpu.VMEM((CAPACITY, POINTS, POINTS), BF16),
            pltpu.VMEM((LEAVES, POINTS, POINTS), BF16),
            pltpu.VMEM((LEAVES, 2 * RANK, POINTS), BF16),
            pltpu.SMEM((CAPACITY, 3 * LEAVES), F32),
            pltpu.VMEM((LEAVES, RHS, POINTS), F32),
            pltpu.VMEM((LEAVES, RHS, POINTS), F32),
            pltpu.VMEM((2 * LEAVES, RHS, POINTS), F32),
            pltpu.VMEM((PRODUCTS, CLOSE, 6, *tile), BF16),
            pltpu.VMEM((PRODUCTS, far_chips, 3, *tile), BF16),
            pltpu.VMEM((PRODUCTS, CLOSE, 4, *tile), BF16),
            pltpu.VMEM((PRODUCTS, far_chips, 2, *tile), BF16),
            pltpu.VMEM(sides, BF16),
            pltpu.VMEM(sides, BF16),
            pltpu.VMEM(sides, BF16),
            pltpu.VMEM(sides, BF16),
            pltpu.SemaphoreType.DMA((LOADS + 1, 2)),
            pltpu.SemaphoreType.DMA((PRODUCTS, 2)),
            pltpu.SemaphoreType.DMA((PRODUCTS, 1 + GROUPS)),
            pltpu.SemaphoreType.DMA((PRODUCTS, 2)),
            pltpu.SemaphoreType.DMA((PRODUCTS, 1 + GROUPS)),
            pltpu.SemaphoreType.DMA((PRODUCTS, 4)),
        ],
        compiler_params=pltpu.CompilerParams(
            collective_id=0, has_side_effects=True, vmem_limit_bytes=56 * 1024 * 1024
        ),
        name="h2_products",
    )(
        start_vector,
        leaf_size,
        diag_blocks,
        near_blocks,
        near_count,
        near_first,
        near_second,
        leaf_basis,
        transfer,
        coupling.transpose(1, 2, 0),
        send_slot,
        far_target,
    )


def solution(mesh):
    in_specs = (
        P("clu", None, None),
        P("clu"),
        P("clu", None, None),
        P("clu", None, None),
        P("clu"),
        P("clu"),
        P("clu"),
        P("clu", None, None),
        P("clu", None, None),
        P("clu", None, None),
        P("clu", None),
        P("clu", None),
    )
    out_specs = P(None, "clu", None, None)
    return jax.shard_map(
        on_device, mesh=mesh, in_specs=in_specs, out_specs=out_specs, check_vma=False
    )
```

```python
import functools
import math

import jax
import jax.numpy as jnp
from jax import lax
from jax.experimental import pallas as pl
from jax.experimental.pallas import tpu as pltpu
from jax.sharding import PartitionSpec as P

PRODUCTS = 4
REACH = 8
CLOSE = REACH + 1
NEAR = 2 * REACH + 1
GROUPS = 3
LOADS = 4
LEAVES = 4
RANK = 64
HALF = RANK // 2
RHS = 8
POINTS = 256
CAPACITY = 16
STRIDE = 4
MESH = pl.DeviceIdType.MESH
F32 = jnp.float32
BF16 = jnp.bfloat16


def nn(a, b):
    return jnp.dot(a, b, preferred_element_type=F32)


def nt(a, b):
    return lax.dot_general(a, b, (((1,), (1,)), ((), ())), preferred_element_type=F32)


def swap_halves(a):
    return pltpu.roll(a, RANK, 1)


def pairs_of(first, count):
    return [[first + i for i in range(k, min(k + 2, count))] for k in range(0, count, 2)]


def side_by_side(parts):
    return parts[0] if len(parts) == 1 else jnp.concatenate(parts, axis=1)


def kernel(
    devices,
    start_hbm,
    leaf_size,
    diag_hbm,
    near_hbm,
    near_count,
    near_first,
    near_second,
    basis_hbm,
    transfer_hbm,
    coupling,
    send_slot,
    far_target,
    out_hbm,
    start,
    basis,
    transfer,
    raw,
    turned,
    parent_w,
    leaf_w,
    near,
    diag,
    both_basis,
    pick,
    point_mask,
    vector,
    out,
    extended,
    send,
    recv,
    x_out,
    x_in,
    near_out,
    near_in,
    load_sem,
    out_sem,
    send_sem,
    recv_sem,
    side_sem,
):
    me = lax.axis_index("clu")
    far_count = devices - NEAR
    group = far_count // GROUPS
    load_rows = HALF // LOADS
    pair_count = 2 * devices

    def wrap(index):
        if devices & (devices - 1):
            return lax.rem(index, devices)
        return index & (devices - 1)

    def peer(j):
        return wrap(me + (j - REACH + devices))

    def far_peer(g, i):
        return wrap(me + (CLOSE + GROUPS * i) + g)

    def close_tile(j):
        return 2 * j

    def leaf_tile(j):
        return 2 * j + 1

    def far_tile(j):
        return j + NEAR

    raw_loads = [
        [
            pltpu.make_async_copy(
                coupling.at[pl.ds(first, load_rows)],
                raw.at[pl.ds(first, load_rows)],
                load_sem.at[c, h],
            )
            for h, first in enumerate((c * load_rows, HALF + c * load_rows))
        ]
        for c in range(LOADS)
    ]
    near_load = pltpu.make_async_copy(near_hbm, near, load_sem.at[LOADS, 0])
    diag_load = pltpu.make_async_copy(diag_hbm, diag, load_sem.at[LOADS, 1])
    small_loads = [
        pltpu.make_async_copy(start_hbm, start, load_sem.at[LOADS + 1, 0]),
        pltpu.make_async_copy(basis_hbm, basis, load_sem.at[LOADS + 1, 1]),
        pltpu.make_async_copy(transfer_hbm, transfer, load_sem.at[LOADS + 2, 0]),
    ]
    for loads in raw_loads:
        for load in loads:
            load.start()
    for load in small_loads:
        load.start()
    near_load.start()
    diag_load.start()

    barrier = pltpu.get_barrier_semaphore()

    def greet(step):
        pl.semaphore_signal(
            barrier, inc=1, device_id=(wrap(me + step),), device_id_type=MESH
        )

    turns = HALF - load_rows
    greetings = (devices - 1) // turns
    for step in range(1 + turns * greetings, devices):
        greet(step)

    for load in small_loads:
        load.wait()

    point_ids = lax.broadcasted_iota(jnp.int32, (RHS, POINTS), 1)
    for l in range(LEAVES):
        inside = jnp.where(point_ids < leaf_size[l], 1.0, 0.0)
        point_mask[l] = inside
        vector[l] = start[l] * inside

    for l in range(LEAVES):
        moved = transfer[l].T
        high = moved.astype(BF16)
        low = (moved - high.astype(F32)).astype(BF16)
        own = basis[l]
        both_basis[l] = jnp.concatenate(
            [own.astype(F32), nn(high, own) + nn(low, own)], axis=0
        ).astype(BF16)

    def turn(k, signals):
        both = jnp.concatenate([raw[k], raw[k + HALF]], axis=0)
        turned[pl.ds(k, pair_count, stride=HALF), :] = both.T
        for i in range(signals):
            greet(1 + signals * k + i)
        e = k // 2
        live = e < near_count[0]
        for i in range(6):
            column = 6 * (k % 2) + i
            leaf = jnp.where(column < LEAVES, near_first[e], near_second[e] + LEAVES)
            pick[e, column] = jnp.where(live & (leaf == column), 1.0, 0.0)

    for c in range(LOADS):
        for load in raw_loads[c]:
            load.wait()
        signals = greetings if c < LOADS - 1 else 0
        lax.fori_loop(
            c * load_rows,
            (c + 1) * load_rows,
            lambda k, carry: (turn(k, signals), carry)[1],
            0,
            unroll=4,
        )

    lane = lax.broadcasted_iota(jnp.int32, (RANK, 2 * RANK), 1)
    row = lax.broadcasted_iota(jnp.int32, (RANK, 2 * RANK), 0)
    unit = jnp.where(lane == row + RANK, 1.0, 0.0).astype(BF16)
    left = lax.broadcasted_iota(jnp.int32, (2 * RHS, 2 * RANK), 1) < RANK

    def repeated(mask):
        return jnp.concatenate([mask.astype(BF16)] * (RANK // (2 * RHS)), axis=0)

    def build(w, j, device, level, slots):
        column = 2 * device + level
        low = turned[pl.ds(pl.multiple_of(column * HALF, HALF), HALF), :]
        wide = jnp.concatenate([low, swap_halves(low)], axis=0).astype(BF16)
        target, source = far_target[0, column], send_slot[0, column]
        for i, s in enumerate(slots):
            coupled = jnp.where(left, jnp.where(target == s, 1.0, 0.0), 0.0)
            handed = jnp.where(left, 0.0, jnp.where(source == s, 1.0, 0.0))
            w[j, i * RANK : (i + 1) * RANK, :] = wide * repeated(coupled) + unit * repeated(
                handed
            )

    leaf_slots = range(LEAVES)
    parent_slots = range(LEAVES, LEAVES + LEAVES // 2)

    def build_near(j, carry):
        build(leaf_w, j, peer(j), 0, leaf_slots)
        build(parent_w, j, peer(j), 1, parent_slots)
        return carry

    def build_far(i, carry):
        for g in range(GROUPS):
            build(parent_w, NEAR + g * group + i, far_peer(g, i), 1, parent_slots)
        return carry

    lax.fori_loop(0, NEAR, build_near, 0)
    lax.fori_loop(0, group, build_far, 0)

    near_load.wait()
    diag_load.wait()
    pl.semaphore_wait(barrier, devices - 1)

    half = lax.broadcasted_iota(jnp.int32, (RHS, 2 * RANK), 1) < RANK

    def remote(src, dst, out_sem, in_sem, target):
        return pltpu.make_async_remote_copy(
            src_ref=src,
            dst_ref=dst,
            send_sem=out_sem,
            recv_sem=in_sem,
            device_id=(target,),
            device_id_type=MESH,
        )

    def x_copy(n):
        return remote(
            x_out.at[n], x_in.at[n], side_sem.at[n, 0], side_sem.at[n, 1], peer(REACH - 1)
        )

    def near_copy(n):
        return remote(
            near_out.at[n], near_in.at[n], side_sem.at[n, 2], side_sem.at[n, 3], peer(REACH + 1)
        )

    def out_copy(n):
        return pltpu.make_async_copy(out.at[n], out_hbm.at[n], out_sem.at[n])

    def far_copy(n, g, i):
        w = g * group + i
        return remote(
            send.at[n, pl.ds(2 * NEAR + w, 1)],
            recv.at[n, pl.ds(2 * NEAR + far_count - 1 - w, 1)],
            send_sem.at[n],
            recv_sem.at[n, 1 + g],
            far_peer(g, i),
        )

    def close_copy(n, j):
        return remote(
            send.at[n, pl.ds(close_tile(j), 2)],
            recv.at[n, pl.ds(close_tile(NEAR - 1 - j), 2)],
            send_sem.at[n],
            recv_sem.at[n, 0],
            peer(j),
        )

    spread_by = next(k for k in range(3 * group // 8, group + 2) if k and math.gcd(k, group) == 1)
    order = [i * spread_by % group for i in range(group)]

    def product(n, carry):
        exact = [vector[l] for l in range(LEAVES)]
        rounded = [value.astype(BF16) for value in exact]
        x_out[n] = jnp.concatenate(exact, axis=0).astype(BF16)
        x_copy(n).start()

        coef = [nt(rounded[l], both_basis[l]) for l in range(LEAVES)]
        leaf_coef = jnp.concatenate(
            [
                jnp.where(half, coef[0], swap_halves(coef[1])),
                jnp.where(half, coef[2], swap_halves(coef[3])),
            ],
            axis=1,
        ).astype(BF16)
        parent_coef = jnp.where(
            half, swap_halves(coef[0] + coef[1]), coef[2] + coef[3]
        ).astype(BF16)

        def fill(values, w, js, place):
            made = nn(values, side_by_side([w[j] for j in js]))
            for i, j in enumerate(js):
                tile = swap_halves(made[:, i * 2 * RANK : (i + 1) * 2 * RANK]).astype(BF16)
                if isinstance(j, int) and j == REACH:
                    recv[n, place(j)] = tile
                else:
                    send[n, place(j)] = tile

        def far_fills(g):
            return [
                functools.partial(fill, parent_coef, parent_w, js, far_tile)
                for js in pairs_of(NEAR + g * group, group)
            ]

        def interleave(fills, g):
            done = 0
            for k, step in enumerate(fills):
                step()
                upto = (k + 1) * group // len(fills)
                for i in order[done:upto]:
                    far_copy(n, g, i).start()
                done = upto

        for step in far_fills(0):
            step()

        def fill_next(g, carry):
            interleave(far_fills(g), g - 1)
            return carry

        lax.fori_loop(1, GROUPS, fill_next, 0)
        interleave(
            [
                functools.partial(fill, values, w, js, place)
                for js in pairs_of(0, NEAR)
                for values, w, place in (
                    (parent_coef, parent_w, close_tile),
                    (leaf_coef, leaf_w, leaf_tile),
                )
            ],
            GROUPS - 1,
        )
        for j in range(NEAR):
            if j != REACH:
                close_copy(n, j).start()

        for l in range(LEAVES):
            extended[l] = rounded[l].astype(F32)

        def add_backward(step, sofar):
            for i in range(STRIDE):
                e = step * STRIDE + i
                own = extended[near_first[e]]
                spread = jnp.concatenate(
                    [own * pick[e, LEAVES + s] for s in range(2 * LEAVES)], axis=0
                ).astype(BF16)
                sofar = sofar + nn(spread, near[e])
            return sofar

        backward = lax.fori_loop(
            0,
            CAPACITY // STRIDE,
            add_backward,
            jnp.zeros((2 * LEAVES * RHS, POINTS), F32),
        )
        near_out[n] = backward[LEAVES * RHS :].astype(BF16)
        near_copy(n).start()
        total = backward[: LEAVES * RHS] + jnp.concatenate(
            [nn(rounded[l], diag[l]) for l in range(LEAVES)], axis=0
        )

        x_copy(n).wait_recv()
        following = x_in[n].astype(F32)
        for l in range(LEAVES):
            extended[LEAVES + l] = following[l * RHS : (l + 1) * RHS]

        def add_forward(step, sofar):
            for i in range(STRIDE):
                e = step * STRIDE + i
                other = extended[near_second[e]]
                spread = jnp.concatenate(
                    [other * pick[e, t] for t in range(LEAVES)], axis=0
                ).astype(BF16)
                sofar = sofar + nt(spread, near[e])
            return sofar

        total = lax.fori_loop(0, CAPACITY // STRIDE, add_forward, total)

        def take(w, first, count, place, sofar):
            for js in pairs_of(first, count):
                got = side_by_side([recv[n, place(j)] for j in js])
                sofar = sofar + nt(got, side_by_side([w[j] for j in js]))
            return sofar

        def arrived(first, count, box):
            tiles = recv.at[n, pl.ds(first, count)]
            pltpu.make_async_copy(tiles, tiles, recv_sem.at[n, box]).wait()

        arrived(0, 2 * (NEAR - 1), 0)
        leaf_far = jnp.zeros((RHS, LEAVES * RANK), F32)
        leaf_far = take(leaf_w, 0, NEAR, leaf_tile, leaf_far)
        parent_far = jnp.zeros((RHS, 2 * RANK), F32)
        parent_far = take(parent_w, 0, NEAR, close_tile, parent_far)

        def take_group(g, sofar):
            first = devices - (g + 1) * group
            arrived(far_tile(first), group, 1 + g)
            return take(parent_w, first, group, far_tile, sofar)

        parent_far = lax.fori_loop(0, GROUPS, take_group, parent_far)

        near_copy(n).wait_recv()
        total = total + near_in[n].astype(F32)
        for l in range(LEAVES):
            pair = leaf_far[:, (l // 2) * 2 * RANK : (l // 2 + 1) * 2 * RANK]
            both = jnp.where(
                half,
                pair if l % 2 == 0 else swap_halves(pair),
                swap_halves(parent_far) if l < 2 else parent_far,
            ).astype(BF16)
            value = total[l * RHS : (l + 1) * RHS] + nn(both, both_basis[l])
            value = value * point_mask[l]
            vector[l] = value
            out[n, l] = value
        out_copy(n).start()
        return carry

    lax.fori_loop(0, PRODUCTS, product, 0)

    def finish(n, carry):
        sent = send.at[n, pl.ds(0, 2 * (NEAR - 1) + far_count)]
        pltpu.make_async_copy(sent, sent, send_sem.at[n]).wait()
        x_copy(n).wait_send()
        near_copy(n).wait_send()
        out_copy(n).wait()
        return carry

    lax.fori_loop(0, PRODUCTS, finish, 0)


def on_device(
    start_vector,
    leaf_size,
    diag_blocks,
    near_blocks,
    near_count,
    near_first,
    near_second,
    leaf_basis,
    transfer,
    coupling,
    send_slot,
    far_target,
):
    devices = lax.axis_size("clu")
    tiles = devices + NEAR
    smem = pl.BlockSpec(memory_space=pltpu.SMEM)
    hbm = pl.BlockSpec(memory_space=pltpu.HBM)
    sides = (PRODUCTS, LEAVES * RHS, POINTS)
    return pl.pallas_call(
        functools.partial(kernel, devices),
        out_shape=jax.ShapeDtypeStruct((PRODUCTS, LEAVES, RHS, POINTS), F32),
        in_specs=[
            hbm,
            smem,
            hbm,
            hbm,
            smem,
            smem,
            smem,
            hbm,
            hbm,
            hbm,
            smem,
            smem,
        ],
        out_specs=hbm,
        scratch_shapes=[
            pltpu.VMEM((LEAVES, RHS, POINTS), F32),
            pltpu.VMEM((LEAVES, RANK, POINTS), BF16),
            pltpu.VMEM((LEAVES, RANK, RANK), F32),
            pltpu.VMEM((RANK, RANK, 2 * devices), F32),
            pltpu.VMEM((2 * devices * HALF, 2 * RANK), F32),
            pltpu.VMEM((devices, 2 * RANK, 2 * RANK), BF16),
            pltpu.VMEM((NEAR, LEAVES * RANK, 2 * RANK), BF16),
            pltpu.VMEM((CAPACITY, POINTS, POINTS), BF16),
            pltpu.VMEM((LEAVES, POINTS, POINTS), BF16),
            pltpu.VMEM((LEAVES, 2 * RANK, POINTS), BF16),
            pltpu.SMEM((CAPACITY, 3 * LEAVES), F32),
            pltpu.VMEM((LEAVES, RHS, POINTS), F32),
            pltpu.VMEM((LEAVES, RHS, POINTS), F32),
            pltpu.VMEM((PRODUCTS, LEAVES, RHS, POINTS), F32),
            pltpu.VMEM((2 * LEAVES, RHS, POINTS), F32),
            pltpu.VMEM((PRODUCTS, tiles, RHS, 2 * RANK), BF16),
            pltpu.VMEM((PRODUCTS, tiles, RHS, 2 * RANK), BF16),
            pltpu.VMEM(sides, BF16),
            pltpu.VMEM(sides, BF16),
            pltpu.VMEM(sides, BF16),
            pltpu.VMEM(sides, BF16),
            pltpu.SemaphoreType.DMA((LOADS + 3, 2)),
            pltpu.SemaphoreType.DMA((PRODUCTS,)),
            pltpu.SemaphoreType.DMA((PRODUCTS,)),
            pltpu.SemaphoreType.DMA((PRODUCTS, 1 + GROUPS)),
            pltpu.SemaphoreType.DMA((PRODUCTS, 4)),
        ],
        compiler_params=pltpu.CompilerParams(
            collective_id=0, has_side_effects=True, vmem_limit_bytes=56 * 1024 * 1024
        ),
        name="h2_products",
    )(
        start_vector,
        leaf_size,
        diag_blocks,
        near_blocks,
        near_count,
        near_first,
        near_second,
        leaf_basis,
        transfer,
        coupling.transpose(1, 2, 0),
        send_slot,
        far_target,
    )


def solution(mesh):
    in_specs = (
        P("clu", None, None),
        P("clu"),
        P("clu", None, None),
        P("clu", None, None),
        P("clu"),
        P("clu"),
        P("clu"),
        P("clu", None, None),
        P("clu", None, None),
        P("clu", None, None),
        P("clu", None),
        P("clu", None),
    )
    out_specs = P(None, "clu", None, None)
    return jax.shard_map(
        on_device, mesh=mesh, in_specs=in_specs, out_specs=out_specs, check_vma=False
    )
```

```python
import functools
import math

import jax
import jax.numpy as jnp
from jax import lax
from jax.experimental import pallas as pl
from jax.experimental.pallas import tpu as pltpu
from jax.sharding import PartitionSpec as P

PRODUCTS = 4
REACH = 8
CLOSE = REACH + 1
NEAR = 2 * REACH + 1
GROUPS = 3
LOADS = 4
LEAVES = 4
RANK = 64
HALF = RANK // 2
RHS = 8
POINTS = 256
CAPACITY = 16
STRIDE = 4
MESH = pl.DeviceIdType.MESH
F32 = jnp.float32
BF16 = jnp.bfloat16


def nn(a, b):
    return jnp.dot(a, b, preferred_element_type=F32)


def nt(a, b):
    return lax.dot_general(a, b, (((1,), (1,)), ((), ())), preferred_element_type=F32)


def swap_halves(a):
    return pltpu.roll(a, RANK, 1)


def pairs_of(first, count):
    return [[first + i for i in range(k, min(k + 2, count))] for k in range(0, count, 2)]


def side_by_side(parts):
    return parts[0] if len(parts) == 1 else jnp.concatenate(parts, axis=1)


def kernel(
    devices,
    start_hbm,
    leaf_size,
    diag_hbm,
    near_hbm,
    near_count,
    near_first,
    near_second,
    basis_hbm,
    transfer_hbm,
    coupling,
    send_slot,
    far_target,
    out_hbm,
    start,
    basis,
    transfer,
    raw,
    turned,
    parent_w,
    leaf_w,
    near,
    diag,
    both_basis,
    pick,
    point_mask,
    vector,
    out,
    extended,
    send,
    recv,
    x_out,
    x_in,
    near_out,
    near_in,
    load_sem,
    out_sem,
    send_sem,
    recv_sem,
    side_sem,
):
    me = lax.axis_index("clu")
    far_count = devices - NEAR
    group = far_count // GROUPS
    load_rows = HALF // LOADS
    pair_count = 2 * devices

    def wrap(index):
        if devices & (devices - 1):
            return lax.rem(index, devices)
        return index & (devices - 1)

    def peer(j):
        return wrap(me + (j - REACH + devices))

    def far_peer(g, i):
        return wrap(me + (CLOSE + GROUPS * i) + g)

    def close_tile(j):
        return 2 * j

    def leaf_tile(j):
        return 2 * j + 1

    def far_tile(j):
        return j + NEAR

    raw_loads = [
        [
            pltpu.make_async_copy(
                coupling.at[pl.ds(first, load_rows)],
                raw.at[pl.ds(first, load_rows)],
                load_sem.at[c, h],
            )
            for h, first in enumerate((c * load_rows, HALF + c * load_rows))
        ]
        for c in range(LOADS)
    ]
    near_load = pltpu.make_async_copy(near_hbm, near, load_sem.at[LOADS, 0])
    diag_load = pltpu.make_async_copy(diag_hbm, diag, load_sem.at[LOADS, 1])
    small_loads = [
        pltpu.make_async_copy(start_hbm, start, load_sem.at[LOADS + 1, 0]),
        pltpu.make_async_copy(basis_hbm, basis, load_sem.at[LOADS + 1, 1]),
        pltpu.make_async_copy(transfer_hbm, transfer, load_sem.at[LOADS + 2, 0]),
    ]
    for loads in raw_loads:
        for load in loads:
            load.start()
    for load in small_loads:
        load.start()
    near_load.start()
    diag_load.start()

    barrier = pltpu.get_barrier_semaphore()

    def greet(step, carry):
        pl.semaphore_signal(
            barrier, inc=1, device_id=(wrap(me + step),), device_id_type=MESH
        )
        return carry

    lax.fori_loop(1, devices, greet, 0)

    for load in small_loads:
        load.wait()

    point_ids = lax.broadcasted_iota(jnp.int32, (RHS, POINTS), 1)
    for l in range(LEAVES):
        inside = jnp.where(point_ids < leaf_size[l], 1.0, 0.0)
        point_mask[l] = inside
        vector[l] = start[l] * inside

    for l in range(LEAVES):
        moved = transfer[l].T
        high = moved.astype(BF16)
        low = (moved - high.astype(F32)).astype(BF16)
        own = basis[l]
        both_basis[l] = jnp.concatenate(
            [own.astype(F32), nn(high, own) + nn(low, own)], axis=0
        ).astype(BF16)

    def turn(k, carry):
        both = jnp.concatenate([raw[k], raw[k + HALF]], axis=0)
        turned[pl.ds(k, pair_count, stride=HALF), :] = both.T
        e = k // 2
        live = e < near_count[0]
        for i in range(6):
            column = 6 * (k % 2) + i
            leaf = jnp.where(column < LEAVES, near_first[e], near_second[e] + LEAVES)
            pick[e, column] = jnp.where(live & (leaf == column), 1.0, 0.0)
        return carry

    for c in range(LOADS):
        for load in raw_loads[c]:
            load.wait()
        lax.fori_loop(c * load_rows, (c + 1) * load_rows, turn, 0, unroll=4)

    lane = lax.broadcasted_iota(jnp.int32, (RANK, 2 * RANK), 1)
    row = lax.broadcasted_iota(jnp.int32, (RANK, 2 * RANK), 0)
    unit = jnp.where(lane == row + RANK, 1.0, 0.0).astype(BF16)
    left = lax.broadcasted_iota(jnp.int32, (2 * RHS, 2 * RANK), 1) < RANK

    def repeated(mask):
        return jnp.concatenate([mask.astype(BF16)] * (RANK // (2 * RHS)), axis=0)

    def build(w, j, device, level, slots):
        column = 2 * device + level
        low = turned[pl.ds(pl.multiple_of(column * HALF, HALF), HALF), :]
        wide = jnp.concatenate([low, swap_halves(low)], axis=0).astype(BF16)
        target, source = far_target[0, column], send_slot[0, column]
        for i, s in enumerate(slots):
            coupled = jnp.where(left, jnp.where(target == s, 1.0, 0.0), 0.0)
            handed = jnp.where(left, 0.0, jnp.where(source == s, 1.0, 0.0))
            w[j, i * RANK : (i + 1) * RANK, :] = wide * repeated(coupled) + unit * repeated(
                handed
            )

    leaf_slots = range(LEAVES)
    parent_slots = range(LEAVES, LEAVES + LEAVES // 2)

    def build_near(j, carry):
        build(leaf_w, j, peer(j), 0, leaf_slots)
        build(parent_w, j, peer(j), 1, parent_slots)
        return carry

    def build_far(i, carry):
        for g in range(GROUPS):
            build(parent_w, NEAR + g * group + i, far_peer(g, i), 1, parent_slots)
        return carry

    lax.fori_loop(0, NEAR, build_near, 0)
    lax.fori_loop(0, group, build_far, 0)

    near_load.wait()
    diag_load.wait()
    pl.semaphore_wait(barrier, devices - 1)

    half = lax.broadcasted_iota(jnp.int32, (RHS, 2 * RANK), 1) < RANK

    def remote(src, dst, out_sem, in_sem, target):
        return pltpu.make_async_remote_copy(
            src_ref=src,
            dst_ref=dst,
            send_sem=out_sem,
            recv_sem=in_sem,
            device_id=(target,),
            device_id_type=MESH,
        )

    def x_copy(n):
        return remote(
            x_out.at[n], x_in.at[n], side_sem.at[n, 0], side_sem.at[n, 1], peer(REACH - 1)
        )

    def near_copy(n):
        return remote(
            near_out.at[n], near_in.at[n], side_sem.at[n, 2], side_sem.at[n, 3], peer(REACH + 1)
        )

    def out_copy(n):
        return pltpu.make_async_copy(out.at[n], out_hbm.at[n], out_sem.at[n])

    def far_copy(n, g, i):
        w = g * group + i
        return remote(
            send.at[n, pl.ds(2 * NEAR + w, 1)],
            recv.at[n, pl.ds(2 * NEAR + far_count - 1 - w, 1)],
            send_sem.at[n],
            recv_sem.at[n, 1 + g],
            far_peer(g, i),
        )

    def close_copy(n, j):
        return remote(
            send.at[n, pl.ds(close_tile(j), 2)],
            recv.at[n, pl.ds(close_tile(NEAR - 1 - j), 2)],
            send_sem.at[n],
            recv_sem.at[n, 0],
            peer(j),
        )

    spread_by = next(k for k in range(3 * group // 8, group + 2) if k and math.gcd(k, group) == 1)
    order = [i * spread_by % group for i in range(group)]

    def product(n, carry):
        exact = [vector[l] for l in range(LEAVES)]
        rounded = [value.astype(BF16) for value in exact]
        x_out[n] = jnp.concatenate(exact, axis=0).astype(BF16)
        x_copy(n).start()

        coef = [nt(rounded[l], both_basis[l]) for l in range(LEAVES)]
        leaf_coef = jnp.concatenate(
            [
                jnp.where(half, coef[0], swap_halves(coef[1])),
                jnp.where(half, coef[2], swap_halves(coef[3])),
            ],
            axis=1,
        ).astype(BF16)
        parent_coef = jnp.where(
            half, swap_halves(coef[0] + coef[1]), coef[2] + coef[3]
        ).astype(BF16)

        def fill(values, w, first, count, place):
            for js in pairs_of(first, count):
                made = nn(values, side_by_side([w[j] for j in js]))
                for i, j in enumerate(js):
                    tile = swap_halves(made[:, i * 2 * RANK : (i + 1) * 2 * RANK]).astype(BF16)
                    if isinstance(j, int) and j == REACH:
                        recv[n, place(j)] = tile
                    else:
                        send[n, place(j)] = tile

        def send_group(g, carry):
            fill(parent_coef, parent_w, NEAR + g * group, group, far_tile)
            for i in order:
                far_copy(n, g, i).start()
            return carry

        lax.fori_loop(0, GROUPS, send_group, 0)
        fill(parent_coef, parent_w, 0, NEAR, close_tile)
        fill(leaf_coef, leaf_w, 0, NEAR, leaf_tile)
        for j in range(NEAR):
            if j != REACH:
                close_copy(n, j).start()

        for l in range(LEAVES):
            extended[l] = rounded[l].astype(F32)

        def add_backward(step, sofar):
            for i in range(STRIDE):
                e = step * STRIDE + i
                own = extended[near_first[e]]
                spread = jnp.concatenate(
                    [own * pick[e, LEAVES + s] for s in range(2 * LEAVES)], axis=0
                ).astype(BF16)
                sofar = sofar + nn(spread, near[e])
            return sofar

        backward = lax.fori_loop(
            0,
            CAPACITY // STRIDE,
            add_backward,
            jnp.zeros((2 * LEAVES * RHS, POINTS), F32),
        )
        near_out[n] = backward[LEAVES * RHS :].astype(BF16)
        near_copy(n).start()
        total = backward[: LEAVES * RHS] + jnp.concatenate(
            [nn(rounded[l], diag[l]) for l in range(LEAVES)], axis=0
        )

        x_copy(n).wait_recv()
        following = x_in[n].astype(F32)
        for l in range(LEAVES):
            extended[LEAVES + l] = following[l * RHS : (l + 1) * RHS]

        def add_forward(step, sofar):
            for i in range(STRIDE):
                e = step * STRIDE + i
                other = extended[near_second[e]]
                spread = jnp.concatenate(
                    [other * pick[e, t] for t in range(LEAVES)], axis=0
                ).astype(BF16)
                sofar = sofar + nt(spread, near[e])
            return sofar

        total = lax.fori_loop(0, CAPACITY // STRIDE, add_forward, total)

        def take(w, first, count, place, sofar):
            for js in pairs_of(first, count):
                got = side_by_side([recv[n, place(j)] for j in js])
                sofar = sofar + nt(got, side_by_side([w[j] for j in js]))
            return sofar

        def arrived(first, count, box):
            tiles = recv.at[n, pl.ds(first, count)]
            pltpu.make_async_copy(tiles, tiles, recv_sem.at[n, box]).wait()

        arrived(0, 2 * (NEAR - 1), 0)
        leaf_far = jnp.zeros((RHS, LEAVES * RANK), F32)
        leaf_far = take(leaf_w, 0, NEAR, leaf_tile, leaf_far)
        parent_far = jnp.zeros((RHS, 2 * RANK), F32)
        parent_far = take(parent_w, 0, NEAR, close_tile, parent_far)

        def take_group(g, sofar):
            first = devices - (g + 1) * group
            arrived(far_tile(first), group, 1 + g)
            return take(parent_w, first, group, far_tile, sofar)

        parent_far = lax.fori_loop(0, GROUPS, take_group, parent_far)

        near_copy(n).wait_recv()
        total = total + near_in[n].astype(F32)
        for l in range(LEAVES):
            pair = leaf_far[:, (l // 2) * 2 * RANK : (l // 2 + 1) * 2 * RANK]
            both = jnp.where(
                half,
                pair if l % 2 == 0 else swap_halves(pair),
                swap_halves(parent_far) if l < 2 else parent_far,
            ).astype(BF16)
            value = total[l * RHS : (l + 1) * RHS] + nn(both, both_basis[l])
            value = value * point_mask[l]
            vector[l] = value
            out[n, l] = value
        out_copy(n).start()
        return carry

    lax.fori_loop(0, PRODUCTS, product, 0)

    def finish(n, carry):
        sent = send.at[n, pl.ds(0, 2 * (NEAR - 1) + far_count)]
        pltpu.make_async_copy(sent, sent, send_sem.at[n]).wait()
        x_copy(n).wait_send()
        near_copy(n).wait_send()
        out_copy(n).wait()
        return carry

    lax.fori_loop(0, PRODUCTS, finish, 0)


def on_device(
    start_vector,
    leaf_size,
    diag_blocks,
    near_blocks,
    near_count,
    near_first,
    near_second,
    leaf_basis,
    transfer,
    coupling,
    send_slot,
    far_target,
):
    devices = lax.axis_size("clu")
    tiles = devices + NEAR
    smem = pl.BlockSpec(memory_space=pltpu.SMEM)
    hbm = pl.BlockSpec(memory_space=pltpu.HBM)
    sides = (PRODUCTS, LEAVES * RHS, POINTS)
    return pl.pallas_call(
        functools.partial(kernel, devices),
        out_shape=jax.ShapeDtypeStruct((PRODUCTS, LEAVES, RHS, POINTS), F32),
        in_specs=[
            hbm,
            smem,
            hbm,
            hbm,
            smem,
            smem,
            smem,
            hbm,
            hbm,
            hbm,
            smem,
            smem,
        ],
        out_specs=hbm,
        scratch_shapes=[
            pltpu.VMEM((LEAVES, RHS, POINTS), F32),
            pltpu.VMEM((LEAVES, RANK, POINTS), BF16),
            pltpu.VMEM((LEAVES, RANK, RANK), F32),
            pltpu.VMEM((RANK, RANK, 2 * devices), F32),
            pltpu.VMEM((2 * devices * HALF, 2 * RANK), F32),
            pltpu.VMEM((devices, 2 * RANK, 2 * RANK), BF16),
            pltpu.VMEM((NEAR, LEAVES * RANK, 2 * RANK), BF16),
            pltpu.VMEM((CAPACITY, POINTS, POINTS), BF16),
            pltpu.VMEM((LEAVES, POINTS, POINTS), BF16),
            pltpu.VMEM((LEAVES, 2 * RANK, POINTS), BF16),
            pltpu.SMEM((CAPACITY, 3 * LEAVES), F32),
            pltpu.VMEM((LEAVES, RHS, POINTS), F32),
            pltpu.VMEM((LEAVES, RHS, POINTS), F32),
            pltpu.VMEM((PRODUCTS, LEAVES, RHS, POINTS), F32),
            pltpu.VMEM((2 * LEAVES, RHS, POINTS), F32),
            pltpu.VMEM((PRODUCTS, tiles, RHS, 2 * RANK), BF16),
            pltpu.VMEM((PRODUCTS, tiles, RHS, 2 * RANK), BF16),
            pltpu.VMEM(sides, BF16),
            pltpu.VMEM(sides, BF16),
            pltpu.VMEM(sides, BF16),
            pltpu.VMEM(sides, BF16),
            pltpu.SemaphoreType.DMA((LOADS + 3, 2)),
            pltpu.SemaphoreType.DMA((PRODUCTS,)),
            pltpu.SemaphoreType.DMA((PRODUCTS,)),
            pltpu.SemaphoreType.DMA((PRODUCTS, 1 + GROUPS)),
            pltpu.SemaphoreType.DMA((PRODUCTS, 4)),
        ],
        compiler_params=pltpu.CompilerParams(
            collective_id=0, has_side_effects=True, vmem_limit_bytes=56 * 1024 * 1024
        ),
        name="h2_products",
    )(
        start_vector,
        leaf_size,
        diag_blocks,
        near_blocks,
        near_count,
        near_first,
        near_second,
        leaf_basis,
        transfer,
        coupling.transpose(1, 2, 0),
        send_slot,
        far_target,
    )


def solution(mesh):
    in_specs = (
        P("clu", None, None),
        P("clu"),
        P("clu", None, None),
        P("clu", None, None),
        P("clu"),
        P("clu"),
        P("clu"),
        P("clu", None, None),
        P("clu", None, None),
        P("clu", None, None),
        P("clu", None),
        P("clu", None),
    )
    out_specs = P(None, "clu", None, None)
    return jax.shard_map(
        on_device, mesh=mesh, in_specs=in_specs, out_specs=out_specs, check_vma=False
    )
```

```python
import functools

import jax
import jax.numpy as jnp
from jax import lax
from jax.experimental import pallas as pl
from jax.experimental.pallas import tpu as pltpu
from jax.sharding import PartitionSpec as P

PRODUCTS = 4
REACH = 8
CLOSE = 2 * REACH + 1
GROUPS = 4
STEP = 37
LOADS = 4
LEAVES = 4
PARENTS = LEAVES // 2
RANK = 64
HALF = RANK // 2
RHS = 8
POINTS = 256
CAPACITY = 16
STRIDE = 4
MESH = pl.DeviceIdType.MESH
F32 = jnp.float32
BF16 = jnp.bfloat16


def nn(a, b):
    return jnp.dot(a, b, preferred_element_type=F32)


def nt(a, b):
    return lax.dot_general(a, b, (((1,), (1,)), ((), ())), preferred_element_type=F32)


def swap_halves(a):
    return pltpu.roll(a, RANK, 1)


def side_by_side(parts):
    return parts[0] if len(parts) == 1 else jnp.concatenate(parts, axis=1)


def kernel(
    devices,
    start_hbm,
    leaf_size,
    diag_hbm,
    near_hbm,
    near_count,
    near_first,
    near_second,
    basis_hbm,
    transfer_hbm,
    coupling,
    send_slot,
    far_target,
    out_hbm,
    start,
    basis,
    transfer,
    raw,
    turned,
    parent_w,
    leaf_w,
    parent_slots,
    leaf_slots,
    near,
    diag,
    both_basis,
    pick,
    point_mask,
    vector,
    out,
    extended,
    send,
    recv,
    leaf_send,
    leaf_recv,
    x_out,
    x_in,
    near_out,
    near_in,
    load_sem,
    out_sem,
    send_sem,
    recv_sem,
    side_sem,
):
    me = lax.axis_index("clu")
    group = devices // GROUPS
    load_rows = HALF // LOADS
    pair_count = 2 * devices

    def wrap(index):
        if devices & (devices - 1):
            return lax.rem(index, devices)
        return index & (devices - 1)

    def partner(w):
        return wrap(me + STEP * (w + 1))

    def leaf_partner(v):
        return wrap(me + (v - REACH + devices))

    raw_loads = [
        [
            pltpu.make_async_copy(
                coupling.at[pl.ds(first, load_rows)],
                raw.at[pl.ds(first, load_rows)],
                load_sem.at[c, h],
            )
            for h, first in enumerate((c * load_rows, HALF + c * load_rows))
        ]
        for c in range(LOADS)
    ]
    near_load = pltpu.make_async_copy(near_hbm, near, load_sem.at[LOADS, 0])
    diag_load = pltpu.make_async_copy(diag_hbm, diag, load_sem.at[LOADS, 1])
    small_loads = [
        pltpu.make_async_copy(start_hbm, start, load_sem.at[LOADS + 1, 0]),
        pltpu.make_async_copy(basis_hbm, basis, load_sem.at[LOADS + 1, 1]),
        pltpu.make_async_copy(transfer_hbm, transfer, load_sem.at[LOADS + 2, 0]),
    ]
    for loads in raw_loads:
        for load in loads:
            load.start()
    for load in small_loads:
        load.start()
    near_load.start()
    diag_load.start()

    barrier = pltpu.get_barrier_semaphore()

    def greet(step, carry):
        pl.semaphore_signal(
            barrier, inc=1, device_id=(wrap(me + step),), device_id_type=MESH
        )
        return carry

    lax.fori_loop(1, devices, greet, 0)

    for load in small_loads:
        load.wait()

    point_ids = lax.broadcasted_iota(jnp.int32, (RHS, POINTS), 1)
    for l in range(LEAVES):
        inside = jnp.where(point_ids < leaf_size[l], 1.0, 0.0)
        point_mask[l] = inside
        vector[l] = start[l] * inside

    for l in range(LEAVES):
        moved = transfer[l].T
        high = moved.astype(BF16)
        low = (moved - high.astype(F32)).astype(BF16)
        own = basis[l]
        both_basis[l] = jnp.concatenate(
            [nn(high, own) + nn(low, own), own.astype(F32)], axis=0
        ).astype(BF16)

    def turn(k, carry):
        both = jnp.concatenate([raw[k], raw[k + HALF]], axis=0)
        turned[pl.ds(k, pair_count, stride=HALF), :] = both.T
        e = k // 2
        live = e < near_count[0]
        for i in range(6):
            column = 6 * (k % 2) + i
            leaf = jnp.where(column < LEAVES, near_first[e], near_second[e] + LEAVES)
            pick[e, column] = jnp.where(live & (leaf == column), 1.0, 0.0)
        return carry

    for c in range(LOADS):
        for load in raw_loads[c]:
            load.wait()
        lax.fori_loop(c * load_rows, (c + 1) * load_rows, turn, 0, unroll=4)

    left = lax.broadcasted_iota(jnp.int32, (RHS, 2 * RANK), 1) < RANK

    def on_left(rows):
        return jnp.concatenate([left] * (rows // RHS), axis=0)

    def build(w, slots, u, first, second):
        tiles = [
            turned[pl.ds(pl.multiple_of(column * HALF, HALF), HALF), :]
            for column in (first, second)
        ]
        swapped = [swap_halves(tile) for tile in tiles]
        w[u] = jnp.concatenate(
            [
                jnp.where(on_left(HALF), tiles[0], swapped[1]),
                jnp.where(on_left(HALF), swapped[0], tiles[1]),
            ],
            axis=0,
        ).astype(BF16)
        slots[u, 0] = jnp.where(left, far_target[0, first], far_target[0, second])
        slots[u, 1] = jnp.where(left, send_slot[0, first], send_slot[0, second])
        slots[u, 2] = jnp.where(left, send_slot[0, second], send_slot[0, first])

    def build_parent(u, carry):
        build(
            parent_w, parent_slots, u, 2 * partner(2 * u) + 1, 2 * partner(2 * u + 1) + 1
        )
        return carry

    def build_leaf(u, carry):
        build(leaf_w, leaf_slots, u, 2 * leaf_partner(2 * u), 2 * leaf_partner(2 * u + 1))
        return carry

    lax.fori_loop(0, devices // 2, build_parent, 0, unroll=8)
    lax.fori_loop(0, (CLOSE + 1) // 2, build_leaf, 0, unroll=3)
    for n in range(PRODUCTS):
        leaf_recv[n, CLOSE] = jnp.zeros((RHS, 2 * RANK), BF16)

    near_load.wait()
    diag_load.wait()
    pl.semaphore_wait(barrier, devices - 1)

    def remote(src, dst, out_sem, in_sem, target):
        return pltpu.make_async_remote_copy(
            src_ref=src,
            dst_ref=dst,
            send_sem=out_sem,
            recv_sem=in_sem,
            device_id=(target,),
            device_id_type=MESH,
        )

    def x_copy(n):
        return remote(
            x_out.at[n], x_in.at[n], side_sem.at[n, 0], side_sem.at[n, 1], leaf_partner(REACH - 1)
        )

    def near_copy(n):
        return remote(
            near_out.at[n], near_in.at[n], side_sem.at[n, 2], side_sem.at[n, 3], leaf_partner(REACH + 1)
        )

    def out_copy(n):
        return pltpu.make_async_copy(out.at[n], out_hbm.at[n], out_sem.at[n])

    def parent_copy(n, g, i):
        w = g * group + i
        return remote(
            send.at[n, pl.ds(w, 1)],
            recv.at[n, pl.ds(devices - 2 - w, 1)],
            send_sem.at[n, 0],
            recv_sem.at[n, g],
            partner(w),
        )

    def leaf_copy(n, v):
        return remote(
            leaf_send.at[n, pl.ds(v, 1)],
            leaf_recv.at[n, pl.ds(2 * REACH - v, 1)],
            send_sem.at[n, 1],
            recv_sem.at[n, GROUPS],
            leaf_partner(v),
        )

    def wait_for(tiles, sem):
        pltpu.make_async_copy(tiles, tiles, sem).wait()

    def chosen(slot, rows, first):
        count = rows.shape[0] // RHS
        result = rows[(count - 1) * RHS :]
        for t in reversed(range(count - 1)):
            result = jnp.where(slot == first + t, rows[t * RHS : (t + 1) * RHS], result)
        return result

    def kept(slot, value, first, count):
        return jnp.concatenate(
            [jnp.where(slot == first + t, value, 0.0) for t in range(count)], axis=0
        )

    def twos(first, count):
        return [[first + i for i in range(k, min(k + 2, count))] for k in range(0, count, 2)]

    def product(n, carry):
        exact = [vector[l] for l in range(LEAVES)]
        rounded = [value.astype(BF16) for value in exact]
        x_out[n] = jnp.concatenate(exact, axis=0).astype(BF16)
        x_copy(n).start()

        coef = [nt(rounded[l], both_basis[l]) for l in range(LEAVES)]
        parent = jnp.concatenate(
            [coef[2 * q] + coef[2 * q + 1] for q in range(PARENTS)], axis=0
        )
        leaf = jnp.concatenate(coef, axis=0)
        leaf_turned = swap_halves(leaf)
        parent_twice = jnp.where(on_left(PARENTS * RHS), parent, swap_halves(parent))
        leaf_twice = jnp.where(on_left(LEAVES * RHS), leaf_turned, leaf)
        parent_rows = parent[:, :RANK].astype(BF16)
        leaf_rows = leaf_turned[:, :RANK].astype(BF16)

        def fill(rows, twice, w, slots, first_slot, first, count, store):
            for us in twos(first, count):
                made = nn(rows, side_by_side([w[u] for u in us]))
                for i, u in enumerate(us):
                    block = made[:, i * 2 * RANK : (i + 1) * 2 * RANK]
                    outward = swap_halves(chosen(slots[u, 0], block, first_slot))
                    own = chosen(slots[u, 1], twice, first_slot)
                    store(2 * u, jnp.where(left, own, outward).astype(BF16))
                    store(2 * u + 1, jnp.where(left, outward, own).astype(BF16))

        def store_parent(w, tile):
            if isinstance(w, int) and w == devices - 1:
                recv[n, w] = tile
            else:
                send[n, w] = tile

        def store_leaf(v, tile):
            if v == REACH:
                leaf_recv[n, v] = tile
            elif v < CLOSE:
                leaf_send[n, v] = tile

        def send_group(g, count):
            fill(
                parent_rows,
                parent_twice,
                parent_w,
                parent_slots,
                LEAVES,
                g * (group // 2),
                group // 2,
                store_parent,
            )
            for i in range(count):
                parent_copy(n, g, i).start()

        def send_whole_group(g, carry):
            send_group(g, group)
            return carry

        lax.fori_loop(0, GROUPS - 1, send_whole_group, 0)
        send_group(GROUPS - 1, group - 1)
        fill(
            leaf_rows, leaf_twice, leaf_w, leaf_slots, 0, 0, (CLOSE + 1) // 2, store_leaf
        )
        for v in range(CLOSE):
            if v != REACH:
                leaf_copy(n, v).start()

        for l in range(LEAVES):
            extended[l] = rounded[l].astype(F32)

        def add_backward(step, sofar):
            for i in range(STRIDE):
                e = step * STRIDE + i
                own = extended[near_first[e]]
                spread = jnp.concatenate(
                    [own * pick[e, LEAVES + s] for s in range(2 * LEAVES)], axis=0
                ).astype(BF16)
                sofar = sofar + nn(spread, near[e])
            return sofar

        backward = lax.fori_loop(
            0,
            CAPACITY // STRIDE,
            add_backward,
            jnp.zeros((2 * LEAVES * RHS, POINTS), F32),
        )
        near_out[n] = backward[LEAVES * RHS :].astype(BF16)
        near_copy(n).start()
        total = backward[: LEAVES * RHS] + jnp.concatenate(
            [nn(rounded[l], diag[l]) for l in range(LEAVES)], axis=0
        )

        x_copy(n).wait_recv()
        following = x_in[n].astype(F32)
        for l in range(LEAVES):
            extended[LEAVES + l] = following[l * RHS : (l + 1) * RHS]

        def add_forward(step, sofar):
            for i in range(STRIDE):
                e = step * STRIDE + i
                other = extended[near_second[e]]
                spread = jnp.concatenate(
                    [other * pick[e, t] for t in range(LEAVES)], axis=0
                ).astype(BF16)
                sofar = sofar + nt(spread, near[e])
            return sofar

        total = lax.fori_loop(0, CAPACITY // STRIDE, add_forward, total)

        def take(box, w, slots, first_slot, slot_count, first, count, sofar):
            through, handed = sofar
            for us in twos(first, count):
                rows = []
                for u in us:
                    even, odd = box[n, 2 * u].astype(F32), box[n, 2 * u + 1].astype(F32)
                    incoming = jnp.where(left, even, odd)
                    outcome = jnp.where(left, odd, even)
                    rows.append(kept(slots[u, 0], incoming, first_slot, slot_count))
                    handed = handed + kept(slots[u, 2], outcome, first_slot, slot_count)
                through = through + nt(
                    side_by_side(rows).astype(BF16), side_by_side([w[u] for u in us])
                )
            return through, handed

        def nothing(count):
            return (
                jnp.zeros((count * RHS, RANK), F32),
                jnp.zeros((count * RHS, 2 * RANK), F32),
            )

        def take_group(g, sofar):
            first = (GROUPS - 1 - g) * (group // 2)
            return take(
                recv, parent_w, parent_slots, LEAVES, PARENTS, first, group // 2, sofar
            )

        def take_whole_group(g, sofar):
            arrived = recv.at[n, pl.ds(devices - 1 - (g + 1) * group, group)]
            wait_for(arrived, recv_sem.at[n, g])
            return take_group(g, sofar)

        parent_sum = lax.fori_loop(0, GROUPS - 1, take_whole_group, nothing(PARENTS))
        wait_for(recv.at[n, pl.ds(0, group - 1)], recv_sem.at[n, GROUPS - 1])
        parent_sum = take_group(GROUPS - 1, parent_sum)
        wait_for(leaf_recv.at[n, pl.ds(0, CLOSE - 1)], recv_sem.at[n, GROUPS])
        leaf_sum = take(
            leaf_recv,
            leaf_w,
            leaf_slots,
            0,
            LEAVES,
            0,
            (CLOSE + 1) // 2,
            nothing(LEAVES),
        )

        def whole(through, handed):
            return through + (handed + swap_halves(handed))[:, :RANK]

        parent_far = whole(*parent_sum)
        leaf_far = whole(*leaf_sum)

        near_copy(n).wait_recv()
        total = total + near_in[n].astype(F32)
        for l in range(LEAVES):
            q = l // 2
            both = jnp.concatenate(
                [parent_far[q * RHS : (q + 1) * RHS], leaf_far[l * RHS : (l + 1) * RHS]], axis=1
            ).astype(BF16)
            value = total[l * RHS : (l + 1) * RHS] + nn(both, both_basis[l])
            value = value * point_mask[l]
            vector[l] = value
            out[n, l] = value
        out_copy(n).start()
        return carry

    lax.fori_loop(0, PRODUCTS, product, 0)

    def finish(n, carry):
        wait_for(send.at[n, pl.ds(0, devices - 1)], send_sem.at[n, 0])
        wait_for(leaf_send.at[n, pl.ds(0, CLOSE - 1)], send_sem.at[n, 1])
        x_copy(n).wait_send()
        near_copy(n).wait_send()
        out_copy(n).wait()
        return carry

    lax.fori_loop(0, PRODUCTS, finish, 0)


def on_device(
    start_vector,
    leaf_size,
    diag_blocks,
    near_blocks,
    near_count,
    near_first,
    near_second,
    leaf_basis,
    transfer,
    coupling,
    send_slot,
    far_target,
):
    devices = lax.axis_size("clu")
    tile = (RHS, 2 * RANK)
    close_pairs = (CLOSE + 1) // 2
    smem = pl.BlockSpec(memory_space=pltpu.SMEM)
    hbm = pl.BlockSpec(memory_space=pltpu.HBM)
    sides = (PRODUCTS, LEAVES * RHS, POINTS)
    return pl.pallas_call(
        functools.partial(kernel, devices),
        out_shape=jax.ShapeDtypeStruct((PRODUCTS, LEAVES, RHS, POINTS), F32),
        in_specs=[
            hbm,
            smem,
            hbm,
            hbm,
            smem,
            smem,
            smem,
            hbm,
            hbm,
            hbm,
            smem,
            smem,
        ],
        out_specs=hbm,
        scratch_shapes=[
            pltpu.VMEM((LEAVES, RHS, POINTS), F32),
            pltpu.VMEM((LEAVES, RANK, POINTS), BF16),
            pltpu.VMEM((LEAVES, RANK, RANK), F32),
            pltpu.VMEM((RANK, RANK, 2 * devices), F32),
            pltpu.VMEM((2 * devices * HALF, 2 * RANK), F32),
            pltpu.VMEM((devices // 2, RANK, 2 * RANK), BF16),
            pltpu.VMEM((close_pairs, RANK, 2 * RANK), BF16),
            pltpu.VMEM((devices // 2, 3, *tile), jnp.int32),
            pltpu.VMEM((close_pairs, 3, *tile), jnp.int32),
            pltpu.VMEM((CAPACITY, POINTS, POINTS), BF16),
            pltpu.VMEM((LEAVES, POINTS, POINTS), BF16),
            pltpu.VMEM((LEAVES, 2 * RANK, POINTS), BF16),
            pltpu.SMEM((CAPACITY, 3 * LEAVES), F32),
            pltpu.VMEM((LEAVES, RHS, POINTS), F32),
            pltpu.VMEM((LEAVES, RHS, POINTS), F32),
            pltpu.VMEM((PRODUCTS, LEAVES, RHS, POINTS), F32),
            pltpu.VMEM((2 * LEAVES, RHS, POINTS), F32),
            pltpu.VMEM((PRODUCTS, devices, *tile), BF16),
            pltpu.VMEM((PRODUCTS, devices, *tile), BF16),
            pltpu.VMEM((PRODUCTS, CLOSE + 1, *tile), BF16),
            pltpu.VMEM((PRODUCTS, CLOSE + 1, *tile), BF16),
            pltpu.VMEM(sides, BF16),
            pltpu.VMEM(sides, BF16),
            pltpu.VMEM(sides, BF16),
            pltpu.VMEM(sides, BF16),
            pltpu.SemaphoreType.DMA((LOADS + 3, 2)),
            pltpu.SemaphoreType.DMA((PRODUCTS,)),
            pltpu.SemaphoreType.DMA((PRODUCTS, 2)),
            pltpu.SemaphoreType.DMA((PRODUCTS, GROUPS + 1)),
            pltpu.SemaphoreType.DMA((PRODUCTS, 4)),
        ],
        compiler_params=pltpu.CompilerParams(
            collective_id=0, has_side_effects=True, vmem_limit_bytes=56 * 1024 * 1024
        ),
        name="h2_products",
    )(
        start_vector,
        leaf_size,
        diag_blocks,
        near_blocks,
        near_count,
        near_first,
        near_second,
        leaf_basis,
        transfer,
        coupling.transpose(1, 2, 0),
        send_slot,
        far_target,
    )


def solution(mesh):
    in_specs = (
        P("clu", None, None),
        P("clu"),
        P("clu", None, None),
        P("clu", None, None),
        P("clu"),
        P("clu"),
        P("clu"),
        P("clu", None, None),
        P("clu", None, None),
        P("clu", None, None),
        P("clu", None),
        P("clu", None),
    )
    out_specs = P(None, "clu", None, None)
    return jax.shard_map(
        on_device, mesh=mesh, in_specs=in_specs, out_specs=out_specs, check_vma=False
    )
```

```python
import functools

import jax
import jax.numpy as jnp
from jax import lax
from jax.experimental import pallas as pl
from jax.experimental.pallas import tpu as pltpu
from jax.sharding import PartitionSpec as P

PRODUCTS = 4
REACH = 8
LEAF_ROWS = 32
CLOSE = 2 * REACH + 1
GROUPS = 4
GREETINGS = 7
LOADS = 4
LEAVES = 4
PARENTS = LEAVES // 2
RANK = 64
HALF = RANK // 2
RHS = 8
POINTS = 256
CAPACITY = 16
STRIDE = 4
MESH = pl.DeviceIdType.MESH
F32 = jnp.float32
BF16 = jnp.bfloat16


def nn(a, b):
    return jnp.dot(a, b, preferred_element_type=F32)


def nt(a, b):
    return lax.dot_general(a, b, (((1,), (1,)), ((), ())), preferred_element_type=F32)


def swap_halves(a):
    return pltpu.roll(a, RANK, 1)


def side_by_side(parts):
    return parts[0] if len(parts) == 1 else jnp.concatenate(parts, axis=1)


def kernel(
    devices,
    start_hbm,
    leaf_size,
    diag_hbm,
    near_hbm,
    near_count,
    near_first,
    near_second,
    basis_hbm,
    transfer_hbm,
    coupling,
    send_slot,
    far_target,
    out_hbm,
    start,
    basis,
    transfer,
    raw,
    turned,
    parent_w,
    leaf_w,
    parent_slots,
    leaf_slots,
    near,
    diag,
    both_basis,
    point_mask,
    vector,
    out,
    extended,
    send,
    recv,
    leaf_send,
    leaf_recv,
    x_out,
    x_in,
    near_out,
    near_in,
    load_sem,
    out_sem,
    send_sem,
    recv_sem,
    side_sem,
):
    me = lax.axis_index("clu")
    group = devices // GROUPS
    load_rows = HALF // LOADS
    pair_count = 2 * devices

    def wrap(index):
        if devices & (devices - 1):
            return lax.rem(index, devices)
        return index & (devices - 1)

    def flipped(index, w):
        return index + w - 2 * (index & w)

    def partner(w):
        return flipped(me, w)

    def leaf_partner(v):
        return wrap(me + (v - REACH + devices))

    raw_loads = [
        [
            pltpu.make_async_copy(
                coupling.at[pl.ds(first, load_rows)],
                raw.at[pl.ds(first, load_rows)],
                load_sem.at[c, h],
            )
            for h, first in enumerate((c * load_rows, HALF + c * load_rows))
        ]
        for c in range(LOADS)
    ]
    near_load = pltpu.make_async_copy(near_hbm, near, load_sem.at[LOADS, 0])
    diag_load = pltpu.make_async_copy(diag_hbm, diag, load_sem.at[LOADS, 1])
    small_loads = [
        pltpu.make_async_copy(start_hbm, start, load_sem.at[LOADS + 1, 0]),
        pltpu.make_async_copy(basis_hbm, basis, load_sem.at[LOADS + 1, 1]),
        pltpu.make_async_copy(transfer_hbm, transfer, load_sem.at[LOADS + 2, 0]),
    ]
    for loads in raw_loads:
        for load in loads:
            load.start()
    for load in small_loads:
        load.start()
    near_load.start()
    diag_load.start()

    barrier = pltpu.get_barrier_semaphore()

    def greet(w):
        pl.semaphore_signal(
            barrier, inc=1, device_id=(partner(w),), device_id_type=MESH
        )

    def greet_some(k, carry):
        for i in range(GREETINGS):
            greet(1 + k * GREETINGS + i)
        return carry

    lax.fori_loop(0, (devices - 1) // GREETINGS, greet_some, 0)
    for w in range(1 + (devices - 1) // GREETINGS * GREETINGS, devices):
        greet(w)

    for load in small_loads:
        load.wait()

    point_ids = lax.broadcasted_iota(jnp.int32, (RHS, POINTS), 1)
    for l in range(LEAVES):
        inside = jnp.where(point_ids < leaf_size[l], 1.0, 0.0)
        point_mask[l] = inside
        vector[l] = start[l] * inside

    for l in range(LEAVES):
        moved = transfer[l].T
        high = moved.astype(BF16)
        low = (moved - high.astype(F32)).astype(BF16)
        own = basis[l]
        both_basis[l] = jnp.concatenate(
            [nn(high, own) + nn(low, own), own.astype(F32)], axis=0
        ).astype(BF16)

    def one_hot(rows, wanted):
        row = lax.broadcasted_iota(jnp.int32, (rows, pair_count), 0)
        column = lax.broadcasted_iota(jnp.int32, (rows, pair_count), 1)
        return jnp.where(column == wanted(row), 1.0, 0.0)

    needed = jnp.concatenate(
        [
            one_hot(devices, lambda w: 2 * flipped(me, w) + 1),
            one_hot(LEAF_ROWS, lambda v: 2 * leaf_partner(v)),
        ],
        axis=0,
    ).astype(BF16)

    def turn(k, carry):
        both = jnp.concatenate([raw[k], raw[k + HALF]], axis=0).astype(BF16)
        turned[pl.ds(k, devices + LEAF_ROWS, stride=HALF), :] = nt(needed, both)
        return carry

    for c in range(LOADS):
        for load in raw_loads[c]:
            load.wait()
        lax.fori_loop(c * load_rows, (c + 1) * load_rows, turn, 0, unroll=4)

    left = lax.broadcasted_iota(jnp.int32, (RHS, 2 * RANK), 1) < RANK

    def on_left(rows):
        return jnp.concatenate([left] * (rows // RHS), axis=0)

    def build(w, slots, u, row, first, second):
        tiles = [
            turned[pl.ds(pl.multiple_of((row + i) * HALF, HALF), HALF), :] for i in range(2)
        ]
        swapped = [swap_halves(tile) for tile in tiles]
        w[u] = jnp.concatenate(
            [
                jnp.where(on_left(HALF), tiles[0], swapped[1]),
                jnp.where(on_left(HALF), swapped[0], tiles[1]),
            ],
            axis=0,
        ).astype(BF16)
        slots[u, 0] = jnp.where(left, far_target[0, first], far_target[0, second])
        slots[u, 1] = jnp.where(left, send_slot[0, first], send_slot[0, second])
        slots[u, 2] = jnp.where(left, send_slot[0, second], send_slot[0, first])

    def build_parent(u, carry):
        first, second = [2 * partner(2 * u + i) + 1 for i in range(2)]
        build(parent_w, parent_slots, u, 2 * u, first, second)
        return carry

    def build_leaf(u, carry):
        first, second = [2 * leaf_partner(2 * u + i) for i in range(2)]
        build(leaf_w, leaf_slots, u, devices + 2 * u, first, second)
        return carry

    lax.fori_loop(0, devices // 2, build_parent, 0, unroll=8)
    lax.fori_loop(0, (CLOSE + 1) // 2, build_leaf, 0, unroll=3)
    for n in range(PRODUCTS):
        leaf_recv[n, CLOSE] = jnp.zeros((RHS, 2 * RANK), BF16)

    near_load.wait()
    diag_load.wait()
    pl.semaphore_wait(barrier, devices - 1)

    def remote(src, dst, out_sem, in_sem, target):
        return pltpu.make_async_remote_copy(
            src_ref=src,
            dst_ref=dst,
            send_sem=out_sem,
            recv_sem=in_sem,
            device_id=(target,),
            device_id_type=MESH,
        )

    def x_copy(n):
        return remote(
            x_out.at[n], x_in.at[n], side_sem.at[n, 0], side_sem.at[n, 1], leaf_partner(REACH - 1)
        )

    def near_copy(n):
        return remote(
            near_out.at[n], near_in.at[n], side_sem.at[n, 2], side_sem.at[n, 3], leaf_partner(REACH + 1)
        )

    def out_copy(n):
        return pltpu.make_async_copy(out.at[n], out_hbm.at[n], out_sem.at[n])

    def parent_copy(n, w, g):
        return remote(
            send.at[n, pl.ds(w, 1)],
            recv.at[n, pl.ds(w, 1)],
            send_sem.at[n, 0],
            recv_sem.at[n, g],
            partner(w),
        )

    def leaf_copy(n, v):
        return remote(
            leaf_send.at[n, pl.ds(v, 1)],
            leaf_recv.at[n, pl.ds(2 * REACH - v, 1)],
            send_sem.at[n, 1],
            recv_sem.at[n, GROUPS],
            leaf_partner(v),
        )

    def wait_for(tiles, sem):
        pltpu.make_async_copy(tiles, tiles, sem).wait()

    def chosen(slot, rows, first):
        count = rows.shape[0] // RHS
        result = rows[(count - 1) * RHS :]
        for t in reversed(range(count - 1)):
            result = jnp.where(slot == first + t, rows[t * RHS : (t + 1) * RHS], result)
        return result

    def kept(slot, value, first, count):
        return jnp.concatenate(
            [jnp.where(slot == first + t, value, 0.0) for t in range(count)], axis=0
        )

    def twos(first, count):
        return [[first + i for i in range(k, min(k + 2, count))] for k in range(0, count, 2)]

    def hops(u):
        return sum((0, 1, 2, 1)[u >> shift & 3] for shift in (0, 2, 4))

    chips = devices // 2
    order = sorted(range(1, chips), key=lambda u: (-hops(u), u * 37 % chips)) + [0]
    chip_groups = [order[g * chips // GROUPS : (g + 1) * chips // GROUPS] for g in range(GROUPS)]

    def product(n, carry):
        exact = [vector[l] for l in range(LEAVES)]
        rounded = [value.astype(BF16) for value in exact]
        x_out[n] = jnp.concatenate(exact, axis=0).astype(BF16)
        x_copy(n).start()

        coef = [nt(rounded[l], both_basis[l]) for l in range(LEAVES)]
        parent = jnp.concatenate(
            [coef[2 * q] + coef[2 * q + 1] for q in range(PARENTS)], axis=0
        )
        leaf = jnp.concatenate(coef, axis=0)
        leaf_turned = swap_halves(leaf)
        parent_twice = jnp.where(on_left(PARENTS * RHS), parent, swap_halves(parent))
        leaf_twice = jnp.where(on_left(LEAVES * RHS), leaf_turned, leaf)
        parent_rows = parent[:, :RANK].astype(BF16)
        leaf_rows = leaf_turned[:, :RANK].astype(BF16)

        def fill(rows, twice, w, slots, first_slot, first, count, store):
            for us in twos(first, count):
                made = nn(rows, side_by_side([w[u] for u in us]))
                for i, u in enumerate(us):
                    block = made[:, i * 2 * RANK : (i + 1) * 2 * RANK]
                    outward = swap_halves(chosen(slots[u, 0], block, first_slot))
                    own = chosen(slots[u, 1], twice, first_slot)
                    store(2 * u, jnp.where(left, own, outward).astype(BF16))
                    store(2 * u + 1, jnp.where(left, outward, own).astype(BF16))

        def store_parent(w, tile):
            send[n, w] = tile

        def store_leaf(v, tile):
            if v == REACH:
                leaf_recv[n, v] = tile
            elif v < CLOSE:
                leaf_send[n, v] = tile

        def fill_group(g, carry):
            fill(
                parent_rows,
                parent_twice,
                parent_w,
                parent_slots,
                LEAVES,
                g * (group // 2),
                group // 2,
                store_parent,
            )
            return carry

        lax.fori_loop(0, GROUPS, fill_group, 0)
        for g in range(GROUPS):
            for u in chip_groups[g]:
                for w in (2 * u, 2 * u + 1):
                    if w:
                        parent_copy(n, w, g).start()
        fill(
            leaf_rows, leaf_twice, leaf_w, leaf_slots, 0, 0, (CLOSE + 1) // 2, store_leaf
        )
        for v in range(CLOSE):
            if v != REACH:
                leaf_copy(n, v).start()

        for l in range(LEAVES):
            extended[l] = rounded[l].astype(F32)

        def live_slot(slots, e):
            slot = jnp.where(e < near_count[0], slots[e], -1)
            return jnp.full((RHS, POINTS), slot, jnp.int32)

        def add_backward(step, sofar):
            for i in range(STRIDE):
                e = step * STRIDE + i
                own = extended[near_first[e]]
                slot = live_slot(near_second, e)
                spread = jnp.concatenate(
                    [jnp.where(slot == s, own, 0.0) for s in range(2 * LEAVES)], axis=0
                ).astype(BF16)
                sofar = sofar + nn(spread, near[e])
            return sofar

        backward = lax.fori_loop(
            0,
            CAPACITY // STRIDE,
            add_backward,
            jnp.zeros((2 * LEAVES * RHS, POINTS), F32),
        )
        near_out[n] = backward[LEAVES * RHS :].astype(BF16)
        near_copy(n).start()
        total = backward[: LEAVES * RHS] + jnp.concatenate(
            [nn(rounded[l], diag[l]) for l in range(LEAVES)], axis=0
        )

        x_copy(n).wait_recv()
        following = x_in[n].astype(F32)
        for l in range(LEAVES):
            extended[LEAVES + l] = following[l * RHS : (l + 1) * RHS]

        def add_forward(step, sofar):
            for i in range(STRIDE):
                e = step * STRIDE + i
                other = extended[near_second[e]]
                slot = live_slot(near_first, e)
                spread = jnp.concatenate(
                    [jnp.where(slot == t, other, 0.0) for t in range(LEAVES)], axis=0
                ).astype(BF16)
                sofar = sofar + nt(spread, near[e])
            return sofar

        total = lax.fori_loop(0, CAPACITY // STRIDE, add_forward, total)

        def take(box, w, slots, first_slot, slot_count, pairs, sofar):
            through, handed = sofar
            for k in range(0, len(pairs), 2):
                us, rows = pairs[k : k + 2], []
                for u in us:
                    outer = send if u == 0 and box is recv else box
                    even = outer[n, 2 * u].astype(F32)
                    odd = box[n, 2 * u + 1].astype(F32)
                    incoming = jnp.where(left, even, odd)
                    outcome = jnp.where(left, odd, even)
                    rows.append(kept(slots[u, 0], incoming, first_slot, slot_count))
                    handed = handed + kept(slots[u, 2], outcome, first_slot, slot_count)
                through = through + nt(
                    side_by_side(rows).astype(BF16), side_by_side([w[u] for u in us])
                )
            return through, handed

        def nothing(count):
            return (
                jnp.zeros((count * RHS, RANK), F32),
                jnp.zeros((count * RHS, 2 * RANK), F32),
            )

        parent_sum = nothing(PARENTS)
        for g in range(GROUPS):
            messages = group if g < GROUPS - 1 else group - 1
            wait_for(recv.at[n, pl.ds(1, messages)], recv_sem.at[n, g])
            parent_sum = take(
                recv, parent_w, parent_slots, LEAVES, PARENTS, chip_groups[g], parent_sum
            )
        wait_for(leaf_recv.at[n, pl.ds(0, CLOSE - 1)], recv_sem.at[n, GROUPS])
        leaf_sum = take(
            leaf_recv,
            leaf_w,
            leaf_slots,
            0,
            LEAVES,
            list(range((CLOSE + 1) // 2)),
            nothing(LEAVES),
        )

        def whole(through, handed):
            return through + (handed + swap_halves(handed))[:, :RANK]

        parent_far = whole(*parent_sum)
        leaf_far = whole(*leaf_sum)

        near_copy(n).wait_recv()
        total = total + near_in[n].astype(F32)
        for l in range(LEAVES):
            q = l // 2
            both = jnp.concatenate(
                [parent_far[q * RHS : (q + 1) * RHS], leaf_far[l * RHS : (l + 1) * RHS]], axis=1
            ).astype(BF16)
            value = total[l * RHS : (l + 1) * RHS] + nn(both, both_basis[l])
            value = value * point_mask[l]
            vector[l] = value
            out[n, l] = value
        out_copy(n).start()
        return carry

    lax.fori_loop(0, PRODUCTS, product, 0)

    def finish(n, carry):
        wait_for(send.at[n, pl.ds(1, devices - 1)], send_sem.at[n, 0])
        wait_for(leaf_send.at[n, pl.ds(0, CLOSE - 1)], send_sem.at[n, 1])
        x_copy(n).wait_send()
        near_copy(n).wait_send()
        out_copy(n).wait()
        return carry

    lax.fori_loop(0, PRODUCTS, finish, 0)


def on_device(
    start_vector,
    leaf_size,
    diag_blocks,
    near_blocks,
    near_count,
    near_first,
    near_second,
    leaf_basis,
    transfer,
    coupling,
    send_slot,
    far_target,
):
    devices = lax.axis_size("clu")
    tile = (RHS, 2 * RANK)
    close_pairs = (CLOSE + 1) // 2
    smem = pl.BlockSpec(memory_space=pltpu.SMEM)
    hbm = pl.BlockSpec(memory_space=pltpu.HBM)
    sides = (PRODUCTS, LEAVES * RHS, POINTS)
    return pl.pallas_call(
        functools.partial(kernel, devices),
        out_shape=jax.ShapeDtypeStruct((PRODUCTS, LEAVES, RHS, POINTS), F32),
        in_specs=[
            hbm,
            smem,
            hbm,
            hbm,
            smem,
            smem,
            smem,
            hbm,
            hbm,
            hbm,
            smem,
            smem,
        ],
        out_specs=hbm,
        scratch_shapes=[
            pltpu.VMEM((LEAVES, RHS, POINTS), F32),
            pltpu.VMEM((LEAVES, RANK, POINTS), BF16),
            pltpu.VMEM((LEAVES, RANK, RANK), F32),
            pltpu.VMEM((RANK, RANK, 2 * devices), F32),
            pltpu.VMEM(((devices + LEAF_ROWS) * HALF, 2 * RANK), F32),
            pltpu.VMEM((devices // 2, RANK, 2 * RANK), BF16),
            pltpu.VMEM((close_pairs, RANK, 2 * RANK), BF16),
            pltpu.VMEM((devices // 2, 3, *tile), jnp.int32),
            pltpu.VMEM((close_pairs, 3, *tile), jnp.int32),
            pltpu.VMEM((CAPACITY, POINTS, POINTS), BF16),
            pltpu.VMEM((LEAVES, POINTS, POINTS), BF16),
            pltpu.VMEM((LEAVES, 2 * RANK, POINTS), BF16),
            pltpu.VMEM((LEAVES, RHS, POINTS), F32),
            pltpu.VMEM((LEAVES, RHS, POINTS), F32),
            pltpu.VMEM((PRODUCTS, LEAVES, RHS, POINTS), F32),
            pltpu.VMEM((2 * LEAVES, RHS, POINTS), F32),
            pltpu.VMEM((PRODUCTS, devices, *tile), BF16),
            pltpu.VMEM((PRODUCTS, devices, *tile), BF16),
            pltpu.VMEM((PRODUCTS, CLOSE + 1, *tile), BF16),
            pltpu.VMEM((PRODUCTS, CLOSE + 1, *tile), BF16),
            pltpu.VMEM(sides, BF16),
            pltpu.VMEM(sides, BF16),
            pltpu.VMEM(sides, BF16),
            pltpu.VMEM(sides, BF16),
            pltpu.SemaphoreType.DMA((LOADS + 3, 2)),
            pltpu.SemaphoreType.DMA((PRODUCTS,)),
            pltpu.SemaphoreType.DMA((PRODUCTS, 2)),
            pltpu.SemaphoreType.DMA((PRODUCTS, GROUPS + 1)),
            pltpu.SemaphoreType.DMA((PRODUCTS, 4)),
        ],
        compiler_params=pltpu.CompilerParams(
            collective_id=0, has_side_effects=True, vmem_limit_bytes=56 * 1024 * 1024
        ),
        name="h2_products",
    )(
        start_vector,
        leaf_size,
        diag_blocks,
        near_blocks,
        near_count,
        near_first,
        near_second,
        leaf_basis,
        transfer,
        coupling.transpose(1, 2, 0),
        send_slot,
        far_target,
    )


def solution(mesh):
    in_specs = (
        P("clu", None, None),
        P("clu"),
        P("clu", None, None),
        P("clu", None, None),
        P("clu"),
        P("clu"),
        P("clu"),
        P("clu", None, None),
        P("clu", None, None),
        P("clu", None, None),
        P("clu", None),
        P("clu", None),
    )
    out_specs = P(None, "clu", None, None)
    return jax.shard_map(
        on_device, mesh=mesh, in_specs=in_specs, out_specs=out_specs, check_vma=False
    )
```

```python
import functools

import jax
import jax.numpy as jnp
from jax import lax
from jax.experimental import pallas as pl
from jax.experimental.pallas import tpu as pltpu
from jax.sharding import PartitionSpec as P

PRODUCTS = 4
REACH = 8
LEAF_ROWS = 32
CLOSE = 2 * REACH + 1
GROUPS = 4
GREETINGS = 7
LOADS = 4
LEAVES = 4
PARENTS = LEAVES // 2
RANK = 64
HALF = RANK // 2
RHS = 8
POINTS = 256
CAPACITY = 16
STRIDE = 8
MESH = pl.DeviceIdType.MESH
F32 = jnp.float32
BF16 = jnp.bfloat16


def nn(a, b):
    return jnp.dot(a, b, preferred_element_type=F32)


def nt(a, b):
    return lax.dot_general(a, b, (((1,), (1,)), ((), ())), preferred_element_type=F32)


def swap_halves(a):
    return pltpu.roll(a, RANK, 1)


def side_by_side(parts):
    return parts[0] if len(parts) == 1 else jnp.concatenate(parts, axis=1)


def kernel(
    devices,
    start_hbm,
    leaf_size,
    diag_hbm,
    near_hbm,
    near_count,
    near_first,
    near_second,
    basis_hbm,
    transfer_hbm,
    coupling,
    send_slot,
    far_target,
    out_hbm,
    start,
    basis,
    transfer,
    raw,
    turned,
    parent_w,
    leaf_w,
    parent_slots,
    leaf_slots,
    near,
    diag,
    both_basis,
    gram,
    coefs,
    last_far,
    point_mask,
    vector,
    out,
    extended,
    send,
    recv,
    leaf_send,
    leaf_recv,
    x_out,
    x_in,
    near_out,
    near_in,
    load_sem,
    out_sem,
    send_sem,
    recv_sem,
    side_sem,
):
    me = lax.axis_index("clu")
    group = devices // GROUPS
    load_rows = HALF // LOADS
    pair_count = 2 * devices

    def wrap(index):
        if devices & (devices - 1):
            return lax.rem(index, devices)
        return index & (devices - 1)

    def flipped(index, w):
        return index + w - 2 * (index & w)

    def partner(w):
        return flipped(me, w)

    def leaf_partner(v):
        return wrap(me + (v - REACH + devices))

    raw_loads = [
        [
            pltpu.make_async_copy(
                coupling.at[pl.ds(first, load_rows)],
                raw.at[pl.ds(first, load_rows)],
                load_sem.at[c, h],
            )
            for h, first in enumerate((c * load_rows, HALF + c * load_rows))
        ]
        for c in range(LOADS)
    ]
    near_load = pltpu.make_async_copy(near_hbm, near, load_sem.at[LOADS, 0])
    diag_load = pltpu.make_async_copy(diag_hbm, diag, load_sem.at[LOADS, 1])
    small_loads = [
        pltpu.make_async_copy(start_hbm, start, load_sem.at[LOADS + 1, 0]),
        pltpu.make_async_copy(basis_hbm, basis, load_sem.at[LOADS + 1, 1]),
        pltpu.make_async_copy(transfer_hbm, transfer, load_sem.at[LOADS + 2, 0]),
    ]
    for loads in raw_loads:
        for load in loads:
            load.start()
    for load in small_loads:
        load.start()
    near_load.start()
    diag_load.start()

    barrier = pltpu.get_barrier_semaphore()

    def greet(w):
        pl.semaphore_signal(
            barrier, inc=1, device_id=(partner(w),), device_id_type=MESH
        )

    def greet_some(k, carry):
        for i in range(GREETINGS):
            greet(1 + k * GREETINGS + i)
        return carry

    lax.fori_loop(0, (devices - 1) // GREETINGS, greet_some, 0)
    for w in range(1 + (devices - 1) // GREETINGS * GREETINGS, devices):
        greet(w)

    for load in small_loads:
        load.wait()

    point_ids = lax.broadcasted_iota(jnp.int32, (RHS, POINTS), 1)
    for l in range(LEAVES):
        inside = jnp.where(point_ids < leaf_size[l], 1.0, 0.0)
        point_mask[l] = inside
        vector[l] = start[l] * inside

    for l in range(LEAVES):
        moved = transfer[l].T
        high = moved.astype(BF16)
        low = (moved - high.astype(F32)).astype(BF16)
        own = basis[l]
        both_basis[l] = jnp.concatenate(
            [nn(high, own) + nn(low, own), own.astype(F32)], axis=0
        ).astype(BF16)
        masked = both_basis[l].astype(F32) * point_mask[l][:1]
        gram[l] = nt(masked.astype(BF16), both_basis[l]).astype(BF16)
        coefs[l] = nt(vector[l].astype(BF16), both_basis[l])
        last_far[l] = jnp.zeros((RHS, 2 * RANK), F32)

    def one_hot(rows, wanted):
        row = lax.broadcasted_iota(jnp.int32, (rows, pair_count), 0)
        column = lax.broadcasted_iota(jnp.int32, (rows, pair_count), 1)
        return jnp.where(column == wanted(row), 1.0, 0.0)

    needed = jnp.concatenate(
        [
            one_hot(devices, lambda w: 2 * flipped(me, w) + 1),
            one_hot(LEAF_ROWS, lambda v: 2 * leaf_partner(v)),
        ],
        axis=0,
    ).astype(BF16)

    def turn(k, carry):
        both = jnp.concatenate([raw[k], raw[k + HALF]], axis=0).astype(BF16)
        turned[pl.ds(k, devices + LEAF_ROWS, stride=HALF), :] = nt(needed, both)
        return carry

    for c in range(LOADS):
        for load in raw_loads[c]:
            load.wait()
        lax.fori_loop(c * load_rows, (c + 1) * load_rows, turn, 0, unroll=4)

    left = lax.broadcasted_iota(jnp.int32, (RHS, 2 * RANK), 1) < RANK

    def on_left(rows):
        return jnp.concatenate([left] * (rows // RHS), axis=0)

    def build(w, slots, u, row, first, second):
        tiles = [
            turned[pl.ds(pl.multiple_of((row + i) * HALF, HALF), HALF), :] for i in range(2)
        ]
        swapped = [swap_halves(tile) for tile in tiles]
        w[u] = jnp.concatenate(
            [
                jnp.where(on_left(HALF), tiles[0], swapped[1]),
                jnp.where(on_left(HALF), swapped[0], tiles[1]),
            ],
            axis=0,
        ).astype(BF16)
        slots[u, 0] = jnp.where(left, far_target[0, first], far_target[0, second])
        slots[u, 1] = jnp.where(left, send_slot[0, first], send_slot[0, second])
        slots[u, 2] = jnp.where(left, send_slot[0, second], send_slot[0, first])

    def build_parent(u, carry):
        first, second = [2 * partner(2 * u + i) + 1 for i in range(2)]
        build(parent_w, parent_slots, u, 2 * u, first, second)
        return carry

    def build_leaf(u, carry):
        first, second = [2 * leaf_partner(2 * u + i) for i in range(2)]
        build(leaf_w, leaf_slots, u, devices + 2 * u, first, second)
        return carry

    lax.fori_loop(0, devices // 2, build_parent, 0, unroll=8)
    lax.fori_loop(0, (CLOSE + 1) // 2, build_leaf, 0, unroll=3)
    for n in range(PRODUCTS):
        leaf_recv[n, CLOSE] = jnp.zeros((RHS, 2 * RANK), BF16)

    near_load.wait()
    diag_load.wait()
    pl.semaphore_wait(barrier, devices - 1)

    def remote(src, dst, out_sem, in_sem, target):
        return pltpu.make_async_remote_copy(
            src_ref=src,
            dst_ref=dst,
            send_sem=out_sem,
            recv_sem=in_sem,
            device_id=(target,),
            device_id_type=MESH,
        )

    def x_copy(n):
        return remote(
            x_out.at[n], x_in.at[n], side_sem.at[n, 0], side_sem.at[n, 1], leaf_partner(REACH - 1)
        )

    def near_copy(n):
        return remote(
            near_out.at[n], near_in.at[n], side_sem.at[n, 2], side_sem.at[n, 3], leaf_partner(REACH + 1)
        )

    def out_copy(n):
        return pltpu.make_async_copy(out.at[n + 1], out_hbm.at[n], out_sem.at[n])

    def parent_copy(n, w, g):
        return remote(
            send.at[n, pl.ds(w, 1)],
            recv.at[n, pl.ds(w, 1)],
            send_sem.at[n, 0],
            recv_sem.at[n, g],
            partner(w),
        )

    def leaf_copy(n, v):
        return remote(
            leaf_send.at[n, pl.ds(v, 1)],
            leaf_recv.at[n, pl.ds(2 * REACH - v, 1)],
            send_sem.at[n, 1],
            recv_sem.at[n, GROUPS],
            leaf_partner(v),
        )

    def wait_for(tiles, sem):
        pltpu.make_async_copy(tiles, tiles, sem).wait()

    def chosen(slot, rows, first):
        count = rows.shape[0] // RHS
        result = rows[(count - 1) * RHS :]
        for t in reversed(range(count - 1)):
            result = jnp.where(slot == first + t, rows[t * RHS : (t + 1) * RHS], result)
        return result

    def kept(slot, value, first, count):
        return jnp.concatenate(
            [jnp.where(slot == first + t, value, 0.0) for t in range(count)], axis=0
        )

    def hops(u):
        return sum((0, 1, 2, 1)[u >> shift & 3] for shift in (0, 2, 4))

    chips = devices // 2
    order = sorted(range(1, chips), key=lambda u: (-hops(u), u * 37 % chips)) + [0]
    leaf_pairs = list(range((CLOSE + 1) // 2))
    cuts = [0, chips // 8, 3 * chips // 8, 11 * chips // 16, chips]
    chip_groups = [order[cuts[g] : cuts[g + 1]] for g in range(GROUPS)]

    def finish_vector(n):
        values = []
        for l in range(LEAVES):
            value = vector[l] + nn(last_far[l].astype(BF16), both_basis[l])
            value = value * point_mask[l]
            out[n, l] = value
            values.append(value)
        return values

    def product(n, carry):
        coef = [coefs[l] for l in range(LEAVES)]

        parent = jnp.concatenate(
            [coef[2 * q] + coef[2 * q + 1] for q in range(PARENTS)], axis=0
        )
        leaf = jnp.concatenate(coef, axis=0)
        leaf_turned = swap_halves(leaf)
        parent_twice = jnp.where(on_left(PARENTS * RHS), parent, swap_halves(parent))
        leaf_twice = jnp.where(on_left(LEAVES * RHS), leaf_turned, leaf)
        parent_rows = parent[:, :RANK].astype(BF16)
        leaf_rows = leaf_turned[:, :RANK].astype(BF16)

        def fill(rows, twice, w, slots, first_slot, pairs, store):
            for k in range(0, len(pairs), 2):
                us = pairs[k : k + 2]
                made = nn(rows, side_by_side([w[u] for u in us]))
                for i, u in enumerate(us):
                    block = made[:, i * 2 * RANK : (i + 1) * 2 * RANK]
                    outward = swap_halves(chosen(slots[u, 0], block, first_slot))
                    own = chosen(slots[u, 1], twice, first_slot)
                    store(2 * u, jnp.where(left, own, outward).astype(BF16))
                    store(2 * u + 1, jnp.where(left, outward, own).astype(BF16))

        def store_parent(w, tile):
            send[n, w] = tile

        def store_leaf(v, tile):
            if v == REACH:
                leaf_recv[n, v] = tile
            elif v < CLOSE:
                leaf_send[n, v] = tile

        for g in range(GROUPS):
            fill(
                parent_rows,
                parent_twice,
                parent_w,
                parent_slots,
                LEAVES,
                chip_groups[g],
                store_parent,
            )
            for u in chip_groups[g]:
                for w in (2 * u, 2 * u + 1):
                    if w:
                        parent_copy(n, w, g).start()
        fill(
            leaf_rows, leaf_twice, leaf_w, leaf_slots, 0, leaf_pairs, store_leaf
        )
        for v in range(CLOSE):
            if v != REACH:
                leaf_copy(n, v).start()

        exact = finish_vector(n)
        rounded = [value.astype(BF16) for value in exact]
        x_out[n] = jnp.concatenate(exact, axis=0).astype(BF16)
        x_copy(n).start()

        @pl.when(n > 0)
        def _():
            out_copy(n - 1).start()

        for l in range(LEAVES):
            extended[l] = rounded[l].astype(F32)

        def live_slot(slots, e):
            slot = jnp.where(e < near_count[0], slots[e], -1)
            return jnp.full((RHS, POINTS), slot, jnp.int32)

        def add_backward(step, sofar):
            for i in range(STRIDE):
                e = step * STRIDE + i
                own = extended[near_first[e]]
                slot = live_slot(near_second, e)
                spread = jnp.concatenate(
                    [jnp.where(slot == s, own, 0.0) for s in range(2 * LEAVES)], axis=0
                ).astype(BF16)
                sofar = sofar + nn(spread, near[e])
            return sofar

        backward = lax.fori_loop(
            0,
            CAPACITY // STRIDE,
            add_backward,
            jnp.zeros((2 * LEAVES * RHS, POINTS), F32),
        )
        near_out[n] = backward[LEAVES * RHS :].astype(BF16)
        near_copy(n).start()
        total = backward[: LEAVES * RHS] + jnp.concatenate(
            [nn(rounded[l], diag[l]) for l in range(LEAVES)], axis=0
        )

        x_copy(n).wait_recv()
        following = x_in[n].astype(F32)
        for l in range(LEAVES):
            extended[LEAVES + l] = following[l * RHS : (l + 1) * RHS]

        def add_forward(step, sofar):
            for i in range(STRIDE):
                e = step * STRIDE + i
                other = extended[near_second[e]]
                slot = live_slot(near_first, e)
                spread = jnp.concatenate(
                    [jnp.where(slot == t, other, 0.0) for t in range(LEAVES)], axis=0
                ).astype(BF16)
                sofar = sofar + nt(spread, near[e])
            return sofar

        total = lax.fori_loop(0, CAPACITY // STRIDE, add_forward, total)

        def take(box, w, slots, first_slot, slot_count, pairs, sofar):
            through, handed = sofar
            for k in range(0, len(pairs), 2):
                us, rows = pairs[k : k + 2], []
                for u in us:
                    outer = send if u == 0 and box is recv else box
                    even = outer[n, 2 * u].astype(F32)
                    odd = box[n, 2 * u + 1].astype(F32)
                    incoming = jnp.where(left, even, odd)
                    outcome = jnp.where(left, odd, even)
                    rows.append(kept(slots[u, 0], incoming, first_slot, slot_count))
                    handed = handed + kept(slots[u, 2], outcome, first_slot, slot_count)
                through = through + nt(
                    side_by_side(rows).astype(BF16), side_by_side([w[u] for u in us])
                )
            return through, handed

        def nothing(count):
            return (
                jnp.zeros((count * RHS, RANK), F32),
                jnp.zeros((count * RHS, 2 * RANK), F32),
            )

        near_copy(n).wait_recv()
        total = total + near_in[n].astype(F32)
        near_coef = []
        for l in range(LEAVES):
            value = total[l * RHS : (l + 1) * RHS] * point_mask[l]
            vector[l] = value
            near_coef.append(nt(value.astype(BF16), both_basis[l]))

        parent_sum = nothing(PARENTS)
        for g in range(GROUPS):
            messages = 2 * len(chip_groups[g]) - (1 if g == GROUPS - 1 else 0)
            wait_for(recv.at[n, pl.ds(1, messages)], recv_sem.at[n, g])
            if g == GROUPS - 1:
                wait_for(leaf_recv.at[n, pl.ds(0, CLOSE - 1)], recv_sem.at[n, GROUPS])
            parent_sum = take(
                recv, parent_w, parent_slots, LEAVES, PARENTS, chip_groups[g], parent_sum
            )
        leaf_sum = take(
            leaf_recv, leaf_w, leaf_slots, 0, LEAVES, leaf_pairs, nothing(LEAVES)
        )

        def whole(through, handed):
            return through + (handed + swap_halves(handed))[:, :RANK]

        parent_far = whole(*parent_sum)
        leaf_far = whole(*leaf_sum)

        for l in range(LEAVES):
            q = l // 2
            both = jnp.concatenate(
                [parent_far[q * RHS : (q + 1) * RHS], leaf_far[l * RHS : (l + 1) * RHS]], axis=1
            )
            last_far[l] = both
            coefs[l] = near_coef[l] + nn(both.astype(BF16), gram[l])
        return carry

    lax.fori_loop(0, PRODUCTS, product, 0)
    finish_vector(PRODUCTS)
    out_copy(PRODUCTS - 1).start()

    def finish(n, carry):
        wait_for(send.at[n, pl.ds(1, devices - 1)], send_sem.at[n, 0])
        wait_for(leaf_send.at[n, pl.ds(0, CLOSE - 1)], send_sem.at[n, 1])
        x_copy(n).wait_send()
        near_copy(n).wait_send()
        out_copy(n).wait()
        return carry

    lax.fori_loop(0, PRODUCTS, finish, 0)


def on_device(
    start_vector,
    leaf_size,
    diag_blocks,
    near_blocks,
    near_count,
    near_first,
    near_second,
    leaf_basis,
    transfer,
    coupling,
    send_slot,
    far_target,
):
    devices = lax.axis_size("clu")
    tile = (RHS, 2 * RANK)
    close_pairs = (CLOSE + 1) // 2
    smem = pl.BlockSpec(memory_space=pltpu.SMEM)
    hbm = pl.BlockSpec(memory_space=pltpu.HBM)
    sides = (PRODUCTS, LEAVES * RHS, POINTS)
    return pl.pallas_call(
        functools.partial(kernel, devices),
        out_shape=jax.ShapeDtypeStruct((PRODUCTS, LEAVES, RHS, POINTS), F32),
        in_specs=[
            hbm,
            smem,
            hbm,
            hbm,
            smem,
            smem,
            smem,
            hbm,
            hbm,
            hbm,
            smem,
            smem,
        ],
        out_specs=hbm,
        scratch_shapes=[
            pltpu.VMEM((LEAVES, RHS, POINTS), F32),
            pltpu.VMEM((LEAVES, RANK, POINTS), BF16),
            pltpu.VMEM((LEAVES, RANK, RANK), F32),
            pltpu.VMEM((RANK, RANK, 2 * devices), F32),
            pltpu.VMEM(((devices + LEAF_ROWS) * HALF, 2 * RANK), F32),
            pltpu.VMEM((devices // 2, RANK, 2 * RANK), BF16),
            pltpu.VMEM((close_pairs, RANK, 2 * RANK), BF16),
            pltpu.VMEM((devices // 2, 3, *tile), jnp.int32),
            pltpu.VMEM((close_pairs, 3, *tile), jnp.int32),
            pltpu.VMEM((CAPACITY, POINTS, POINTS), BF16),
            pltpu.VMEM((LEAVES, POINTS, POINTS), BF16),
            pltpu.VMEM((LEAVES, 2 * RANK, POINTS), BF16),
            pltpu.VMEM((LEAVES, 2 * RANK, 2 * RANK), BF16),
            pltpu.VMEM((LEAVES, *tile), F32),
            pltpu.VMEM((LEAVES, *tile), F32),
            pltpu.VMEM((LEAVES, RHS, POINTS), F32),
            pltpu.VMEM((LEAVES, RHS, POINTS), F32),
            pltpu.VMEM((PRODUCTS + 1, LEAVES, RHS, POINTS), F32),
            pltpu.VMEM((2 * LEAVES, RHS, POINTS), F32),
            pltpu.VMEM((PRODUCTS, devices, *tile), BF16),
            pltpu.VMEM((PRODUCTS, devices, *tile), BF16),
            pltpu.VMEM((PRODUCTS, CLOSE + 1, *tile), BF16),
            pltpu.VMEM((PRODUCTS, CLOSE + 1, *tile), BF16),
            pltpu.VMEM(sides, BF16),
            pltpu.VMEM(sides, BF16),
            pltpu.VMEM(sides, BF16),
            pltpu.VMEM(sides, BF16),
            pltpu.SemaphoreType.DMA((LOADS + 3, 2)),
            pltpu.SemaphoreType.DMA((PRODUCTS,)),
            pltpu.SemaphoreType.DMA((PRODUCTS, 2)),
            pltpu.SemaphoreType.DMA((PRODUCTS, GROUPS + 1)),
            pltpu.SemaphoreType.DMA((PRODUCTS, 4)),
        ],
        compiler_params=pltpu.CompilerParams(
            collective_id=0, has_side_effects=True, vmem_limit_bytes=56 * 1024 * 1024
        ),
        name="h2_products",
    )(
        start_vector,
        leaf_size,
        diag_blocks,
        near_blocks,
        near_count,
        near_first,
        near_second,
        leaf_basis,
        transfer,
        coupling.transpose(1, 2, 0),
        send_slot,
        far_target,
    )


def solution(mesh):
    in_specs = (
        P("clu", None, None),
        P("clu"),
        P("clu", None, None),
        P("clu", None, None),
        P("clu"),
        P("clu"),
        P("clu"),
        P("clu", None, None),
        P("clu", None, None),
        P("clu", None, None),
        P("clu", None),
        P("clu", None),
    )
    out_specs = P(None, "clu", None, None)
    return jax.shard_map(
        on_device, mesh=mesh, in_specs=in_specs, out_specs=out_specs, check_vma=False
    )
```

```python
import functools

import jax
import jax.numpy as jnp
from jax import lax
from jax.experimental import pallas as pl
from jax.experimental.pallas import tpu as pltpu
from jax.sharding import PartitionSpec as P

PRODUCTS = 4
REACH = 8
LEAF_ROWS = 32
CLOSE = 2 * REACH + 1
GROUPS = 4
GREETINGS = 7
LOADS = 4
LEAVES = 4
PARENTS = LEAVES // 2
RANK = 64
HALF = RANK // 2
RHS = 8
POINTS = 256
CAPACITY = 16
STRIDE = 8
MESH = pl.DeviceIdType.MESH
F32 = jnp.float32
BF16 = jnp.bfloat16


def nn(a, b):
    return jnp.dot(a, b, preferred_element_type=F32)


def nt(a, b):
    return lax.dot_general(a, b, (((1,), (1,)), ((), ())), preferred_element_type=F32)


def swap_halves(a):
    return pltpu.roll(a, RANK, 1)


def side_by_side(parts):
    return parts[0] if len(parts) == 1 else jnp.concatenate(parts, axis=1)


def kernel(
    devices,
    start_hbm,
    leaf_size,
    diag_hbm,
    near_hbm,
    near_count,
    near_first,
    near_second,
    basis_hbm,
    transfer_hbm,
    coupling,
    send_slot,
    far_target,
    out_hbm,
    start,
    basis,
    transfer,
    raw,
    turned,
    parent_w,
    leaf_w,
    parent_slots,
    leaf_slots,
    near,
    diag,
    both_basis,
    gram,
    coefs,
    last_far,
    point_mask,
    vector,
    out,
    extended,
    hand,
    send,
    recv,
    leaf_send,
    leaf_recv,
    x_out,
    x_in,
    near_out,
    near_in,
    load_sem,
    out_sem,
    hand_sem,
    handed_sem,
    send_sem,
    recv_sem,
    side_sem,
):
    me = lax.axis_index("clu")
    chips = devices // 2
    group = chips // GROUPS
    load_rows = HALF // LOADS
    pair_count = 2 * devices

    def wrap(index):
        if devices & (devices - 1):
            return lax.rem(index, devices)
        return index & (devices - 1)

    def flipped(index, w):
        return index + w - 2 * (index & w)

    def mixed(w):
        return flipped(w, 4 * (w & 24) & (devices - 1))

    def partner(w):
        return flipped(me, mixed(w))

    def leaf_partner(v):
        return wrap(me + (v - REACH + devices))

    raw_loads = [
        [
            pltpu.make_async_copy(
                coupling.at[pl.ds(first, load_rows)],
                raw.at[pl.ds(first, load_rows)],
                load_sem.at[c, h],
            )
            for h, first in enumerate((c * load_rows, HALF + c * load_rows))
        ]
        for c in range(LOADS)
    ]
    near_load = pltpu.make_async_copy(near_hbm, near, load_sem.at[LOADS, 0])
    diag_load = pltpu.make_async_copy(diag_hbm, diag, load_sem.at[LOADS, 1])
    small_loads = [
        pltpu.make_async_copy(start_hbm, start, load_sem.at[LOADS + 1, 0]),
        pltpu.make_async_copy(basis_hbm, basis, load_sem.at[LOADS + 1, 1]),
        pltpu.make_async_copy(transfer_hbm, transfer, load_sem.at[LOADS + 2, 0]),
    ]
    for loads in raw_loads:
        for load in loads:
            load.start()
    for load in small_loads:
        load.start()
    near_load.start()
    diag_load.start()

    barrier = pltpu.get_barrier_semaphore()

    def greet(w):
        pl.semaphore_signal(
            barrier, inc=1, device_id=(partner(w),), device_id_type=MESH
        )

    def greet_some(k, carry):
        for i in range(GREETINGS):
            greet(1 + k * GREETINGS + i)
        return carry

    lax.fori_loop(0, (devices - 1) // GREETINGS, greet_some, 0)
    for w in range(1 + (devices - 1) // GREETINGS * GREETINGS, devices):
        greet(w)

    for load in small_loads:
        load.wait()

    point_ids = lax.broadcasted_iota(jnp.int32, (RHS, POINTS), 1)
    for l in range(LEAVES):
        inside = jnp.where(point_ids < leaf_size[l], 1.0, 0.0)
        point_mask[l] = inside
        vector[l] = start[l] * inside

    for l in range(LEAVES):
        moved = transfer[l].T
        high = moved.astype(BF16)
        low = (moved - high.astype(F32)).astype(BF16)
        own = basis[l]
        both_basis[l] = jnp.concatenate(
            [nn(high, own) + nn(low, own), own.astype(F32)], axis=0
        ).astype(BF16)
        masked = both_basis[l].astype(F32) * point_mask[l][:1]
        gram[l] = nt(masked.astype(BF16), both_basis[l]).astype(BF16)
        coefs[l] = nt(vector[l].astype(BF16), both_basis[l])
        last_far[l] = jnp.zeros((RHS, 2 * RANK), F32)

    def one_hot(rows, wanted):
        row = lax.broadcasted_iota(jnp.int32, (rows, pair_count), 0)
        column = lax.broadcasted_iota(jnp.int32, (rows, pair_count), 1)
        return jnp.where(column == wanted(row), 1.0, 0.0)

    needed = jnp.concatenate(
        [
            one_hot(devices, lambda w: 2 * partner(w) + 1),
            one_hot(LEAF_ROWS, lambda v: 2 * leaf_partner(v)),
        ],
        axis=0,
    ).astype(BF16)

    def turn(k, carry):
        both = jnp.concatenate([raw[k], raw[k + HALF]], axis=0).astype(BF16)
        turned[pl.ds(k, devices + LEAF_ROWS, stride=HALF), :] = nt(needed, both)
        return carry

    for c in range(LOADS):
        for load in raw_loads[c]:
            load.wait()
        lax.fori_loop(c * load_rows, (c + 1) * load_rows, turn, 0, unroll=4)

    left = lax.broadcasted_iota(jnp.int32, (RHS, 2 * RANK), 1) < RANK

    def on_left(rows):
        return jnp.concatenate([left] * (rows // RHS), axis=0)

    def build(w, slots, u, row, first, second):
        tiles = [
            turned[pl.ds(pl.multiple_of((row + i) * HALF, HALF), HALF), :] for i in range(2)
        ]
        swapped = [swap_halves(tile) for tile in tiles]
        w[u] = jnp.concatenate(
            [
                jnp.where(on_left(HALF), tiles[0], swapped[1]),
                jnp.where(on_left(HALF), swapped[0], tiles[1]),
            ],
            axis=0,
        ).astype(BF16)
        slots[u, 0] = jnp.where(left, far_target[0, first], far_target[0, second])
        slots[u, 1] = jnp.where(left, send_slot[0, first], send_slot[0, second])
        slots[u, 2] = jnp.where(left, send_slot[0, second], send_slot[0, first])

    def build_parent(u, carry):
        first, second = [2 * partner(2 * u + i) + 1 for i in range(2)]
        build(parent_w, parent_slots, u, 2 * u, first, second)
        return carry

    def build_leaf(u, carry):
        first, second = [2 * leaf_partner(2 * u + i) for i in range(2)]
        build(leaf_w, leaf_slots, u, devices + 2 * u, first, second)
        return carry

    lax.fori_loop(0, devices // 2, build_parent, 0, unroll=8)
    lax.fori_loop(0, (CLOSE + 1) // 2, build_leaf, 0, unroll=3)
    for n in range(PRODUCTS):
        leaf_recv[n, CLOSE] = jnp.zeros((RHS, 2 * RANK), BF16)

    near_load.wait()
    diag_load.wait()
    pl.semaphore_wait(barrier, devices - 1)

    def remote(src, dst, out_sem, in_sem, target):
        return pltpu.make_async_remote_copy(
            src_ref=src,
            dst_ref=dst,
            send_sem=out_sem,
            recv_sem=in_sem,
            device_id=(target,),
            device_id_type=MESH,
        )

    def x_copy(n):
        return remote(
            x_out.at[n], x_in.at[n], side_sem.at[n, 0], side_sem.at[n, 1], leaf_partner(REACH - 1)
        )

    def near_copy(n):
        return remote(
            near_out.at[n], near_in.at[n], side_sem.at[n, 2], side_sem.at[n, 3], leaf_partner(REACH + 1)
        )

    def out_copy(n):
        return pltpu.make_async_copy(out.at[n + 1], out_hbm.at[n], out_sem.at[n])

    def hand_copy(n, g):
        chips_of = pl.ds(g * group, group)
        return remote(
            hand.at[n, chips_of],
            send.at[n, chips_of, 1],
            hand_sem.at[n],
            handed_sem.at[n, g],
            partner(1),
        )

    def parent_copy(n, u, g):
        return remote(
            send.at[n, u],
            recv.at[n, u],
            send_sem.at[n, 0],
            recv_sem.at[n, g],
            partner(2 * u),
        )

    def leaf_copy(n, v):
        return remote(
            leaf_send.at[n, pl.ds(v, 1)],
            leaf_recv.at[n, pl.ds(2 * REACH - v, 1)],
            send_sem.at[n, 1],
            recv_sem.at[n, GROUPS],
            leaf_partner(v),
        )

    def wait_for(tiles, sem):
        pltpu.make_async_copy(tiles, tiles, sem).wait()

    def chosen(slot, rows, first):
        count = rows.shape[0] // RHS
        result = rows[(count - 1) * RHS :]
        for t in reversed(range(count - 1)):
            result = jnp.where(slot == first + t, rows[t * RHS : (t + 1) * RHS], result)
        return result

    def kept(slot, value, first, count):
        return jnp.concatenate(
            [jnp.where(slot == first + t, value, 0.0) for t in range(count)], axis=0
        )

    def hops(u):
        return sum((0, 1, 2, 1)[mixed(2 * u) >> shift & 3] for shift in (1, 3, 5))

    def chips_in(g):
        return list(range(g * group, (g + 1) * group))

    leaf_pairs = list(range((CLOSE + 1) // 2))

    def finish_vector(n):
        values = []
        for l in range(LEAVES):
            value = vector[l] + nn(last_far[l].astype(BF16), both_basis[l])
            value = value * point_mask[l]
            out[n, l] = value
            values.append(value)
        return values

    def product(n, carry):
        coef = [coefs[l] for l in range(LEAVES)]

        parent = jnp.concatenate(
            [coef[2 * q] + coef[2 * q + 1] for q in range(PARENTS)], axis=0
        )
        leaf = jnp.concatenate(coef, axis=0)
        leaf_turned = swap_halves(leaf)
        parent_twice = jnp.where(on_left(PARENTS * RHS), parent, swap_halves(parent))
        leaf_twice = jnp.where(on_left(LEAVES * RHS), leaf_turned, leaf)
        parent_rows = parent[:, :RANK].astype(BF16)
        leaf_rows = leaf_turned[:, :RANK].astype(BF16)

        def fill(rows, twice, w, slots, first_slot, pairs, store):
            for k in range(0, len(pairs), 2):
                us = pairs[k : k + 2]
                made = nn(rows, side_by_side([w[u] for u in us]))
                for i, u in enumerate(us):
                    block = made[:, i * 2 * RANK : (i + 1) * 2 * RANK]
                    outward = swap_halves(chosen(slots[u, 0], block, first_slot))
                    own = chosen(slots[u, 1], twice, first_slot)
                    store(2 * u, jnp.where(left, own, outward).astype(BF16))
                    store(2 * u + 1, jnp.where(left, outward, own).astype(BF16))

        def store_parent(w, tile):
            if w % 2:
                hand[n, w // 2] = tile
            else:
                send[n, w // 2, 0] = tile

        def store_leaf(v, tile):
            if v == REACH:
                leaf_recv[n, v] = tile
            elif v < CLOSE:
                leaf_send[n, v] = tile

        def fill_group(g):
            fill(
                parent_rows,
                parent_twice,
                parent_w,
                parent_slots,
                LEAVES,
                chips_in(g),
                store_parent,
            )
            hand_copy(n, g).start()

        def send_group(g):
            wait_for(send.at[n, pl.ds(g * group, group), 1], handed_sem.at[n, g])
            for u in sorted(chips_in(g), key=hops, reverse=True):
                if u:
                    parent_copy(n, u, g).start()

        fill_group(1)
        fill_group(2)
        fill_group(3)
        send_group(1)
        fill_group(0)
        send_group(2)
        fill(
            leaf_rows, leaf_twice, leaf_w, leaf_slots, 0, leaf_pairs, store_leaf
        )
        for v in range(CLOSE):
            if v != REACH:
                leaf_copy(n, v).start()

        send_group(3)
        exact = finish_vector(n)
        rounded = [value.astype(BF16) for value in exact]
        x_out[n] = jnp.concatenate(exact, axis=0).astype(BF16)
        x_copy(n).start()

        send_group(0)

        @pl.when(n > 0)
        def _():
            out_copy(n - 1).start()

        for l in range(LEAVES):
            extended[l] = rounded[l].astype(F32)

        def live_slot(slots, e):
            slot = jnp.where(e < near_count[0], slots[e], -1)
            return jnp.full((RHS, POINTS), slot, jnp.int32)

        def add_backward(step, sofar):
            for i in range(STRIDE):
                e = step * STRIDE + i
                own = extended[near_first[e]]
                slot = live_slot(near_second, e)
                spread = jnp.concatenate(
                    [jnp.where(slot == s, own, 0.0) for s in range(2 * LEAVES)], axis=0
                ).astype(BF16)
                sofar = sofar + nn(spread, near[e])
            return sofar

        backward = lax.fori_loop(
            0,
            CAPACITY // STRIDE,
            add_backward,
            jnp.zeros((2 * LEAVES * RHS, POINTS), F32),
        )
        near_out[n] = backward[LEAVES * RHS :].astype(BF16)
        near_copy(n).start()
        total = backward[: LEAVES * RHS] + jnp.concatenate(
            [nn(rounded[l], diag[l]) for l in range(LEAVES)], axis=0
        )

        x_copy(n).wait_recv()
        following = x_in[n].astype(F32)
        for l in range(LEAVES):
            extended[LEAVES + l] = following[l * RHS : (l + 1) * RHS]

        def add_forward(step, sofar):
            for i in range(STRIDE):
                e = step * STRIDE + i
                other = extended[near_second[e]]
                slot = live_slot(near_first, e)
                spread = jnp.concatenate(
                    [jnp.where(slot == t, other, 0.0) for t in range(LEAVES)], axis=0
                ).astype(BF16)
                sofar = sofar + nt(spread, near[e])
            return sofar

        total = lax.fori_loop(0, CAPACITY // STRIDE, add_forward, total)

        def take(tiles, w, slots, first_slot, slot_count, pairs, sofar):
            through, handed = sofar
            for k in range(0, len(pairs), 2):
                us, rows = pairs[k : k + 2], []
                for u in us:
                    even, odd = [tile.astype(F32) for tile in tiles(u)]
                    incoming = jnp.where(left, even, odd)
                    outcome = jnp.where(left, odd, even)
                    rows.append(kept(slots[u, 0], incoming, first_slot, slot_count))
                    handed = handed + kept(slots[u, 2], outcome, first_slot, slot_count)
                through = through + nt(
                    side_by_side(rows).astype(BF16), side_by_side([w[u] for u in us])
                )
            return through, handed

        def nothing(count):
            return (
                jnp.zeros((count * RHS, RANK), F32),
                jnp.zeros((count * RHS, 2 * RANK), F32),
            )

        near_copy(n).wait_recv()
        total = total + near_in[n].astype(F32)
        near_coef = []
        for l in range(LEAVES):
            value = total[l * RHS : (l + 1) * RHS] * point_mask[l]
            vector[l] = value
            near_coef.append(nt(value.astype(BF16), both_basis[l]))

        def parent_tiles(u):
            box = send if isinstance(u, int) and u == 0 else recv
            return box[n, u, 0], box[n, u, 1]

        def leaf_tiles(u):
            return leaf_recv[n, 2 * u], leaf_recv[n, 2 * u + 1]

        def take_group(g, sofar):
            pairs = [g * group + i for i in range(group)]
            return take(
                parent_tiles, parent_w, parent_slots, LEAVES, PARENTS, pairs, sofar
            )

        def take_whole_group(g, sofar):
            wait_for(recv.at[n, pl.ds(g * group, group)], recv_sem.at[n, g])
            return take_group(g, sofar)

        parent_sum = lax.fori_loop(1, GROUPS, take_whole_group, nothing(PARENTS))
        wait_for(recv.at[n, pl.ds(1, group - 1)], recv_sem.at[n, 0])
        wait_for(leaf_recv.at[n, pl.ds(0, CLOSE - 1)], recv_sem.at[n, GROUPS])
        parent_sum = take_group(0, parent_sum)
        leaf_sum = take(
            leaf_tiles, leaf_w, leaf_slots, 0, LEAVES, leaf_pairs, nothing(LEAVES)
        )

        def whole(through, handed):
            return through + (handed + swap_halves(handed))[:, :RANK]

        parent_far = whole(*parent_sum)
        leaf_far = whole(*leaf_sum)

        for l in range(LEAVES):
            q = l // 2
            both = jnp.concatenate(
                [parent_far[q * RHS : (q + 1) * RHS], leaf_far[l * RHS : (l + 1) * RHS]], axis=1
            )
            last_far[l] = both
            coefs[l] = near_coef[l] + nn(both.astype(BF16), gram[l])
        return carry

    lax.fori_loop(0, PRODUCTS, product, 0)
    finish_vector(PRODUCTS)
    out_copy(PRODUCTS - 1).start()

    def finish(n, carry):
        wait_for(hand.at[n], hand_sem.at[n])
        wait_for(send.at[n, pl.ds(1, chips - 1)], send_sem.at[n, 0])
        wait_for(leaf_send.at[n, pl.ds(0, CLOSE - 1)], send_sem.at[n, 1])
        x_copy(n).wait_send()
        near_copy(n).wait_send()
        out_copy(n).wait()
        return carry

    lax.fori_loop(0, PRODUCTS, finish, 0)


def on_device(
    start_vector,
    leaf_size,
    diag_blocks,
    near_blocks,
    near_count,
    near_first,
    near_second,
    leaf_basis,
    transfer,
    coupling,
    send_slot,
    far_target,
):
    devices = lax.axis_size("clu")
    tile = (RHS, 2 * RANK)
    close_pairs = (CLOSE + 1) // 2
    smem = pl.BlockSpec(memory_space=pltpu.SMEM)
    hbm = pl.BlockSpec(memory_space=pltpu.HBM)
    sides = (PRODUCTS, LEAVES * RHS, POINTS)
    return pl.pallas_call(
        functools.partial(kernel, devices),
        out_shape=jax.ShapeDtypeStruct((PRODUCTS, LEAVES, RHS, POINTS), F32),
        in_specs=[
            hbm,
            smem,
            hbm,
            hbm,
            smem,
            smem,
            smem,
            hbm,
            hbm,
            hbm,
            smem,
            smem,
        ],
        out_specs=hbm,
        scratch_shapes=[
            pltpu.VMEM((LEAVES, RHS, POINTS), F32),
            pltpu.VMEM((LEAVES, RANK, POINTS), BF16),
            pltpu.VMEM((LEAVES, RANK, RANK), F32),
            pltpu.VMEM((RANK, RANK, 2 * devices), F32),
            pltpu.VMEM(((devices + LEAF_ROWS) * HALF, 2 * RANK), F32),
            pltpu.VMEM((devices // 2, RANK, 2 * RANK), BF16),
            pltpu.VMEM((close_pairs, RANK, 2 * RANK), BF16),
            pltpu.VMEM((devices // 2, 3, *tile), jnp.int32),
            pltpu.VMEM((close_pairs, 3, *tile), jnp.int32),
            pltpu.VMEM((CAPACITY, POINTS, POINTS), BF16),
            pltpu.VMEM((LEAVES, POINTS, POINTS), BF16),
            pltpu.VMEM((LEAVES, 2 * RANK, POINTS), BF16),
            pltpu.VMEM((LEAVES, 2 * RANK, 2 * RANK), BF16),
            pltpu.VMEM((LEAVES, *tile), F32),
            pltpu.VMEM((LEAVES, *tile), F32),
            pltpu.VMEM((LEAVES, RHS, POINTS), F32),
            pltpu.VMEM((LEAVES, RHS, POINTS), F32),
            pltpu.VMEM((PRODUCTS + 1, LEAVES, RHS, POINTS), F32),
            pltpu.VMEM((2 * LEAVES, RHS, POINTS), F32),
            pltpu.VMEM((PRODUCTS, devices // 2, *tile), BF16),
            pltpu.VMEM((PRODUCTS, devices // 2, 2, *tile), BF16),
            pltpu.VMEM((PRODUCTS, devices // 2, 2, *tile), BF16),
            pltpu.VMEM((PRODUCTS, CLOSE + 1, *tile), BF16),
            pltpu.VMEM((PRODUCTS, CLOSE + 1, *tile), BF16),
            pltpu.VMEM(sides, BF16),
            pltpu.VMEM(sides, BF16),
            pltpu.VMEM(sides, BF16),
            pltpu.VMEM(sides, BF16),
            pltpu.SemaphoreType.DMA((LOADS + 3, 2)),
            pltpu.SemaphoreType.DMA((PRODUCTS,)),
            pltpu.SemaphoreType.DMA((PRODUCTS,)),
            pltpu.SemaphoreType.DMA((PRODUCTS, GROUPS)),
            pltpu.SemaphoreType.DMA((PRODUCTS, 2)),
            pltpu.SemaphoreType.DMA((PRODUCTS, GROUPS + 1)),
            pltpu.SemaphoreType.DMA((PRODUCTS, 4)),
        ],
        compiler_params=pltpu.CompilerParams(
            collective_id=0, has_side_effects=True, vmem_limit_bytes=56 * 1024 * 1024
        ),
        name="h2_products",
    )(
        start_vector,
        leaf_size,
        diag_blocks,
        near_blocks,
        near_count,
        near_first,
        near_second,
        leaf_basis,
        transfer,
        coupling.transpose(1, 2, 0),
        send_slot,
        far_target,
    )


def solution(mesh):
    in_specs = (
        P("clu", None, None),
        P("clu"),
        P("clu", None, None),
        P("clu", None, None),
        P("clu"),
        P("clu"),
        P("clu"),
        P("clu", None, None),
        P("clu", None, None),
        P("clu", None, None),
        P("clu", None),
        P("clu", None),
    )
    out_specs = P(None, "clu", None, None)
    return jax.shard_map(
        on_device, mesh=mesh, in_specs=in_specs, out_specs=out_specs, check_vma=False
    )
```

```python
import functools

import jax
import jax.numpy as jnp
from jax import lax
from jax.experimental import pallas as pl
from jax.experimental.pallas import tpu as pltpu
from jax.sharding import PartitionSpec as P

PRODUCTS = 4
REACH = 8
LEAF_ROWS = 32
CLOSE = 2 * REACH + 1
GROUPS = 4
GREETINGS = 7
LOADS = 4
LEAVES = 4
PARENTS = LEAVES // 2
RANK = 64
HALF = RANK // 2
RHS = 8
POINTS = 256
CAPACITY = 16
STRIDE = 8
MESH = pl.DeviceIdType.MESH
F32 = jnp.float32
BF16 = jnp.bfloat16


def nn(a, b):
    return jnp.dot(a, b, preferred_element_type=F32)


def nt(a, b):
    return lax.dot_general(a, b, (((1,), (1,)), ((), ())), preferred_element_type=F32)


def swap_halves(a):
    return pltpu.roll(a, RANK, 1)


def side_by_side(parts):
    return parts[0] if len(parts) == 1 else jnp.concatenate(parts, axis=1)


def kernel(
    devices,
    start_hbm,
    leaf_size,
    diag_hbm,
    near_hbm,
    near_count,
    near_first,
    near_second,
    basis_hbm,
    transfer_hbm,
    coupling,
    send_slot,
    far_target,
    out_hbm,
    start,
    basis,
    transfer,
    raw,
    turned,
    parent_w,
    leaf_w,
    parent_slots,
    leaf_slots,
    near,
    diag,
    both_basis,
    gram,
    coefs,
    last_far,
    point_mask,
    vector,
    out,
    extended,
    send,
    recv,
    leaf_send,
    leaf_recv,
    x_out,
    x_in,
    near_out,
    near_in,
    load_sem,
    out_sem,
    send_sem,
    recv_sem,
    side_sem,
):
    me = lax.axis_index("clu")
    group = devices // GROUPS
    load_rows = HALF // LOADS
    pair_count = 2 * devices

    def wrap(index):
        if devices & (devices - 1):
            return lax.rem(index, devices)
        return index & (devices - 1)

    def flipped(index, w):
        return index + w - 2 * (index & w)

    def partner(w):
        return flipped(me, w)

    def leaf_partner(v):
        return wrap(me + (v - REACH + devices))

    raw_loads = [
        [
            pltpu.make_async_copy(
                coupling.at[pl.ds(first, load_rows)],
                raw.at[pl.ds(first, load_rows)],
                load_sem.at[c, h],
            )
            for h, first in enumerate((c * load_rows, HALF + c * load_rows))
        ]
        for c in range(LOADS)
    ]
    near_load = pltpu.make_async_copy(near_hbm, near, load_sem.at[LOADS, 0])
    diag_load = pltpu.make_async_copy(diag_hbm, diag, load_sem.at[LOADS, 1])
    small_loads = [
        pltpu.make_async_copy(start_hbm, start, load_sem.at[LOADS + 1, 0]),
        pltpu.make_async_copy(basis_hbm, basis, load_sem.at[LOADS + 1, 1]),
        pltpu.make_async_copy(transfer_hbm, transfer, load_sem.at[LOADS + 2, 0]),
    ]
    for loads in raw_loads:
        for load in loads:
            load.start()
    for load in small_loads:
        load.start()
    near_load.start()
    diag_load.start()

    barrier = pltpu.get_barrier_semaphore()

    def greet(w):
        pl.semaphore_signal(
            barrier, inc=1, device_id=(partner(w),), device_id_type=MESH
        )

    def greet_some(k, carry):
        for i in range(GREETINGS):
            greet(1 + k * GREETINGS + i)
        return carry

    lax.fori_loop(0, (devices - 1) // GREETINGS, greet_some, 0)
    for w in range(1 + (devices - 1) // GREETINGS * GREETINGS, devices):
        greet(w)

    for load in small_loads:
        load.wait()

    point_ids = lax.broadcasted_iota(jnp.int32, (RHS, POINTS), 1)
    for l in range(LEAVES):
        inside = jnp.where(point_ids < leaf_size[l], 1.0, 0.0)
        point_mask[l] = inside
        vector[l] = start[l] * inside

    for l in range(LEAVES):
        moved = transfer[l].T
        high = moved.astype(BF16)
        low = (moved - high.astype(F32)).astype(BF16)
        own = basis[l]
        both_basis[l] = jnp.concatenate(
            [nn(high, own) + nn(low, own), own.astype(F32)], axis=0
        ).astype(BF16)
        masked = both_basis[l].astype(F32) * point_mask[l][:1]
        gram[l] = nt(masked.astype(BF16), both_basis[l]).astype(BF16)
        coefs[l] = nt(vector[l].astype(BF16), both_basis[l])
        last_far[l] = jnp.zeros((RHS, 2 * RANK), F32)

    def one_hot(rows, wanted):
        row = lax.broadcasted_iota(jnp.int32, (rows, pair_count), 0)
        column = lax.broadcasted_iota(jnp.int32, (rows, pair_count), 1)
        return jnp.where(column == wanted(row), 1.0, 0.0)

    needed = jnp.concatenate(
        [
            one_hot(devices, lambda w: 2 * flipped(me, w) + 1),
            one_hot(LEAF_ROWS, lambda v: 2 * leaf_partner(v)),
        ],
        axis=0,
    ).astype(BF16)

    def turn(k, carry):
        both = jnp.concatenate([raw[k], raw[k + HALF]], axis=0).astype(BF16)
        turned[pl.ds(k, devices + LEAF_ROWS, stride=HALF), :] = nt(needed, both)
        return carry

    for c in range(LOADS):
        for load in raw_loads[c]:
            load.wait()
        lax.fori_loop(c * load_rows, (c + 1) * load_rows, turn, 0, unroll=4)

    left = lax.broadcasted_iota(jnp.int32, (RHS, 2 * RANK), 1) < RANK

    def on_left(rows):
        return jnp.concatenate([left] * (rows // RHS), axis=0)

    def build(w, slots, u, row, first, second):
        tiles = [
            turned[pl.ds(pl.multiple_of((row + i) * HALF, HALF), HALF), :] for i in range(2)
        ]
        swapped = [swap_halves(tile) for tile in tiles]
        w[u] = jnp.concatenate(
            [
                jnp.where(on_left(HALF), tiles[0], swapped[1]),
                jnp.where(on_left(HALF), swapped[0], tiles[1]),
            ],
            axis=0,
        ).astype(BF16)
        slots[u, 0] = jnp.where(left, far_target[0, first], far_target[0, second])
        slots[u, 1] = jnp.where(left, send_slot[0, first], send_slot[0, second])
        slots[u, 2] = jnp.where(left, send_slot[0, second], send_slot[0, first])

    def build_parent(u, carry):
        first, second = [2 * partner(2 * u + i) + 1 for i in range(2)]
        build(parent_w, parent_slots, u, 2 * u, first, second)
        return carry

    def build_leaf(u, carry):
        first, second = [2 * leaf_partner(2 * u + i) for i in range(2)]
        build(leaf_w, leaf_slots, u, devices + 2 * u, first, second)
        return carry

    lax.fori_loop(0, devices // 2, build_parent, 0, unroll=8)
    lax.fori_loop(0, (CLOSE + 1) // 2, build_leaf, 0, unroll=3)
    for n in range(PRODUCTS):
        leaf_recv[n, CLOSE] = jnp.zeros((RHS, 2 * RANK), BF16)

    near_load.wait()
    diag_load.wait()
    pl.semaphore_wait(barrier, devices - 1)

    def remote(src, dst, out_sem, in_sem, target):
        return pltpu.make_async_remote_copy(
            src_ref=src,
            dst_ref=dst,
            send_sem=out_sem,
            recv_sem=in_sem,
            device_id=(target,),
            device_id_type=MESH,
        )

    def x_copy(n):
        return remote(
            x_out.at[n], x_in.at[n], side_sem.at[n, 0], side_sem.at[n, 1], leaf_partner(REACH - 1)
        )

    def near_copy(n):
        return remote(
            near_out.at[n], near_in.at[n], side_sem.at[n, 2], side_sem.at[n, 3], leaf_partner(REACH + 1)
        )

    def out_copy(n):
        return pltpu.make_async_copy(out.at[n + 1], out_hbm.at[n], out_sem.at[n])

    def parent_copy(n, w, g):
        return remote(
            send.at[n, pl.ds(w, 1)],
            recv.at[n, pl.ds(w, 1)],
            send_sem.at[n, 0],
            recv_sem.at[n, g],
            partner(w),
        )

    def leaf_copy(n, v):
        return remote(
            leaf_send.at[n, pl.ds(v, 1)],
            leaf_recv.at[n, pl.ds(2 * REACH - v, 1)],
            send_sem.at[n, 1],
            recv_sem.at[n, GROUPS],
            leaf_partner(v),
        )

    def wait_for(tiles, sem):
        pltpu.make_async_copy(tiles, tiles, sem).wait()

    def chosen(slot, rows, first):
        count = rows.shape[0] // RHS
        result = rows[(count - 1) * RHS :]
        for t in reversed(range(count - 1)):
            result = jnp.where(slot == first + t, rows[t * RHS : (t + 1) * RHS], result)
        return result

    def kept(slot, value, first, count):
        return jnp.concatenate(
            [jnp.where(slot == first + t, value, 0.0) for t in range(count)], axis=0
        )

    def hops(u):
        return sum((0, 1, 2, 1)[u >> shift & 3] for shift in (0, 2, 4))

    chips = devices // 2
    order = sorted(range(1, chips), key=lambda u: (-hops(u), u * 37 % chips)) + [0]
    leaf_pairs = list(range((CLOSE + 1) // 2))
    cuts = [0, chips // 8, 3 * chips // 8, 11 * chips // 16, chips]
    chip_groups = [order[cuts[g] : cuts[g + 1]] for g in range(GROUPS)]

    def finish_vector(n):
        values = []
        for l in range(LEAVES):
            value = vector[l] + nn(last_far[l].astype(BF16), both_basis[l])
            value = value * point_mask[l]
            out[n, l] = value
            values.append(value)
        return values

    def product(n, carry):
        coef = [coefs[l] for l in range(LEAVES)]

        parent = jnp.concatenate(
            [coef[2 * q] + coef[2 * q + 1] for q in range(PARENTS)], axis=0
        )
        leaf = jnp.concatenate(coef, axis=0)
        leaf_turned = swap_halves(leaf)
        parent_twice = jnp.where(on_left(PARENTS * RHS), parent, swap_halves(parent))
        leaf_twice = jnp.where(on_left(LEAVES * RHS), leaf_turned, leaf)
        parent_rows = parent[:, :RANK].astype(BF16)
        leaf_rows = leaf_turned[:, :RANK].astype(BF16)

        def fill(rows, twice, w, slots, first_slot, pairs, store):
            for k in range(0, len(pairs), 2):
                us = pairs[k : k + 2]
                made = nn(rows, side_by_side([w[u] for u in us]))
                for i, u in enumerate(us):
                    block = made[:, i * 2 * RANK : (i + 1) * 2 * RANK]
                    outward = swap_halves(chosen(slots[u, 0], block, first_slot))
                    own = chosen(slots[u, 1], twice, first_slot)
                    store(2 * u, jnp.where(left, own, outward).astype(BF16))
                    store(2 * u + 1, jnp.where(left, outward, own).astype(BF16))

        def store_parent(w, tile):
            send[n, w] = tile

        def store_leaf(v, tile):
            if v == REACH:
                leaf_recv[n, v] = tile
            elif v < CLOSE:
                leaf_send[n, v] = tile

        for g in range(GROUPS):
            fill(
                parent_rows,
                parent_twice,
                parent_w,
                parent_slots,
                LEAVES,
                chip_groups[g],
                store_parent,
            )
            for u in chip_groups[g]:
                for w in (2 * u, 2 * u + 1):
                    if w:
                        parent_copy(n, w, g).start()
        fill(
            leaf_rows, leaf_twice, leaf_w, leaf_slots, 0, leaf_pairs, store_leaf
        )
        for v in range(CLOSE):
            if v != REACH:
                leaf_copy(n, v).start()

        exact = finish_vector(n)
        rounded = [value.astype(BF16) for value in exact]
        x_out[n] = jnp.concatenate(exact, axis=0).astype(BF16)
        x_copy(n).start()

        @pl.when(n > 0)
        def _():
            out_copy(n - 1).start()

        for l in range(LEAVES):
            extended[l] = rounded[l].astype(F32)

        def live_slot(slots, e):
            slot = jnp.where(e < near_count[0], slots[e], -1)
            return jnp.full((RHS, POINTS), slot, jnp.int32)

        def add_backward(step, sofar):
            for i in range(STRIDE):
                e = step * STRIDE + i
                own = extended[near_first[e]]
                slot = live_slot(near_second, e)
                spread = jnp.concatenate(
                    [jnp.where(slot == s, own, 0.0) for s in range(2 * LEAVES)], axis=0
                ).astype(BF16)
                sofar = sofar + nn(spread, near[e])
            return sofar

        backward = lax.fori_loop(
            0,
            CAPACITY // STRIDE,
            add_backward,
            jnp.zeros((2 * LEAVES * RHS, POINTS), F32),
        )
        near_out[n] = backward[LEAVES * RHS :].astype(BF16)
        near_copy(n).start()
        total = backward[: LEAVES * RHS] + jnp.concatenate(
            [nn(rounded[l], diag[l]) for l in range(LEAVES)], axis=0
        )

        x_copy(n).wait_recv()
        following = x_in[n].astype(F32)
        for l in range(LEAVES):
            extended[LEAVES + l] = following[l * RHS : (l + 1) * RHS]

        def add_forward(step, sofar):
            for i in range(STRIDE):
                e = step * STRIDE + i
                other = extended[near_second[e]]
                slot = live_slot(near_first, e)
                spread = jnp.concatenate(
                    [jnp.where(slot == t, other, 0.0) for t in range(LEAVES)], axis=0
                ).astype(BF16)
                sofar = sofar + nt(spread, near[e])
            return sofar

        total = lax.fori_loop(0, CAPACITY // STRIDE, add_forward, total)

        def take(box, w, slots, first_slot, slot_count, pairs, sofar):
            through, handed = sofar
            for k in range(0, len(pairs), 2):
                us, rows = pairs[k : k + 2], []
                for u in us:
                    outer = send if u == 0 and box is recv else box
                    even = outer[n, 2 * u].astype(F32)
                    odd = box[n, 2 * u + 1].astype(F32)
                    incoming = jnp.where(left, even, odd)
                    outcome = jnp.where(left, odd, even)
                    rows.append(kept(slots[u, 0], incoming, first_slot, slot_count))
                    handed = handed + kept(slots[u, 2], outcome, first_slot, slot_count)
                through = through + nt(
                    side_by_side(rows).astype(BF16), side_by_side([w[u] for u in us])
                )
            return through, handed

        def nothing(count):
            return (
                jnp.zeros((count * RHS, RANK), F32),
                jnp.zeros((count * RHS, 2 * RANK), F32),
            )

        near_copy(n).wait_recv()
        total = total + near_in[n].astype(F32)
        near_coef = []
        for l in range(LEAVES):
            value = total[l * RHS : (l + 1) * RHS] * point_mask[l]
            vector[l] = value
            near_coef.append(nt(value.astype(BF16), both_basis[l]))

        parent_sum = nothing(PARENTS)
        wait_for(leaf_recv.at[n, pl.ds(0, CLOSE - 1)], recv_sem.at[n, GROUPS])
        leaf_sum = take(
            leaf_recv, leaf_w, leaf_slots, 0, LEAVES, leaf_pairs, nothing(LEAVES)
        )
        for g in reversed(range(GROUPS)):
            messages = 2 * len(chip_groups[g]) - (1 if g == GROUPS - 1 else 0)
            wait_for(recv.at[n, pl.ds(1, messages)], recv_sem.at[n, g])
            parent_sum = take(
                recv, parent_w, parent_slots, LEAVES, PARENTS, chip_groups[g], parent_sum
            )

        def whole(through, handed):
            return through + (handed + swap_halves(handed))[:, :RANK]

        parent_far = whole(*parent_sum)
        leaf_far = whole(*leaf_sum)

        for l in range(LEAVES):
            q = l // 2
            both = jnp.concatenate(
                [parent_far[q * RHS : (q + 1) * RHS], leaf_far[l * RHS : (l + 1) * RHS]], axis=1
            )
            last_far[l] = both
            coefs[l] = near_coef[l] + nn(both.astype(BF16), gram[l])
        return carry

    lax.fori_loop(0, PRODUCTS, product, 0)
    finish_vector(PRODUCTS)
    out_copy(PRODUCTS - 1).start()

    def finish(n, carry):
        wait_for(send.at[n, pl.ds(1, devices - 1)], send_sem.at[n, 0])
        wait_for(leaf_send.at[n, pl.ds(0, CLOSE - 1)], send_sem.at[n, 1])
        x_copy(n).wait_send()
        near_copy(n).wait_send()
        out_copy(n).wait()
        return carry

    lax.fori_loop(0, PRODUCTS, finish, 0)


def on_device(
    start_vector,
    leaf_size,
    diag_blocks,
    near_blocks,
    near_count,
    near_first,
    near_second,
    leaf_basis,
    transfer,
    coupling,
    send_slot,
    far_target,
):
    devices = lax.axis_size("clu")
    tile = (RHS, 2 * RANK)
    close_pairs = (CLOSE + 1) // 2
    smem = pl.BlockSpec(memory_space=pltpu.SMEM)
    hbm = pl.BlockSpec(memory_space=pltpu.HBM)
    sides = (PRODUCTS, LEAVES * RHS, POINTS)
    return pl.pallas_call(
        functools.partial(kernel, devices),
        out_shape=jax.ShapeDtypeStruct((PRODUCTS, LEAVES, RHS, POINTS), F32),
        in_specs=[
            hbm,
            smem,
            hbm,
            hbm,
            smem,
            smem,
            smem,
            hbm,
            hbm,
            hbm,
            smem,
            smem,
        ],
        out_specs=hbm,
        scratch_shapes=[
            pltpu.VMEM((LEAVES, RHS, POINTS), F32),
            pltpu.VMEM((LEAVES, RANK, POINTS), BF16),
            pltpu.VMEM((LEAVES, RANK, RANK), F32),
            pltpu.VMEM((RANK, RANK, 2 * devices), F32),
            pltpu.VMEM(((devices + LEAF_ROWS) * HALF, 2 * RANK), F32),
            pltpu.VMEM((devices // 2, RANK, 2 * RANK), BF16),
            pltpu.VMEM((close_pairs, RANK, 2 * RANK), BF16),
            pltpu.VMEM((devices // 2, 3, *tile), jnp.int32),
            pltpu.VMEM((close_pairs, 3, *tile), jnp.int32),
            pltpu.VMEM((CAPACITY, POINTS, POINTS), BF16),
            pltpu.VMEM((LEAVES, POINTS, POINTS), BF16),
            pltpu.VMEM((LEAVES, 2 * RANK, POINTS), BF16),
            pltpu.VMEM((LEAVES, 2 * RANK, 2 * RANK), BF16),
            pltpu.VMEM((LEAVES, *tile), F32),
            pltpu.VMEM((LEAVES, *tile), F32),
            pltpu.VMEM((LEAVES, RHS, POINTS), F32),
            pltpu.VMEM((LEAVES, RHS, POINTS), F32),
            pltpu.VMEM((PRODUCTS + 1, LEAVES, RHS, POINTS), F32),
            pltpu.VMEM((2 * LEAVES, RHS, POINTS), F32),
            pltpu.VMEM((PRODUCTS, devices, *tile), BF16),
            pltpu.VMEM((PRODUCTS, devices, *tile), BF16),
            pltpu.VMEM((PRODUCTS, CLOSE + 1, *tile), BF16),
            pltpu.VMEM((PRODUCTS, CLOSE + 1, *tile), BF16),
            pltpu.VMEM(sides, BF16),
            pltpu.VMEM(sides, BF16),
            pltpu.VMEM(sides, BF16),
            pltpu.VMEM(sides, BF16),
            pltpu.SemaphoreType.DMA((LOADS + 3, 2)),
            pltpu.SemaphoreType.DMA((PRODUCTS,)),
            pltpu.SemaphoreType.DMA((PRODUCTS, 2)),
            pltpu.SemaphoreType.DMA((PRODUCTS, GROUPS + 1)),
            pltpu.SemaphoreType.DMA((PRODUCTS, 4)),
        ],
        compiler_params=pltpu.CompilerParams(
            collective_id=0, has_side_effects=True, vmem_limit_bytes=56 * 1024 * 1024
        ),
        name="h2_products",
    )(
        start_vector,
        leaf_size,
        diag_blocks,
        near_blocks,
        near_count,
        near_first,
        near_second,
        leaf_basis,
        transfer,
        coupling.transpose(1, 2, 0),
        send_slot,
        far_target,
    )


def solution(mesh):
    in_specs = (
        P("clu", None, None),
        P("clu"),
        P("clu", None, None),
        P("clu", None, None),
        P("clu"),
        P("clu"),
        P("clu"),
        P("clu", None, None),
        P("clu", None, None),
        P("clu", None, None),
        P("clu", None),
        P("clu", None),
    )
    out_specs = P(None, "clu", None, None)
    return jax.shard_map(
        on_device, mesh=mesh, in_specs=in_specs, out_specs=out_specs, check_vma=False
    )
```

```python
import functools

import jax
import jax.numpy as jnp
from jax import lax
from jax.experimental import pallas as pl
from jax.experimental.pallas import tpu as pltpu
from jax.sharding import PartitionSpec as P

PRODUCTS = 4
REACH = 8
LEAF_ROWS = 32
CLOSE = 2 * REACH + 1
CUTS = (0, 8, 16, 26, 38, 50, 64)
GROUPS = len(CUTS) - 1
GREETINGS = 7
LOADS = 4
LEAVES = 4
PARENTS = LEAVES // 2
RANK = 64
HALF = RANK // 2
RHS = 8
POINTS = 256
CAPACITY = 16
STRIDE = 4
MESH = pl.DeviceIdType.MESH
F32 = jnp.float32
BF16 = jnp.bfloat16


def nn(a, b):
    return jnp.dot(a, b, preferred_element_type=F32)


def nt(a, b):
    return lax.dot_general(a, b, (((1,), (1,)), ((), ())), preferred_element_type=F32)


def swap_halves(a):
    return pltpu.roll(a, RANK, 1)


def side_by_side(parts):
    return parts[0] if len(parts) == 1 else jnp.concatenate(parts, axis=1)


def kernel(
    devices,
    start_hbm,
    leaf_size,
    diag_hbm,
    near_hbm,
    near_count,
    near_first,
    near_second,
    basis_hbm,
    transfer_hbm,
    coupling,
    send_slot,
    far_target,
    out_hbm,
    start,
    basis,
    transfer,
    raw,
    turned,
    parent_w,
    leaf_w,
    parent_slots,
    leaf_slots,
    near,
    diag,
    both_basis,
    gram,
    coefs,
    last_far,
    point_mask,
    vector,
    out,
    extended,
    send,
    recv,
    leaf_send,
    leaf_recv,
    x_out,
    x_in,
    near_out,
    near_in,
    load_sem,
    out_sem,
    send_sem,
    recv_sem,
    side_sem,
):
    me = lax.axis_index("clu")
    load_rows = HALF // LOADS
    pair_count = 2 * devices

    def wrap(index):
        if devices & (devices - 1):
            return lax.rem(index, devices)
        return index & (devices - 1)

    def flipped(index, w):
        return index + w - 2 * (index & w)

    def partner(w):
        return flipped(me, w)

    def leaf_partner(v):
        return wrap(me + (v - REACH + devices))

    raw_loads = [
        [
            pltpu.make_async_copy(
                coupling.at[pl.ds(first, load_rows)],
                raw.at[pl.ds(first, load_rows)],
                load_sem.at[c, h],
            )
            for h, first in enumerate((c * load_rows, HALF + c * load_rows))
        ]
        for c in range(LOADS)
    ]
    near_load = pltpu.make_async_copy(near_hbm, near, load_sem.at[LOADS, 0])
    diag_load = pltpu.make_async_copy(diag_hbm, diag, load_sem.at[LOADS, 1])
    small_loads = [
        pltpu.make_async_copy(start_hbm, start, load_sem.at[LOADS + 1, 0]),
        pltpu.make_async_copy(basis_hbm, basis, load_sem.at[LOADS + 1, 1]),
        pltpu.make_async_copy(transfer_hbm, transfer, load_sem.at[LOADS + 2, 0]),
    ]
    for loads in raw_loads:
        for load in loads:
            load.start()
    for load in small_loads:
        load.start()
    near_load.start()
    diag_load.start()

    barrier = pltpu.get_barrier_semaphore()

    def greet(w):
        pl.semaphore_signal(
            barrier, inc=1, device_id=(partner(w),), device_id_type=MESH
        )

    def greet_some(k, carry):
        for i in range(GREETINGS):
            greet(1 + k * GREETINGS + i)
        return carry

    lax.fori_loop(0, (devices - 1) // GREETINGS, greet_some, 0)
    for w in range(1 + (devices - 1) // GREETINGS * GREETINGS, devices):
        greet(w)

    for load in small_loads:
        load.wait()

    point_ids = lax.broadcasted_iota(jnp.int32, (RHS, POINTS), 1)
    for l in range(LEAVES):
        inside = jnp.where(point_ids < leaf_size[l], 1.0, 0.0)
        point_mask[l] = inside
        vector[l] = start[l] * inside

    for l in range(LEAVES):
        moved = transfer[l].T
        high = moved.astype(BF16)
        low = (moved - high.astype(F32)).astype(BF16)
        own = basis[l]
        both_basis[l] = jnp.concatenate(
            [nn(high, own) + nn(low, own), own.astype(F32)], axis=0
        ).astype(BF16)
        masked = both_basis[l].astype(F32) * point_mask[l][:1]
        gram[l] = nt(masked.astype(BF16), both_basis[l]).astype(BF16)
        coefs[l] = nt(vector[l].astype(BF16), both_basis[l])
        last_far[l] = jnp.zeros((RHS, 2 * RANK), F32)

    def one_hot(rows, wanted):
        row = lax.broadcasted_iota(jnp.int32, (rows, pair_count), 0)
        column = lax.broadcasted_iota(jnp.int32, (rows, pair_count), 1)
        return jnp.where(column == wanted(row), 1.0, 0.0)

    needed = jnp.concatenate(
        [
            one_hot(devices, lambda w: 2 * flipped(me, w) + 1),
            one_hot(LEAF_ROWS, lambda v: 2 * leaf_partner(v)),
        ],
        axis=0,
    ).astype(BF16)

    def turn(k, carry):
        both = jnp.concatenate([raw[k], raw[k + HALF]], axis=0).astype(BF16)
        turned[pl.ds(k, devices + LEAF_ROWS, stride=HALF), :] = nt(needed, both)
        return carry

    for c in range(LOADS):
        for load in raw_loads[c]:
            load.wait()
        lax.fori_loop(c * load_rows, (c + 1) * load_rows, turn, 0, unroll=4)

    left = lax.broadcasted_iota(jnp.int32, (RHS, 2 * RANK), 1) < RANK

    def on_left(rows):
        return jnp.concatenate([left] * (rows // RHS), axis=0)

    def build(w, slots, u, row, first, second):
        tiles = [
            turned[pl.ds(pl.multiple_of((row + i) * HALF, HALF), HALF), :] for i in range(2)
        ]
        swapped = [swap_halves(tile) for tile in tiles]
        w[u] = jnp.concatenate(
            [
                jnp.where(on_left(HALF), tiles[0], swapped[1]),
                jnp.where(on_left(HALF), swapped[0], tiles[1]),
            ],
            axis=0,
        ).astype(BF16)
        slots[u, 0] = jnp.where(left, far_target[0, first], far_target[0, second])
        slots[u, 1] = jnp.where(left, send_slot[0, first], send_slot[0, second])
        slots[u, 2] = jnp.where(left, send_slot[0, second], send_slot[0, first])

    def build_parent(u, carry):
        first, second = [2 * partner(2 * u + i) + 1 for i in range(2)]
        build(parent_w, parent_slots, u, 2 * u, first, second)
        return carry

    def build_leaf(u, carry):
        first, second = [2 * leaf_partner(2 * u + i) for i in range(2)]
        build(leaf_w, leaf_slots, u, devices + 2 * u, first, second)
        return carry

    lax.fori_loop(0, devices // 2, build_parent, 0, unroll=8)
    lax.fori_loop(0, (CLOSE + 1) // 2, build_leaf, 0, unroll=3)
    for n in range(PRODUCTS):
        leaf_recv[n, CLOSE] = jnp.zeros((RHS, 2 * RANK), BF16)

    near_load.wait()
    diag_load.wait()
    pl.semaphore_wait(barrier, devices - 1)

    def remote(src, dst, out_sem, in_sem, target):
        return pltpu.make_async_remote_copy(
            src_ref=src,
            dst_ref=dst,
            send_sem=out_sem,
            recv_sem=in_sem,
            device_id=(target,),
            device_id_type=MESH,
        )

    def x_copy(n):
        return remote(
            x_out.at[n], x_in.at[n], side_sem.at[n, 0], side_sem.at[n, 1], leaf_partner(REACH - 1)
        )

    def near_copy(n):
        return remote(
            near_out.at[n], near_in.at[n], side_sem.at[n, 2], side_sem.at[n, 3], leaf_partner(REACH + 1)
        )

    def out_copy(n):
        return pltpu.make_async_copy(out.at[n + 1], out_hbm.at[n], out_sem.at[n])

    def parent_copy(n, w, g):
        return remote(
            send.at[n, pl.ds(w, 1)],
            recv.at[n, pl.ds(w, 1)],
            send_sem.at[n, 0],
            recv_sem.at[n, g],
            partner(w),
        )

    def leaf_copy(n, v):
        return remote(
            leaf_send.at[n, pl.ds(v, 1)],
            leaf_recv.at[n, pl.ds(2 * REACH - v, 1)],
            send_sem.at[n, 1],
            recv_sem.at[n, GROUPS],
            leaf_partner(v),
        )

    def wait_for(tiles, sem):
        pltpu.make_async_copy(tiles, tiles, sem).wait()

    def chosen(slot, rows, first):
        count = rows.shape[0] // RHS
        result = rows[(count - 1) * RHS :]
        for t in reversed(range(count - 1)):
            result = jnp.where(slot == first + t, rows[t * RHS : (t + 1) * RHS], result)
        return result

    def kept(slot, value, first, count):
        return jnp.concatenate(
            [jnp.where(slot == first + t, value, 0.0) for t in range(count)], axis=0
        )

    def hops(u):
        return sum((0, 1, 2, 1)[u >> shift & 3] for shift in (0, 2, 4))

    chips = devices // 2
    order = sorted(range(1, chips), key=lambda u: (-hops(u), u * 37 % chips)) + [0]
    leaf_pairs = list(range((CLOSE + 1) // 2))
    cuts = [cut * chips // CUTS[-1] for cut in CUTS]
    chip_groups = [order[cuts[g] : cuts[g + 1]] for g in range(GROUPS)]

    def finish_vector(n):
        values = []
        for l in range(LEAVES):
            value = vector[l] + nn(last_far[l].astype(BF16), both_basis[l])
            value = value * point_mask[l]
            out[n, l] = value
            values.append(value)
        return values

    def product(n, carry):
        coef = [coefs[l] for l in range(LEAVES)]

        parent = jnp.concatenate(
            [coef[2 * q] + coef[2 * q + 1] for q in range(PARENTS)], axis=0
        )
        leaf = jnp.concatenate(coef, axis=0)
        leaf_turned = swap_halves(leaf)
        parent_twice = jnp.where(on_left(PARENTS * RHS), parent, swap_halves(parent))
        leaf_twice = jnp.where(on_left(LEAVES * RHS), leaf_turned, leaf)
        parent_rows = parent[:, :RANK].astype(BF16)
        leaf_rows = leaf_turned[:, :RANK].astype(BF16)

        def fill(rows, twice, w, slots, first_slot, pairs, store):
            for k in range(0, len(pairs), 2):
                us = pairs[k : k + 2]
                made = nn(rows, side_by_side([w[u] for u in us]))
                for i, u in enumerate(us):
                    block = made[:, i * 2 * RANK : (i + 1) * 2 * RANK]
                    outward = swap_halves(chosen(slots[u, 0], block, first_slot))
                    own = chosen(slots[u, 1], twice, first_slot)
                    store(2 * u, jnp.where(left, own, outward).astype(BF16))
                    store(2 * u + 1, jnp.where(left, outward, own).astype(BF16))

        def store_parent(w, tile):
            send[n, w] = tile

        def store_leaf(v, tile):
            if v == REACH:
                leaf_recv[n, v] = tile
            elif v < CLOSE:
                leaf_send[n, v] = tile

        def fill_group(g):
            fill(
                parent_rows,
                parent_twice,
                parent_w,
                parent_slots,
                LEAVES,
                chip_groups[g],
                store_parent,
            )

        def send_group(g):
            for u in chip_groups[g]:
                for w in (2 * u, 2 * u + 1):
                    if w:
                        parent_copy(n, w, g).start()

        def live_slot(slots, e):
            slot = jnp.where(e < near_count[0], slots[e], -1)
            return jnp.full((RHS, POINTS), slot, jnp.int32)

        def add_backward(step, sofar):
            for i in range(STRIDE):
                e = step * STRIDE + i
                own = extended[near_first[e]]
                slot = live_slot(near_second, e)
                spread = jnp.concatenate(
                    [jnp.where(slot == s, own, 0.0) for s in range(2 * LEAVES)], axis=0
                ).astype(BF16)
                sofar = sofar + nn(spread, near[e])
            return sofar

        def add_forward(step, sofar):
            for i in range(STRIDE):
                e = step * STRIDE + i
                other = extended[near_second[e]]
                slot = live_slot(near_first, e)
                spread = jnp.concatenate(
                    [jnp.where(slot == t, other, 0.0) for t in range(LEAVES)], axis=0
                ).astype(BF16)
                sofar = sofar + nt(spread, near[e])
            return sofar

        fill_group(0)
        send_group(0)

        fill_group(1)
        exact = finish_vector(n)
        rounded = [value.astype(BF16) for value in exact]
        x_out[n] = jnp.concatenate(exact, axis=0).astype(BF16)
        for l in range(LEAVES):
            extended[l] = rounded[l].astype(F32)
        x_copy(n).start()
        send_group(1)

        @pl.when(n > 0)
        def _():
            out_copy(n - 1).start()

        fill_group(2)
        backward = add_backward(0, jnp.zeros((2 * LEAVES * RHS, POINTS), F32))
        send_group(2)

        fill_group(3)
        backward = add_backward(2, add_backward(1, backward))
        send_group(3)

        fill_group(4)
        backward = add_backward(3, backward)
        near_out[n] = backward[LEAVES * RHS :].astype(BF16)
        near_copy(n).start()
        send_group(4)

        fill_group(5)
        total = backward[: LEAVES * RHS] + jnp.concatenate(
            [nn(rounded[l], diag[l]) for l in range(LEAVES)], axis=0
        )
        x_copy(n).wait_recv()
        following = x_in[n].astype(F32)
        for l in range(LEAVES):
            extended[LEAVES + l] = following[l * RHS : (l + 1) * RHS]
        total = add_forward(0, total)
        send_group(5)

        fill(leaf_rows, leaf_twice, leaf_w, leaf_slots, 0, leaf_pairs, store_leaf)
        total = add_forward(1, total)
        for v in range(CLOSE):
            if v != REACH:
                leaf_copy(n, v).start()
        total = add_forward(3, add_forward(2, total))

        def take(box, w, slots, first_slot, slot_count, pairs, sofar):
            through, handed = sofar
            for k in range(0, len(pairs), 2):
                us, rows = pairs[k : k + 2], []
                for u in us:
                    outer = send if u == 0 and box is recv else box
                    even = outer[n, 2 * u].astype(F32)
                    odd = box[n, 2 * u + 1].astype(F32)
                    incoming = jnp.where(left, even, odd)
                    outcome = jnp.where(left, odd, even)
                    rows.append(kept(slots[u, 0], incoming, first_slot, slot_count))
                    handed = handed + kept(slots[u, 2], outcome, first_slot, slot_count)
                through = through + nt(
                    side_by_side(rows).astype(BF16), side_by_side([w[u] for u in us])
                )
            return through, handed

        def nothing(count):
            return (
                jnp.zeros((count * RHS, RANK), F32),
                jnp.zeros((count * RHS, 2 * RANK), F32),
            )

        near_copy(n).wait_recv()
        total = total + near_in[n].astype(F32)
        near_coef = []
        for l in range(LEAVES):
            value = total[l * RHS : (l + 1) * RHS] * point_mask[l]
            vector[l] = value
            near_coef.append(nt(value.astype(BF16), both_basis[l]))

        parent_sum = nothing(PARENTS)
        for g in range(GROUPS):
            messages = 2 * len(chip_groups[g]) - (1 if g == GROUPS - 1 else 0)
            wait_for(recv.at[n, pl.ds(1, messages)], recv_sem.at[n, g])
            if g == GROUPS - 1:
                wait_for(leaf_recv.at[n, pl.ds(0, CLOSE - 1)], recv_sem.at[n, GROUPS])
            parent_sum = take(
                recv, parent_w, parent_slots, LEAVES, PARENTS, chip_groups[g], parent_sum
            )
        leaf_sum = take(
            leaf_recv, leaf_w, leaf_slots, 0, LEAVES, leaf_pairs, nothing(LEAVES)
        )

        def whole(through, handed):
            return through + (handed + swap_halves(handed))[:, :RANK]

        parent_far = whole(*parent_sum)
        leaf_far = whole(*leaf_sum)

        for l in range(LEAVES):
            q = l // 2
            both = jnp.concatenate(
                [parent_far[q * RHS : (q + 1) * RHS], leaf_far[l * RHS : (l + 1) * RHS]], axis=1
            )
            last_far[l] = both
            coefs[l] = near_coef[l] + nn(both.astype(BF16), gram[l])
        return carry

    lax.fori_loop(0, PRODUCTS, product, 0)
    finish_vector(PRODUCTS)
    out_copy(PRODUCTS - 1).start()

    def finish(n, carry):
        wait_for(send.at[n, pl.ds(1, devices - 1)], send_sem.at[n, 0])
        wait_for(leaf_send.at[n, pl.ds(0, CLOSE - 1)], send_sem.at[n, 1])
        x_copy(n).wait_send()
        near_copy(n).wait_send()
        out_copy(n).wait()
        return carry

    lax.fori_loop(0, PRODUCTS, finish, 0)


def on_device(
    start_vector,
    leaf_size,
    diag_blocks,
    near_blocks,
    near_count,
    near_first,
    near_second,
    leaf_basis,
    transfer,
    coupling,
    send_slot,
    far_target,
):
    devices = lax.axis_size("clu")
    tile = (RHS, 2 * RANK)
    close_pairs = (CLOSE + 1) // 2
    smem = pl.BlockSpec(memory_space=pltpu.SMEM)
    hbm = pl.BlockSpec(memory_space=pltpu.HBM)
    sides = (PRODUCTS, LEAVES * RHS, POINTS)
    return pl.pallas_call(
        functools.partial(kernel, devices),
        out_shape=jax.ShapeDtypeStruct((PRODUCTS, LEAVES, RHS, POINTS), F32),
        in_specs=[
            hbm,
            smem,
            hbm,
            hbm,
            smem,
            smem,
            smem,
            hbm,
            hbm,
            hbm,
            smem,
            smem,
        ],
        out_specs=hbm,
        scratch_shapes=[
            pltpu.VMEM((LEAVES, RHS, POINTS), F32),
            pltpu.VMEM((LEAVES, RANK, POINTS), BF16),
            pltpu.VMEM((LEAVES, RANK, RANK), F32),
            pltpu.VMEM((RANK, RANK, 2 * devices), F32),
            pltpu.VMEM(((devices + LEAF_ROWS) * HALF, 2 * RANK), F32),
            pltpu.VMEM((devices // 2, RANK, 2 * RANK), BF16),
            pltpu.VMEM((close_pairs, RANK, 2 * RANK), BF16),
            pltpu.VMEM((devices // 2, 3, *tile), jnp.int32),
            pltpu.VMEM((close_pairs, 3, *tile), jnp.int32),
            pltpu.VMEM((CAPACITY, POINTS, POINTS), BF16),
            pltpu.VMEM((LEAVES, POINTS, POINTS), BF16),
            pltpu.VMEM((LEAVES, 2 * RANK, POINTS), BF16),
            pltpu.VMEM((LEAVES, 2 * RANK, 2 * RANK), BF16),
            pltpu.VMEM((LEAVES, *tile), F32),
            pltpu.VMEM((LEAVES, *tile), F32),
            pltpu.VMEM((LEAVES, RHS, POINTS), F32),
            pltpu.VMEM((LEAVES, RHS, POINTS), F32),
            pltpu.VMEM((PRODUCTS + 1, LEAVES, RHS, POINTS), F32),
            pltpu.VMEM((2 * LEAVES, RHS, POINTS), F32),
            pltpu.VMEM((PRODUCTS, devices, *tile), BF16),
            pltpu.VMEM((PRODUCTS, devices, *tile), BF16),
            pltpu.VMEM((PRODUCTS, CLOSE + 1, *tile), BF16),
            pltpu.VMEM((PRODUCTS, CLOSE + 1, *tile), BF16),
            pltpu.VMEM(sides, BF16),
            pltpu.VMEM(sides, BF16),
            pltpu.VMEM(sides, BF16),
            pltpu.VMEM(sides, BF16),
            pltpu.SemaphoreType.DMA((LOADS + 3, 2)),
            pltpu.SemaphoreType.DMA((PRODUCTS,)),
            pltpu.SemaphoreType.DMA((PRODUCTS, 2)),
            pltpu.SemaphoreType.DMA((PRODUCTS, GROUPS + 1)),
            pltpu.SemaphoreType.DMA((PRODUCTS, 4)),
        ],
        compiler_params=pltpu.CompilerParams(
            collective_id=0, has_side_effects=True, vmem_limit_bytes=56 * 1024 * 1024
        ),
        name="h2_products",
    )(
        start_vector,
        leaf_size,
        diag_blocks,
        near_blocks,
        near_count,
        near_first,
        near_second,
        leaf_basis,
        transfer,
        coupling.transpose(1, 2, 0),
        send_slot,
        far_target,
    )


def solution(mesh):
    in_specs = (
        P("clu", None, None),
        P("clu"),
        P("clu", None, None),
        P("clu", None, None),
        P("clu"),
        P("clu"),
        P("clu"),
        P("clu", None, None),
        P("clu", None, None),
        P("clu", None, None),
        P("clu", None),
        P("clu", None),
    )
    out_specs = P(None, "clu", None, None)
    return jax.shard_map(
        on_device, mesh=mesh, in_specs=in_specs, out_specs=out_specs, check_vma=False
    )
```
